128 devices in a mesh: dp: 4 (over z), ctx: 32 (over x, y, core).
Axes of the slice: x: 4, y: 4, z: 4, core: 2. Of those that a mesh axis runs over, the one named last changes fastest.
Arguments:
- byte_query: bfloat16 [4, 8192, 4096], P('dp', 'ctx'), may hold values from -6 to 6
- byte_key_value: bfloat16 [4, 8192, 2048], P('dp', 'ctx'), may hold values from -6 to 6
- out_grads: bfloat16 [4, 8192, 4096], P('dp', 'ctx'), may hold values from -6 to 6
- patch_starts: int32 [4, 2048], P('dp'), may hold values from 0 to 8191, as said below
- query_gain: float32 [128], replicated, may hold values from 0.1 to 1.9
- key_gain: float32 [128], replicated, may hold values from 0.1 to 1.9
Outputs:
- byte_query_grad: bfloat16 [4, 8192, 4096], P('dp', 'ctx')
- byte_keyval_grad: bfloat16 [4, 8192, 2048], P('dp', 'ctx')
- query_gain_grad: float32 [128], replicated
- key_gain_grad: float32 [128], replicated
The draws below stay inside these ranges and needn't reach their ends.
Inputs may be any that keep to these rules, and one draw needn't show every extreme that they name: `patch_starts`: each row rises strictly and begins with 0. There are integers e_0 to e_(31) in -16 to 16, with e_(31) = 0 and e_(-1) = 0, such that the patches that begin in bytes k * 256 to (k + 1) * 256 - 1 are the patches k * 64 + e_(k - 1) to (k + 1) * 64 + e_k - 1; in every row some e_k is 16 and another is -16.
All inputs are finite; a program needn't handle non-finite values.
Results may differ from the reference program's by a relative error of at most 0.02.
Values may be sent and summed in bfloat16 or wider, within the bound.
No kernel may reach another device: no remote copies, remote signals or barrier semaphores. Data moves between devices by JAX's collectives and lax.ppermute only.
A program may use at most 128 MiB of HBM per device.

```python
import jax
import jax.numpy as jnp
from jax import lax

QUERY_HEADS = 32
KEYVALUE_HEADS = 8
HEAD_SIZE = 128
BYTES_DEV = 256
PATCH_DEV = 64
DRIFT = 16
DOCUMENT_BYTES = 8192
PATCHES = 2048
DOCUMENT_COUNT = 4
N_CTX = 32


def draw_patch_starts(key, part):
    key = jax.random.fold_in(key, 11)

    def one_document(doc_key):
        shift_key, high_key, low_key, score_key = jax.random.split(doc_key, 4)
        shifts = jax.random.randint(shift_key, (N_CTX,), -DRIFT, DRIFT + 1)
        high_at = jax.random.randint(high_key, (), 0, N_CTX - 1)
        low_at = (high_at + jax.random.randint(low_key, (), 1, N_CTX - 1)) % (N_CTX - 1)
        shard_ids = jnp.arange(N_CTX, dtype=jnp.int32)
        shifts = jnp.where(shard_ids == high_at, DRIFT, shifts)
        shifts = jnp.where(shard_ids == low_at, -DRIFT, shifts)
        shifts = jnp.where(shard_ids == N_CTX - 1, 0, shifts)
        before = jnp.concatenate([jnp.zeros((1,), jnp.int32), shifts[:-1]])
        counts = PATCH_DEV + shifts - before
        scores = jax.random.randint(score_key, (N_CTX, BYTES_DEV), 0, 1 << 20) * BYTES_DEV + jnp.arange(BYTES_DEV, dtype=jnp.int32)[None, :]
        scores = scores.at[0, 0].set(jnp.int32(1 << 30))
        ordering = jnp.argsort(-scores, axis=1)
        ranking = jnp.argsort(ordering, axis=1)
        chosen = (ranking < counts[:, None]).reshape(-1)
        picked = jnp.argsort(jnp.where(chosen, 0, 1), stable=True)[:PATCHES]
        return picked.astype(jnp.int32)
    return jax.vmap(one_document)(jax.random.split(key, DOCUMENT_COUNT))


def block_levels(stream_key, extent, cuts, low, top_value):
    loudness = 1.0
    for axis_at, shards_of in cuts:
        steps = jax.random.uniform(jax.random.fold_in(jax.random.fold_in(stream_key, 6), axis_at), (shards_of,), jnp.float32, low / len(cuts), top_value / len(cuts))
        loudness = loudness * jnp.repeat(jnp.exp(steps), extent[axis_at] // shards_of).reshape((-1,) + (1,) * (len(extent) - 1 - axis_at))
    return loudness


def scatter_about(own_key, dims, scale, reach, shards=(), kind=jnp.bfloat16):
    loudness = block_levels(own_key, dims, shards, -0.22, 0.18) if shards else 1.0
    values = jax.random.normal(own_key, dims, jnp.float32) * scale * loudness
    return jnp.minimum(jnp.maximum(values, -reach), reach).astype(kind)


def setup_inputs(seed: int = 0) -> dict:
    splits = jax.random.split(jax.random.key(seed), 7)
    return {
        "byte_query": scatter_about(splits[0], (DOCUMENT_COUNT, DOCUMENT_BYTES, QUERY_HEADS * HEAD_SIZE), 1.0, 6.0, ((0, 4), (1, 32))),
        "byte_key_value": scatter_about(splits[1], (DOCUMENT_COUNT, DOCUMENT_BYTES, 2 * KEYVALUE_HEADS * HEAD_SIZE), 1.0, 6.0, ((0, 4), (1, 32))),
        "out_grads": scatter_about(splits[2], (DOCUMENT_COUNT, DOCUMENT_BYTES, QUERY_HEADS * HEAD_SIZE), 1.0, 6.0, ((0, 4), (1, 32))),
        "patch_starts": draw_patch_starts(jax.random.fold_in(splits[6], 71), 0),
        "query_gain": jnp.clip(1.0 + 0.18 * jax.random.normal(splits[4], (HEAD_SIZE,), jnp.float32), 0.1, 1.9),
        "key_gain": jnp.clip(1.0 + 0.18 * jax.random.normal(splits[5], (HEAD_SIZE,), jnp.float32), 0.1, 1.9),
    }


eps_norm = 1e-06

def normalize(rows, gain):
    inverse = lax.rsqrt(lax.optimization_barrier(jnp.mean(rows * rows, axis=-1, keepdims=True)) + eps_norm)
    unit = rows * inverse
    return (inverse, unit, (unit * gain).astype(jnp.bfloat16))

def norm_back(delta, gain, inverse, unit):
    scaled = delta * gain
    return inverse * (scaled - unit * lax.optimization_barrier(jnp.mean(scaled * unit, axis=-1, keepdims=True)))

def one_document(byte_query, byte_key_value, out_grads, starts, query_gain, key_gain):
    byte_total = byte_query.shape[0]
    patch_count = starts.shape[0]
    repeat_factor = QUERY_HEADS // KEYVALUE_HEADS
    scaling = HEAD_SIZE ** (-0.5)
    positions = jnp.arange(byte_total, dtype=jnp.int32)
    owners = lax.optimization_barrier(jnp.sum((starts[None, :] <= positions[:, None]).astype(jnp.int32), axis=1)) - 1
    patch_ends = jnp.concatenate([starts[1:], jnp.full((1,), byte_total, jnp.int32)])
    patch_lengths = (patch_ends - starts).astype(jnp.float32)[:, None]
    query_sum = jax.ops.segment_sum(byte_query.astype(jnp.float32), owners, num_segments=patch_count)
    key_value_sum = jax.ops.segment_sum(byte_key_value.astype(jnp.float32), owners, num_segments=patch_count)
    grad_sum = jax.ops.segment_sum(out_grads.astype(jnp.float32), owners, num_segments=patch_count)
    query_mean = (query_sum / patch_lengths).reshape(patch_count, QUERY_HEADS, HEAD_SIZE)
    key_average = (key_value_sum[:, :KEYVALUE_HEADS * HEAD_SIZE] / patch_lengths).reshape(patch_count, KEYVALUE_HEADS, HEAD_SIZE)
    value_lower = (key_value_sum[:, KEYVALUE_HEADS * HEAD_SIZE:] / patch_lengths).astype(jnp.bfloat16).reshape(patch_count, KEYVALUE_HEADS, HEAD_SIZE)
    grad_low = grad_sum.astype(jnp.bfloat16).reshape(patch_count, QUERY_HEADS, HEAD_SIZE)
    query_inverse, query_unit, query_norm = normalize(query_mean, query_gain)
    key_inverse, key_unit, key_norm = normalize(key_average, key_gain)
    patch_pos = jnp.arange(patch_count, dtype=jnp.int32)
    allowed = patch_pos[None, :] <= patch_pos[:, None]

    def one_head(head_index):
        group_index = head_index // repeat_factor
        query_head = lax.dynamic_index_in_dim(query_norm, head_index, axis=1, keepdims=False)
        grad_head = lax.dynamic_index_in_dim(grad_low, head_index, axis=1, keepdims=False)
        key_head = lax.dynamic_index_in_dim(key_norm, group_index, axis=1, keepdims=False)
        value_head = lax.dynamic_index_in_dim(value_lower, group_index, axis=1, keepdims=False)
        scores = jnp.dot(query_head, key_head.T, preferred_element_type=jnp.float32) * scaling
        raised = jnp.where(allowed, jnp.exp(scores), 0.0)
        weights = raised / lax.optimization_barrier(jnp.sum(raised, axis=-1, keepdims=True))
        weights_low = weights.astype(jnp.bfloat16)
        dweights = jnp.dot(grad_head, value_head.T, preferred_element_type=jnp.float32)
        row_delta = lax.optimization_barrier(jnp.sum(weights * dweights, axis=-1, keepdims=True))
        dscores = (weights * (dweights - row_delta) * scaling).astype(jnp.bfloat16)
        query_grad = jnp.dot(dscores, key_head, preferred_element_type=jnp.float32)
        key_grad = jnp.dot(dscores.T, query_head, preferred_element_type=jnp.float32)
        value_grad = jnp.dot(weights_low.T, grad_head, preferred_element_type=jnp.float32)
        return (query_grad, key_grad, value_grad)
    query_parts, key_pieces, value_pieces = lax.map(one_head, jnp.arange(QUERY_HEADS, dtype=jnp.int32))
    query_delta = jnp.transpose(query_parts, (1, 0, 2))
    key_change = jnp.transpose(lax.optimization_barrier(jnp.sum(key_pieces.reshape(KEYVALUE_HEADS, repeat_factor, patch_count, HEAD_SIZE), axis=1)), (1, 0, 2))
    value_change = jnp.transpose(lax.optimization_barrier(jnp.sum(value_pieces.reshape(KEYVALUE_HEADS, repeat_factor, patch_count, HEAD_SIZE), axis=1)), (1, 0, 2))
    query_back = norm_back(query_delta, query_gain, query_inverse, query_unit)
    key_backward = norm_back(key_change, key_gain, key_inverse, key_unit)
    gain_query_part = lax.optimization_barrier(jnp.sum(query_delta * query_unit, axis=(0, 1)))
    gain_key_part = lax.optimization_barrier(jnp.sum(key_change * key_unit, axis=(0, 1)))
    query_rows = (query_back.reshape(patch_count, QUERY_HEADS * HEAD_SIZE) / patch_lengths).astype(jnp.bfloat16)
    key_value_rows = jnp.concatenate([key_backward.reshape(patch_count, KEYVALUE_HEADS * HEAD_SIZE) / patch_lengths, value_change.reshape(patch_count, KEYVALUE_HEADS * HEAD_SIZE) / patch_lengths], axis=1).astype(jnp.bfloat16)
    return (query_rows[owners], key_value_rows[owners], gain_query_part, gain_key_part)

def reference(byte_query, byte_key_value, out_grads, patch_starts, query_gain, key_gain):
    query_outs = []
    keyval_outs = []
    gain_query = jnp.zeros((HEAD_SIZE,), jnp.float32)
    gain_key = jnp.zeros((HEAD_SIZE,), jnp.float32)
    for document in range(DOCUMENT_COUNT):
        query_rows, key_value_rows, query_part, key_part = one_document(byte_query[document], byte_key_value[document], out_grads[document], patch_starts[document], query_gain, key_gain)
        query_outs.append(query_rows)
        keyval_outs.append(key_value_rows)
        gain_query = gain_query + query_part
        gain_key = gain_key + key_part
    return (jnp.stack(query_outs), jnp.stack(keyval_outs), gain_query, gain_key)
```

```python
import functools
import math

import jax
import jax.numpy as jnp
from jax import lax
from jax.experimental import pallas as pl
from jax.experimental.pallas import tpu as pltpu
from jax.sharding import PartitionSpec as P

eps_norm = 1e-06
head = 128
below_rows = 32
above_rows = 16
blk = 256
f32 = jnp.float32
bf16 = jnp.bfloat16


def pool_kernel(edges_ref, query_ref, grad_ref, key_ref, value_ref, own_ref, below_ref, above_ref, inv_ref, pick_ref):
    bytes_dev = query_ref.shape[0]
    own = own_ref.shape[1]
    used = below_rows + own + above_rows

    @pl.when(pl.program_id(0) == 0)
    def _():
        start = edges_ref[0:1, :]
        end = edges_ref[1:2, :]
        place = lax.broadcasted_iota(jnp.int32, (bytes_dev, 128), 0)
        inside = jnp.where((start <= place) & (place < end), 1.0, 0.0)
        pick_ref[...] = inside.T.astype(bf16)
        lengths = (end - start).astype(f32)
        row = lax.broadcasted_iota(jnp.int32, (128, 128), 0)
        col = lax.broadcasted_iota(jnp.int32, (128, 128), 1)
        tall = jnp.sum(jnp.where(row == col, lengths, 0.0), axis=1, keepdims=True)
        inv_ref[...] = jnp.broadcast_to(1.0 / tall[below_rows : below_rows + own], inv_ref.shape)

    pick = pick_ref[:used, :]
    at = 0
    for ref in (query_ref, grad_ref, key_ref, value_ref):
        width = ref.shape[1]
        sums = jnp.dot(pick, ref[...], preferred_element_type=f32)
        below_ref[0, :, at : at + width] = sums[:below_rows].astype(bf16)
        own_ref[0, :, at : at + width] = sums[below_rows : below_rows + own]
        above_ref[0, :, at : at + width] = sums[below_rows + own :].astype(bf16)
        at += width


def send_kernel(own_ref, late_ref, early_ref, inv_ref, qgain_ref, kgain_ref, send_ref, mean_ref):
    own = own_ref.shape[1]
    heads = send_ref.shape[0]
    groups = (own_ref.shape[2] // head - 2 * heads) // 2
    inv_len = inv_ref[...]

    def total(tile):
        cols = slice(tile * head, (tile + 1) * head)
        early = early_ref[0, :, cols].astype(f32)
        late = late_ref[0, :, cols].astype(f32)
        gap = jnp.zeros((own - early.shape[0] - late.shape[0], head), f32)
        return own_ref[0, :, cols] + jnp.concatenate([early, gap, late], axis=0)

    def normal(rows, gain):
        inverse = lax.rsqrt(jnp.mean(rows * rows, axis=-1, keepdims=True) + eps_norm)
        return (rows * inverse * gain).astype(bf16)

    for h in range(heads):
        rows = total(h) * inv_len
        mean_ref[0, :, h * head : (h + 1) * head] = rows
        send_ref[h, :, 0:head] = normal(rows, qgain_ref[...])
        send_ref[h, :, head : 2 * head] = total(heads + h).astype(bf16)
    for g in range(groups):
        rows = total(2 * heads + g) * inv_len
        mean_ref[0, :, (heads + g) * head : (heads + g + 1) * head] = rows
        keys = normal(rows, kgain_ref[...])
        values = (total(2 * heads + groups + g) * inv_len).astype(bf16)
        repeat = heads // groups
        for r in range(repeat):
            send_ref[g * repeat + r, :, 2 * head : 3 * head] = keys
            send_ref[g * repeat + r, :, 3 * head : 4 * head] = values


def attend_kernel(x_ref, qgain_ref, kgain_ref, out_ref, gain_ref, keyt_ref, raised_ref, dw_ref, dk_ref, dv_ref, dqt_ref):
    count = x_ref.shape[0] // blk
    scaling = head ** (-0.5)
    raising = scaling * math.log2(math.e)

    def rows(n, part):
        return x_ref[pl.ds(n * blk, blk), part * head : (part + 1) * head]

    def flip(n, c):
        keyt_ref[n] = rows(n, 2).astype(f32).T.astype(bf16)
        return c

    lax.fori_loop(0, count, flip, 0)
    dk_ref[...] = jnp.zeros_like(dk_ref)
    dv_ref[...] = jnp.zeros_like(dv_ref)
    nt = (((1,), (1,)), ((), ()))

    def fold(block):
        return jnp.sum(block.reshape(blk // 8, 8, blk), axis=0)

    def first(i, j, sums, diagonal):
        scores = lax.dot_general(rows(j, 2), rows(i, 0), nt, preferred_element_type=f32)
        raised = jnp.exp2(scores * raising)
        if diagonal:
            key_at = lax.broadcasted_iota(jnp.int32, (blk, blk), 0)
            query_at = lax.broadcasted_iota(jnp.int32, (blk, blk), 1)
            raised = jnp.where(key_at <= query_at, raised, 0.0)
        dweights = lax.dot_general(rows(j, 3), rows(i, 1), nt, preferred_element_type=f32)
        slot = lax.rem(i, 2)
        raised_ref[slot, pl.ds(j * blk, blk), :] = raised
        dw_ref[slot, pl.ds(j * blk, blk), :] = dweights
        return (sums[0] + fold(raised), sums[1] + fold(raised * dweights))

    def second(i, j, inv_sum, delta):
        slot = lax.rem(i, 2)
        weights = raised_ref[slot, pl.ds(j * blk, blk), :] * inv_sum
        dscores = (weights * (dw_ref[slot, pl.ds(j * blk, blk), :] - delta)).astype(bf16)
        at = pl.ds(j * blk, blk)
        dv_ref[at, :] += jnp.dot(weights.astype(bf16), rows(i, 1), preferred_element_type=f32)
        dk_ref[at, :] += jnp.dot(dscores, rows(i, 0), preferred_element_type=f32)
        dqt_ref[...] += jnp.dot(keyt_ref[j], dscores, preferred_element_type=f32)

    def finish(i, total):
        dq = dqt_ref[...].T * scaling
        dqt_ref[...] = jnp.zeros_like(dqt_ref)
        out_ref[pl.ds(i * blk, blk), 0:head] = dq.astype(bf16)
        return total + jnp.sum(dq * rows(i, 0).astype(f32), axis=0, keepdims=True)

    def totals(sums):
        inv_sum = 1.0 / jnp.sum(sums[0], axis=0, keepdims=True)
        return inv_sum, jnp.sum(sums[1], axis=0, keepdims=True) * inv_sum

    zero = jnp.zeros((8, blk), f32)
    dqt_ref[...] = jnp.zeros_like(dqt_ref)
    stats = totals(first(0, 0, (zero, zero), True))

    def row_block(i, carry):
        inv_sum, delta, total = carry

        def both(j, sums):
            sums = first(i + 1, j, sums, False)
            second(i, j, inv_sum, delta)
            return sums

        sums = lax.fori_loop(0, i + 1, both, (zero, zero))
        sums = first(i + 1, i + 1, sums, True)
        total = finish(i, total)
        return totals(sums) + (total,)

    inv_sum, delta, total = lax.fori_loop(0, count - 1, row_block, stats + (jnp.zeros((1, head), f32),))

    def last(j, c):
        second(count - 1, j, inv_sum, delta)
        return c

    lax.fori_loop(0, count, last, 0)
    total = finish(count - 1, total)

    def close(n, key_total):
        at = pl.ds(n * blk, blk)
        dk = dk_ref[at, :] * scaling
        out_ref[at, head : 2 * head] = dk.astype(bf16)
        out_ref[at, 2 * head : 3 * head] = dv_ref[at, :].astype(bf16)
        return key_total + jnp.sum(dk * rows(n, 2).astype(f32), axis=0, keepdims=True)

    key_total = lax.fori_loop(0, count, close, jnp.zeros((1, head), f32))
    gain_ref[0:1, :] = total / qgain_ref[...]
    gain_ref[1:2, :] = key_total / kgain_ref[...]


def back_kernel(x_ref, mean_ref, inv_ref, qgain_ref, kgain_ref, rows_ref, first_ref, last_ref):
    heads = x_ref.shape[0]
    chunks = mean_ref.shape[0]
    per = heads // chunks
    groups = (mean_ref.shape[2] // head - per) * chunks
    repeat = heads // groups
    inv_len = inv_ref[...]
    own = rows_ref.shape[0]

    def put(tile, rows):
        cols = slice(tile * head, (tile + 1) * head)
        rows_ref[:, cols] = rows
        first_ref[:, cols] = rows[:above_rows]
        last_ref[:, cols] = rows[own - below_rows :]

    def back(delta, gain, mean):
        inverse = lax.rsqrt(jnp.mean(mean * mean, axis=-1, keepdims=True) + eps_norm)
        unit = mean * inverse
        scaled = delta * gain
        return inverse * (scaled - unit * jnp.mean(scaled * unit, axis=-1, keepdims=True))

    for h in range(heads):
        at = h % per * head
        mean = mean_ref[h // per, :, at : at + head]
        delta = x_ref[h, :, 0:head].astype(f32)
        put(h, (back(delta, qgain_ref[...], mean) * inv_len).astype(bf16))
    per_group = groups // chunks
    for g in range(groups):
        at = (per + g % per_group) * head
        mean = mean_ref[g // per_group, :, at : at + head]
        key_delta = x_ref[g * repeat, :, head : 2 * head].astype(f32)
        value_delta = x_ref[g * repeat, :, 2 * head : 3 * head].astype(f32)
        for r in range(1, repeat):
            key_delta += x_ref[g * repeat + r, :, head : 2 * head].astype(f32)
            value_delta += x_ref[g * repeat + r, :, 2 * head : 3 * head].astype(f32)
        put(heads + g, (back(key_delta, kgain_ref[...], mean) * inv_len).astype(bf16))
        put(heads + groups + g, (value_delta * inv_len).astype(bf16))


def spread_kernel(edges_ref, *refs):
    parts, outs = refs[:6], refs[6:]
    bytes_dev = outs[0].shape[0]
    start = edges_ref[0:1, :]
    end = edges_ref[1:2, :]
    place = lax.broadcasted_iota(jnp.int32, (bytes_dev, 128), 0)
    pick = jnp.where((start <= place) & (place < end), 1.0, 0.0).astype(bf16)
    used = below_rows + parts[1].shape[0] + above_rows
    pick = pick[:, :used]
    for n, out_ref in enumerate(outs):
        before, own, after = parts[3 * n : 3 * n + 3]
        rows = jnp.concatenate([before[...], own[...], after[...]], axis=0)
        out_ref[...] = jnp.dot(pick, rows, preferred_element_type=f32).astype(bf16)


def shards(byte_query, byte_key_value, out_grads, patch_starts, query_gain, key_gain):
    byte_query, byte_key_value, out_grads = byte_query[0], byte_key_value[0], out_grads[0]
    bytes_dev, query_width = byte_query.shape
    keyval_width = byte_key_value.shape[1]
    heads = query_width // head
    groups = keyval_width // (2 * head)
    devices = lax.axis_size("ctx")
    shard = lax.axis_index("ctx")
    patches = patch_starts.shape[1]
    own = patches // devices
    chunks = 4
    qcols, kcols = query_width // chunks, keyval_width // 2 // chunks
    chunk_cols = 2 * qcols + 2 * kcols
    per = heads // chunks

    padded = jnp.concatenate(
        [
            jnp.zeros((below_rows,), jnp.int32),
            patch_starts[0],
            jnp.full((129,), bytes_dev * devices, jnp.int32),
        ]
    )
    window = lax.dynamic_slice_in_dim(padded, shard * own, 129) - shard * bytes_dev
    edges = jnp.stack([window[:128], window[1:]])

    whole = lambda shape: pl.BlockSpec(shape, lambda i: (0,) * len(shape))
    piece = lambda rows, cols: pl.BlockSpec((1, rows, cols), lambda i: (i, 0, 0))
    sums, below, above, inv_len = pl.pallas_call(
        pool_kernel,
        grid=(chunks,),
        in_specs=[
            whole((2, 128)),
            pl.BlockSpec((bytes_dev, qcols), lambda i: (0, i)),
            pl.BlockSpec((bytes_dev, qcols), lambda i: (0, i)),
            pl.BlockSpec((bytes_dev, kcols), lambda i: (0, i)),
            pl.BlockSpec((bytes_dev, kcols), lambda i: (0, chunks + i)),
        ],
        out_specs=[
            piece(own, chunk_cols),
            piece(below_rows, chunk_cols),
            piece(above_rows, chunk_cols),
            whole((own, head)),
        ],
        out_shape=[
            jax.ShapeDtypeStruct((chunks, own, chunk_cols), f32),
            jax.ShapeDtypeStruct((chunks, below_rows, chunk_cols), bf16),
            jax.ShapeDtypeStruct((chunks, above_rows, chunk_cols), bf16),
            jax.ShapeDtypeStruct((own, head), f32),
        ],
        scratch_shapes=[pltpu.VMEM((128, bytes_dev), bf16)],
        compiler_params=pltpu.CompilerParams(vmem_limit_bytes=32 * 1024 * 1024),
        name="pool",
    )(edges, byte_query, out_grads, byte_key_value, byte_key_value)

    up = [(i, (i + 1) % devices) for i in range(devices)]
    down = [(j, i) for i, j in up]
    late = lax.ppermute(below, "ctx", down)
    early = lax.ppermute(above, "ctx", up)

    qgain, kgain = query_gain[None], key_gain[None]
    send, mean = pl.pallas_call(
        send_kernel,
        grid=(chunks,),
        in_specs=[
            piece(own, chunk_cols),
            piece(below_rows, chunk_cols),
            piece(above_rows, chunk_cols),
            whole((own, head)),
            whole((1, head)),
            whole((1, head)),
        ],
        out_specs=[
            pl.BlockSpec((per, own, 4 * head), lambda i: (i, 0, 0)),
            piece(own, qcols + kcols),
        ],
        out_shape=[
            jax.ShapeDtypeStruct((heads, own, 4 * head), bf16),
            jax.ShapeDtypeStruct((chunks, own, qcols + kcols), f32),
        ],
        compiler_params=pltpu.CompilerParams(vmem_limit_bytes=32 * 1024 * 1024),
        name="send",
    )(sums, late, early, inv_len, qgain, kgain)

    mine = lax.all_to_all(send, "ctx", 0, 0, tiled=True).reshape(patches, 4 * head)

    vmem = pl.BlockSpec(memory_space=pltpu.VMEM)
    grads, gains = pl.pallas_call(
        attend_kernel,
        in_specs=[vmem] * 3,
        out_specs=[vmem] * 2,
        out_shape=[
            jax.ShapeDtypeStruct((patches, 3 * head), bf16),
            jax.ShapeDtypeStruct((2, head), f32),
        ],
        scratch_shapes=[
            pltpu.VMEM((patches // blk, head, blk), bf16),
            pltpu.VMEM((2, patches, blk), f32),
            pltpu.VMEM((2, patches, blk), f32),
            pltpu.VMEM((patches, head), f32),
            pltpu.VMEM((patches, head), f32),
            pltpu.VMEM((head, blk), f32),
        ],
        compiler_params=pltpu.CompilerParams(vmem_limit_bytes=48 * 1024 * 1024),
        name="attend",
    )(mine, qgain, kgain)

    home = lax.all_to_all(grads.reshape(devices, own, 3 * head), "ctx", 0, 0, tiled=True)
    for axis in ("ctx", "dp"):
        span = 1
        while span < lax.axis_size(axis):
            swap = [(i, i ^ span) for i in range(lax.axis_size(axis))]
            gains = gains + lax.ppermute(gains, axis, swap)
            span *= 2

    rows, first_rows, last_rows = pl.pallas_call(
        back_kernel,
        in_specs=[vmem] * 5,
        out_specs=[vmem] * 3,
        out_shape=[
            jax.ShapeDtypeStruct((own, query_width + keyval_width), bf16),
            jax.ShapeDtypeStruct((above_rows, query_width + keyval_width), bf16),
            jax.ShapeDtypeStruct((below_rows, query_width + keyval_width), bf16),
        ],
        compiler_params=pltpu.CompilerParams(vmem_limit_bytes=32 * 1024 * 1024),
        name="back",
    )(home, mean, inv_len, qgain, kgain)
    after = lax.ppermute(first_rows, "ctx", down)
    before = lax.ppermute(last_rows, "ctx", up)

    vcols = keyval_width // chunks
    skip = query_width // vcols
    query_out, keyval_out = pl.pallas_call(
        spread_kernel,
        grid=(chunks,),
        in_specs=[whole((2, 128))]
        + [pl.BlockSpec((n, qcols), lambda i: (0, i)) for n in (below_rows, own, above_rows)]
        + [pl.BlockSpec((n, vcols), lambda i: (0, skip + i)) for n in (below_rows, own, above_rows)],
        out_specs=[
            pl.BlockSpec((bytes_dev, qcols), lambda i: (0, i)),
            pl.BlockSpec((bytes_dev, vcols), lambda i: (0, i)),
        ],
        out_shape=[
            jax.ShapeDtypeStruct((bytes_dev, query_width), bf16),
            jax.ShapeDtypeStruct((bytes_dev, keyval_width), bf16),
        ],
        compiler_params=pltpu.CompilerParams(vmem_limit_bytes=32 * 1024 * 1024),
        name="spread",
    )(edges, before, rows, after, before, rows, after)
    return (query_out[None], keyval_out[None], gains[0], gains[1])


def solution(mesh):
    placed = (
        P("dp", "ctx", None),
        P("dp", "ctx", None),
        P("dp", "ctx", None),
        P("dp", None),
        P(),
        P(),
    )
    return jax.shard_map(
        shards,
        mesh=mesh,
        in_specs=placed,
        out_specs=(P("dp", "ctx", None), P("dp", "ctx", None), P(), P()),
        check_vma=False,
    )
```

```python
import functools
import math

import jax
import jax.numpy as jnp
from jax import lax
from jax.experimental import pallas as pl
from jax.experimental.pallas import tpu as pltpu
from jax.sharding import PartitionSpec as P

eps_norm = 1e-06
head = 128
below_rows = 32
above_rows = 16
edge = 16
query_blk = 1024
key_blk = 256
extra = 8
f32 = jnp.float32
bf16 = jnp.bfloat16
nt = (((1,), (1,)), ((), ()))


def limit(mib):
    return pltpu.CompilerParams(vmem_limit_bytes=mib * 1024 * 1024)


def folded(row, width):
    pieces = [row[:, at : at + width] for at in range(0, row.shape[1], width)]
    return jnp.concatenate(pieces + [jnp.zeros((edge - len(pieces), width), f32)], axis=0)


def unfolded(block, count):
    return jnp.concatenate([block[n : n + 1] for n in range(count)], axis=1)


def bottom(row):
    at = lax.broadcasted_iota(jnp.int32, (edge, row.shape[1]), 0)
    return jnp.where(at == edge - 1, row, 0.0)


def is_even(shard_ref):
    return lax.rem(shard_ref[0], 2) == 0


def put_pair(even, mate_ref, far_ref, at, for_next, for_prev):
    @pl.when(even)
    def _():
        mate_ref[at] = for_next
        far_ref[at] = for_prev

    @pl.when(jnp.logical_not(even))
    def _():
        mate_ref[at] = for_prev
        far_ref[at] = for_next


def get_pair(even, mate_ref, far_ref):
    mate, far = mate_ref[0].astype(f32), far_ref[0].astype(f32)
    return jnp.where(even, mate, far), jnp.where(even, far, mate)


def pool_kernel(shard_ref, edges_ref, query_ref, grad_ref, key_ref, value_ref, own_ref, mate_ref, far_ref, inv_ref, pick_ref):
    bytes_dev = query_ref.shape[0]
    own = own_ref.shape[1]
    used = below_rows + own + above_rows

    @pl.when(pl.program_id(0) == 0)
    def _():
        start = edges_ref[0:1, :]
        end = edges_ref[1:2, :]
        place = lax.broadcasted_iota(jnp.int32, (bytes_dev, 128), 0)
        inside = jnp.where((start <= place) & (place < end), 1.0, 0.0)
        pick_ref[...] = inside.T.astype(bf16)
        lengths = (end - start).astype(f32)
        row = lax.broadcasted_iota(jnp.int32, (128, 128), 0)
        col = lax.broadcasted_iota(jnp.int32, (128, 128), 1)
        tall = jnp.sum(jnp.where(row == col, lengths, 0.0), axis=1, keepdims=True)
        inv_ref[...] = jnp.broadcast_to(1.0 / tall[below_rows : below_rows + own], inv_ref.shape)

    pick = pick_ref[:used, :]
    at = 0
    below, above, lone = [], [], []
    for ref in (query_ref, grad_ref, key_ref, value_ref):
        width = ref.shape[1]
        sums = jnp.dot(pick, ref[...], preferred_element_type=f32)
        own_ref[0, :, at : at + width] = sums[below_rows : below_rows + own]
        lone.append(sums[edge - 1 : edge])
        below.append(sums[edge:below_rows])
        above.append(sums[below_rows + own :])
        at += width
    lone = folded(jnp.concatenate(lone, axis=1), 2 * head)
    for_prev = jnp.concatenate(below + [lone], axis=1).astype(bf16)
    for_next = jnp.concatenate(above + [jnp.zeros_like(lone)], axis=1).astype(bf16)
    put_pair(is_even(shard_ref), mate_ref, far_ref, 0, for_next, for_prev)


def send_kernel(shard_ref, own_ref, mate_ref, far_ref, inv_ref, qgain_ref, kgain_ref, send_ref, mean_ref):
    own = own_ref.shape[1]
    heads = send_ref.shape[0]
    width = own_ref.shape[2]
    groups = (width // head - 2 * heads) // 2
    inv_len = inv_ref[...]
    late, early = get_pair(is_even(shard_ref), mate_ref, far_ref)
    lone = unfolded(late[:, width:], width // (2 * head))

    def total(tile):
        cols = slice(tile * head, (tile + 1) * head)
        gap = jnp.zeros((own - 3 * edge, head), f32)
        return own_ref[0, :, cols] + jnp.concatenate(
            [early[:, cols], gap, bottom(lone[:, cols]), late[:, cols]], axis=0
        )

    def normal(rows, gain):
        inverse = lax.rsqrt(jnp.mean(rows * rows, axis=-1, keepdims=True) + eps_norm)
        return (rows * inverse * gain).astype(bf16)

    for h in range(heads):
        rows = total(h) * inv_len
        mean_ref[0, :, h * head : (h + 1) * head] = rows
        send_ref[h, :, 0:head] = normal(rows, qgain_ref[...])
        send_ref[h, :, head : 2 * head] = total(heads + h).astype(bf16)
    for g in range(groups):
        rows = total(2 * heads + g) * inv_len
        mean_ref[0, :, (heads + g) * head : (heads + g + 1) * head] = rows
        keys = normal(rows, kgain_ref[...])
        values = (total(2 * heads + groups + g) * inv_len).astype(bf16)
        repeat = heads // groups
        for r in range(repeat):
            send_ref[g * repeat + r, :, 2 * head : 3 * head] = keys if r % 2 == 0 else values


def attend_kernel(
    shard_ref,
    mine_ref,
    other_ref,
    qgain_ref,
    kgain_ref,
    dq_ref,
    keep_ref,
    give_ref,
    gain_ref,
    key_ref,
    value_ref,
    keyt_ref,
    raised0_ref,
    raised1_ref,
    dw0_ref,
    dw1_ref,
    dk_ref,
    dv_ref,
    dqt_ref,
):
    patches = mine_ref.shape[0]
    per = query_blk // key_blk
    count = patches // query_blk
    scaling = head ** (-0.5)
    raising = scaling * math.log2(math.e)
    raised_refs, dw_refs = (raised0_ref, raised1_ref), (dw0_ref, dw1_ref)
    even = is_even(shard_ref)

    @pl.when(even)
    def _():
        key_ref[...] = mine_ref[:, 2 * head :]
        value_ref[...] = other_ref[...]

    @pl.when(jnp.logical_not(even))
    def _():
        key_ref[...] = other_ref[...]
        value_ref[...] = mine_ref[:, 2 * head :]

    for n in range(patches // key_blk):
        keyt_ref[n] = key_ref[pl.ds(n * key_blk, key_blk), :].astype(f32).T.astype(bf16)
    dk_ref[...] = jnp.zeros_like(dk_ref)
    dv_ref[...] = jnp.zeros_like(dv_ref)

    def fold(block):
        return jnp.sum(block.reshape(block.shape[0] // 8, 8, block.shape[1]), axis=0)

    def rows(i, lane, part):
        return mine_ref[pl.ds(i * query_blk + lane, query_blk - lane), part * head : (part + 1) * head]

    def first(i, at, lane, sums, diagonal):
        keys = pl.ds(at, key_blk)
        scores = lax.dot_general(key_ref[keys, :], rows(i, lane, 0), nt, preferred_element_type=f32)
        raised = jnp.exp2(scores * raising)
        if diagonal:
            key_at = lax.broadcasted_iota(jnp.int32, raised.shape, 0)
            query_at = lax.broadcasted_iota(jnp.int32, raised.shape, 1)
            raised = jnp.where(key_at <= query_at, raised, 0.0)
        dweights = lax.dot_general(value_ref[keys, :], rows(i, lane, 1), nt, preferred_element_type=f32)
        raised_refs[i % 2][keys, lane:] = raised
        dw_refs[i % 2][keys, lane:] = dweights
        added = fold(raised), fold(raised * dweights)
        if lane:
            none = jnp.zeros((8, lane), f32)
            added = tuple(jnp.concatenate([none, x], axis=1) for x in added)
        return (sums[0] + added[0], sums[1] + added[1])

    def second(i, at, lane, stats):
        keys = pl.ds(at, key_blk)
        inv_sum, delta = stats[0][:, lane:], stats[1][:, lane:]
        weights = raised_refs[i % 2][keys, lane:] * inv_sum
        dscores = (weights * (dw_refs[i % 2][keys, lane:] - delta)).astype(bf16)
        dv_ref[keys, :] += jnp.dot(weights.astype(bf16), rows(i, lane, 1), preferred_element_type=f32)
        dk_ref[keys, :] += jnp.dot(dscores, rows(i, lane, 0), preferred_element_type=f32)
        n = at // key_blk if isinstance(at, int) else lax.div(at, key_blk)
        dqt_ref[:, lane:] += jnp.dot(keyt_ref[n], dscores, preferred_element_type=f32)

    zero = jnp.zeros((8, query_blk), f32)
    total = jnp.zeros((1, head), f32)
    stats = None
    for i in range(count + 1):
        sums = (zero, zero)
        if i > 0:
            dqt_ref[...] = jnp.zeros_like(dqt_ref)

            def both(j, sums, i=i, stats=stats):
                second(i - 1, j * key_blk, 0, stats)
                return first(i, j * key_blk, 0, sums, False) if i < count else sums

            if i > 1:
                sums = lax.fori_loop(0, (i - 1) * per, both, sums, unroll=2)
            for n in range(per):
                at = (i - 1) * query_blk + n * key_blk
                second(i - 1, at, n * key_blk, stats)
                if i < count:
                    sums = first(i, at, 0, sums, False)
        if i < count:
            for n in range(per):
                sums = first(i, i * query_blk + n * key_blk, n * key_blk, sums, True)
        if i > 0:
            at = pl.ds((i - 1) * query_blk, query_blk)
            dq = dqt_ref[...].T * scaling
            dq_ref[at, :] = dq.astype(bf16)
            total = total + jnp.sum(dq * rows(i - 1, 0, 0).astype(f32), axis=0, keepdims=True)
        if i < count:
            inv_sum = 1.0 / jnp.sum(sums[0], axis=0, keepdims=True)
            stats = (inv_sum, jnp.sum(sums[1], axis=0, keepdims=True) * inv_sum)

    key_total = jnp.zeros((1, head), f32)
    for n in range(patches // key_blk):
        at = pl.ds(n * key_blk, key_blk)
        dk = dk_ref[at, :] * scaling
        dk_ref[at, :] = dk
        key_total = key_total + jnp.sum(dk * key_ref[at, :].astype(f32), axis=0, keepdims=True)

    @pl.when(even)
    def _():
        keep_ref[...] = dk_ref[...]
        give_ref[...] = dv_ref[...].astype(bf16)

    @pl.when(jnp.logical_not(even))
    def _():
        keep_ref[...] = dv_ref[...]
        give_ref[...] = dk_ref[...].astype(bf16)

    gain_ref[0:1, :] = total / qgain_ref[...]
    gain_ref[1:2, :] = key_total / kgain_ref[...]


def merge_kernel(dq_ref, keep_ref, got_ref, gain_ref, out_ref):
    gains = jnp.concatenate([gain_ref[0:1, :], gain_ref[1:2, :]], axis=1)
    high = gains.astype(bf16).astype(f32)
    middle = (gains - high).astype(bf16).astype(f32)
    low = gains - high - middle
    tail = jnp.concatenate([high, middle, low, jnp.zeros((extra - 3, 2 * head), f32)], axis=0)
    for n in range(out_ref.shape[0]):
        kept = keep_ref[n] + got_ref[n].astype(f32)
        body = jnp.concatenate([dq_ref[n].astype(f32), kept], axis=1)
        out_ref[n] = jnp.concatenate([body, tail], axis=0).astype(bf16)


def back_kernel(shard_ref, x_ref, mean_ref, inv_ref, qgain_ref, kgain_ref, rows_ref, mate_ref, far_ref, gain_ref):
    heads = x_ref.shape[0]
    chunks, own, width = mean_ref.shape
    per = heads // chunks
    groups = (width // head - per) * chunks
    repeat = heads // groups
    inv_len = inv_ref[...]
    even = is_even(shard_ref)

    def back(delta, gain, mean):
        inverse = lax.rsqrt(jnp.mean(mean * mean, axis=-1, keepdims=True) + eps_norm)
        unit = mean * inverse
        scaled = delta * gain
        return inverse * (scaled - unit * jnp.mean(scaled * unit, axis=-1, keepdims=True))

    def query_rows(h):
        at = h % per * head
        return back(x_ref[h, :own, :head].astype(f32), qgain_ref[...], mean_ref[h // per, :, at : at + head])

    def pair(n):
        low, high = x_ref[n, :own, head:].astype(f32), x_ref[n + 2, :own, head:].astype(f32)
        return low + high

    def keyval_rows(n):
        if n >= groups:
            return pair((n - groups) * repeat + 1)
        at = (per + n % (groups // chunks)) * head
        return back(pair(n * repeat), kgain_ref[...], mean_ref[n // (groups // chunks), :, at : at + head])

    tiles = 2 * groups // chunks
    for c in range(chunks):
        parts = [query_rows(c * per + n) for n in range(per)]
        parts += [keyval_rows(c * tiles + n) for n in range(tiles)]
        parts = [part * inv_len for part in parts]
        for n, part in enumerate(parts):
            rows_ref[c, :, n * head : (n + 1) * head] = part.astype(bf16)
        lone = jnp.concatenate([part[own - edge - 1 : own - edge] for part in parts], axis=1)
        lone = folded(lone, head)
        for_next = jnp.concatenate([part[own - edge :] for part in parts] + [lone], axis=1)
        for_prev = jnp.concatenate([part[:edge] for part in parts] + [jnp.zeros_like(lone)], axis=1)
        put_pair(even, mate_ref, far_ref, c, for_next.astype(bf16), for_prev.astype(bf16))

    tail = x_ref[0, own:, :].astype(f32)
    for h in range(1, heads):
        tail = tail + x_ref[h, own:, :].astype(f32)
    sums = tail[0:1] + tail[1:2] + tail[2:3]
    gain_ref[0:1, :] = sums[:, :head]
    gain_ref[1:2, :] = sums[:, head:]


def spread_kernel(shard_ref, edges_ref, mate_ref, far_ref, rows_ref, query_ref, keyval_ref):
    bytes_dev, query_cols = query_ref.shape
    own, width = rows_ref.shape[1:]
    start = edges_ref[0:1, :]
    end = edges_ref[1:2, :]
    place = lax.broadcasted_iota(jnp.int32, (bytes_dev, 128), 0)
    pick = jnp.where((start <= place) & (place < end), 1.0, 0.0).astype(bf16)
    pick = pick[:, : below_rows + own + above_rows]
    after, before = get_pair(is_even(shard_ref), mate_ref, far_ref)
    lone = bottom(unfolded(before[:, width:], width // head))
    early = jnp.concatenate([lone, before[:, :width]], axis=0).astype(bf16)
    rows = jnp.concatenate([early, rows_ref[0], after[:, :width].astype(bf16)], axis=0)
    out = jnp.dot(pick, rows, preferred_element_type=f32).astype(bf16)
    query_ref[...] = out[:, :query_cols]
    keyval_ref[...] = out[:, query_cols:]


def shards(byte_query, byte_key_value, out_grads, patch_starts, query_gain, key_gain):
    byte_query, byte_key_value, out_grads = byte_query[0], byte_key_value[0], out_grads[0]
    bytes_dev, query_width = byte_query.shape
    keyval_width = byte_key_value.shape[1]
    heads = query_width // head
    devices = lax.axis_size("ctx")
    shard = lax.axis_index("ctx")
    patches = patch_starts.shape[1]
    own = patches // devices
    chunks = 4
    qcols, kcols = query_width // chunks, keyval_width // 2 // chunks
    chunk_cols = 2 * qcols + 2 * kcols
    per = heads // chunks

    padded = jnp.concatenate(
        [
            jnp.zeros((below_rows,), jnp.int32),
            patch_starts[0],
            jnp.full((129,), bytes_dev * devices, jnp.int32),
        ]
    )
    window = lax.dynamic_slice_in_dim(padded, shard * own, 129) - shard * bytes_dev
    edges = jnp.stack([window[:128], window[1:]])
    which = shard.astype(jnp.int32).reshape(1)

    def whole(*shape):
        return pl.BlockSpec(shape, lambda i: (0,) * len(shape))

    def piece(rows, cols):
        return pl.BlockSpec((1, rows, cols), lambda i: (i, 0, 0))

    def shape(kind, *dims):
        return jax.ShapeDtypeStruct(dims, kind)

    smem = pl.BlockSpec(memory_space=pltpu.SMEM)
    vmem = pl.BlockSpec(memory_space=pltpu.VMEM)
    mates = [(i, i ^ 1) for i in range(devices)]
    fars = [(i, i + 1) for i in range(1, devices - 1, 2)]
    fars = fars + [(j, i) for i, j in fars]

    def traded(mate, far):
        return lax.ppermute(mate, "ctx", mates), lax.ppermute(far, "ctx", fars)

    wide = chunk_cols + 2 * head
    sums, mate, far, inv_len = pl.pallas_call(
        pool_kernel,
        grid=(chunks,),
        in_specs=[
            smem,
            whole(2, 128),
            pl.BlockSpec((bytes_dev, qcols), lambda i: (0, i)),
            pl.BlockSpec((bytes_dev, qcols), lambda i: (0, i)),
            pl.BlockSpec((bytes_dev, kcols), lambda i: (0, i)),
            pl.BlockSpec((bytes_dev, kcols), lambda i: (0, chunks + i)),
        ],
        out_specs=[piece(own, chunk_cols), piece(edge, wide), piece(edge, wide), whole(own, head)],
        out_shape=[
            shape(f32, chunks, own, chunk_cols),
            shape(bf16, chunks, edge, wide),
            shape(bf16, chunks, edge, wide),
            shape(f32, own, head),
        ],
        scratch_shapes=[pltpu.VMEM((128, bytes_dev), bf16)],
        compiler_params=limit(56),
        name="pool",
    )(which, edges, byte_query, out_grads, byte_key_value, byte_key_value)
    mate, far = traded(mate, far)

    qgain, kgain = query_gain[None], key_gain[None]
    send, mean = pl.pallas_call(
        send_kernel,
        grid=(chunks,),
        in_specs=[
            smem,
            piece(own, chunk_cols),
            piece(edge, wide),
            piece(edge, wide),
            whole(own, head),
            whole(1, head),
            whole(1, head),
        ],
        out_specs=[
            pl.BlockSpec((per, own, 3 * head), lambda i: (i, 0, 0)),
            piece(own, qcols + kcols),
        ],
        out_shape=[shape(bf16, heads, own, 3 * head), shape(f32, chunks, own, qcols + kcols)],
        compiler_params=limit(32),
        name="send",
    )(which, sums, mate, far, inv_len, qgain, kgain)

    mine = lax.all_to_all(send, "ctx", 0, 0, tiled=True).reshape(patches, 3 * head)
    other = lax.ppermute(mine[:, 2 * head :], "ctx", mates)

    block = (patches, head)
    dq, keep, give, gains = pl.pallas_call(
        attend_kernel,
        in_specs=[smem] + [vmem] * 4,
        out_specs=[vmem] * 4,
        out_shape=[shape(bf16, *block), shape(f32, *block), shape(bf16, *block), shape(f32, 2, head)],
        scratch_shapes=[pltpu.VMEM(block, bf16)] * 2
        + [pltpu.VMEM((patches // key_blk, head, key_blk), bf16)]
        + [pltpu.VMEM((patches, query_blk), f32)] * 4
        + [pltpu.VMEM(block, f32)] * 2
        + [pltpu.VMEM((head, query_blk), f32)],
        compiler_params=limit(56),
        name="attend",
    )(which, mine, other, qgain, kgain)
    got = lax.ppermute(give, "ctx", mates)

    split = (devices, own, head)
    back = pl.pallas_call(
        merge_kernel,
        in_specs=[vmem] * 4,
        out_specs=vmem,
        out_shape=shape(bf16, devices, own + extra, 2 * head),
        compiler_params=limit(32),
        name="merge",
    )(dq.reshape(split), keep.reshape(split), got.reshape(split), gains)
    home = lax.all_to_all(back, "ctx", 0, 0, tiled=True)

    vcols = keyval_width // chunks
    wide = qcols + vcols + head
    rows, mate, far, gains = pl.pallas_call(
        back_kernel,
        in_specs=[smem] + [vmem] * 5,
        out_specs=[vmem] * 4,
        out_shape=[
            shape(bf16, chunks, own, qcols + vcols),
            shape(bf16, chunks, edge, wide),
            shape(bf16, chunks, edge, wide),
            shape(f32, 2, head),
        ],
        compiler_params=limit(32),
        name="back",
    )(which, home, mean, inv_len, qgain, kgain)
    mate, far = traded(mate, far)
    docs = lax.axis_size("dp")
    gains = gains + lax.ppermute(gains, "dp", [(i, i ^ 1) for i in range(docs)])
    gains = gains + lax.ppermute(gains, "dp", [(i, docs - 1 - i) for i in range(docs)])

    query_out, keyval_out = pl.pallas_call(
        spread_kernel,
        grid=(chunks,),
        in_specs=[smem, whole(2, 128), piece(edge, wide), piece(edge, wide), piece(own, qcols + vcols)],
        out_specs=[
            pl.BlockSpec((bytes_dev, qcols), lambda i: (0, i)),
            pl.BlockSpec((bytes_dev, vcols), lambda i: (0, i)),
        ],
        out_shape=[shape(bf16, bytes_dev, query_width), shape(bf16, bytes_dev, keyval_width)],
        compiler_params=limit(32),
        name="spread",
    )(which, edges, mate, far, rows)
    return (query_out[None], keyval_out[None], gains[0], gains[1])


def solution(mesh):
    placed = (
        P("dp", "ctx", None),
        P("dp", "ctx", None),
        P("dp", "ctx", None),
        P("dp", None),
        P(),
        P(),
    )
    return jax.shard_map(
        shards,
        mesh=mesh,
        in_specs=placed,
        out_specs=(P("dp", "ctx", None), P("dp", "ctx", None), P(), P()),
        check_vma=False,
    )
```

```python
import functools
import math

import jax
import jax.numpy as jnp
from jax import lax
from jax.experimental import pallas as pl
from jax.experimental.pallas import tpu as pltpu
from jax.sharding import PartitionSpec as P

eps_norm = 1e-06
head = 128
below_rows = 32
above_rows = 16
edge = 16
query_blk = 1024
key_blk = 256
extra = 8
f32 = jnp.float32
bf16 = jnp.bfloat16
nt = (((1,), (1,)), ((), ()))


def limit(mib):
    return pltpu.CompilerParams(vmem_limit_bytes=mib * 1024 * 1024)


def folded(row, width):
    pieces = [row[:, at : at + width] for at in range(0, row.shape[1], width)]
    return jnp.concatenate(pieces + [jnp.zeros((edge - len(pieces), width), f32)], axis=0)


def unfolded(block, count):
    return jnp.concatenate([block[n : n + 1] for n in range(count)], axis=1)


def bottom(row):
    at = lax.broadcasted_iota(jnp.int32, (edge, row.shape[1]), 0)
    return jnp.where(at == edge - 1, row, 0.0)


def is_even(shard_ref):
    return lax.rem(shard_ref[0], 2) == 0


def put_pair(even, mate_ref, far_ref, at, for_next, for_prev):
    @pl.when(even)
    def _():
        mate_ref[at] = for_next
        far_ref[at] = for_prev

    @pl.when(jnp.logical_not(even))
    def _():
        mate_ref[at] = for_prev
        far_ref[at] = for_next


def get_pair(even, mate_ref, far_ref, at):
    mate, far = mate_ref[at].astype(f32), far_ref[at].astype(f32)
    return jnp.where(even, mate, far), jnp.where(even, far, mate)


def pool_kernel(
    shard_ref,
    starts_ref,
    query_ref,
    keyval_ref,
    grad_ref,
    own_ref,
    mate_ref,
    far_ref,
    inv_ref,
    edges_ref,
    query_buf,
    keyval_buf,
    grad_buf,
    starts_buf,
    sems,
):
    bytes_dev, query_width = query_ref.shape
    half = keyval_ref.shape[1] // 2
    patches = starts_ref.shape[1]
    chunks, own, _ = own_ref.shape
    qcols, kcols = query_width // chunks, half // chunks
    shard = shard_ref[0]
    used = below_rows + own + above_rows

    def parts(c):
        return (
            (query_ref, query_buf, c * qcols, qcols),
            (grad_ref, grad_buf, c * qcols, qcols),
            (keyval_ref, keyval_buf, c * kcols, kcols),
            (keyval_ref, keyval_buf, half + c * kcols, kcols),
        )

    def copies(c):
        return [
            pltpu.make_async_copy(ref.at[:, at : at + width], buf.at[:, at : at + width], sems.at[c, n])
            for n, (ref, buf, at, width) in enumerate(parts(c))
        ]

    starts_copy = pltpu.make_async_copy(starts_ref, starts_buf, sems.at[chunks, 0])
    starts_copy.start()
    for c in range(chunks):
        for copy in copies(c):
            copy.start()

    first_patch = shard * own - below_rows
    starts_copy.wait()
    around = jnp.broadcast_to(starts_buf[...], (8, patches))
    around = pltpu.roll(around, lax.rem(patches - first_patch, patches), 1)
    lane = lax.broadcasted_iota(jnp.int32, (1, 128), 1) + first_patch

    def limited(values, at):
        values = jnp.where(at < 0, 0, jnp.where(at >= patches, bytes_dev * (patches // own), values))
        return values - shard * bytes_dev

    start = limited(around[0:1, 0:128], lane)
    end = limited(around[0:1, 1:129], lane + 1)
    edges_ref[0:1, :] = start
    edges_ref[1:2, :] = end
    place = lax.broadcasted_iota(jnp.int32, (bytes_dev, 128), 0)
    inside = jnp.where((start <= place) & (place < end), 1.0, 0.0)
    pick = inside.T.astype(bf16)[:used, :]
    lengths = (end - start).astype(f32)
    row = lax.broadcasted_iota(jnp.int32, (128, 128), 0)
    col = lax.broadcasted_iota(jnp.int32, (128, 128), 1)
    tall = jnp.sum(jnp.where(row == col, lengths, 0.0), axis=1, keepdims=True)
    inv_ref[...] = jnp.broadcast_to(1.0 / tall[below_rows : below_rows + own], inv_ref.shape)

    even = is_even(shard_ref)
    for c in range(chunks):
        for copy in copies(c):
            copy.wait()
        out = 0
        below, above, lone = [], [], []
        for _, buf, at, width in parts(c):
            sums = jnp.dot(pick, buf[:, at : at + width], preferred_element_type=f32)
            own_ref[c, :, out : out + width] = sums[below_rows : below_rows + own]
            lone.append(sums[edge - 1 : edge])
            below.append(sums[edge:below_rows])
            above.append(sums[below_rows + own :])
            out += width
        lone = folded(jnp.concatenate(lone, axis=1), 2 * head)
        for_prev = jnp.concatenate(below + [lone], axis=1).astype(bf16)
        for_next = jnp.concatenate(above + [jnp.zeros_like(lone)], axis=1).astype(bf16)
        put_pair(even, mate_ref, far_ref, c, for_next, for_prev)


def send_kernel(shard_ref, own_ref, mate_ref, far_ref, inv_ref, qgain_ref, kgain_ref, send_ref, mean_ref):
    chunks, own, width = own_ref.shape
    heads = send_ref.shape[0] // chunks
    groups = (width // head - 2 * heads) // 2
    repeat = heads // groups
    inv_len = inv_ref[...]
    even = is_even(shard_ref)

    def normal(rows, gain):
        inverse = lax.rsqrt(jnp.mean(rows * rows, axis=-1, keepdims=True) + eps_norm)
        return (rows * inverse * gain).astype(bf16)

    def chunk(c, carry):
        late, early = get_pair(even, mate_ref, far_ref, c)
        lone = unfolded(late[:, width:], width // (2 * head))

        def total(tile):
            cols = slice(tile * head, (tile + 1) * head)
            gap = jnp.zeros((own - 3 * edge, head), f32)
            return own_ref[c, :, cols] + jnp.concatenate(
                [early[:, cols], gap, bottom(lone[:, cols]), late[:, cols]], axis=0
            )

        for h in range(heads):
            rows = total(h) * inv_len
            mean_ref[c, :, h * head : (h + 1) * head] = rows
            send_ref[c * heads + h, :, 0:head] = normal(rows, qgain_ref[...])
            send_ref[c * heads + h, :, head : 2 * head] = total(heads + h).astype(bf16)
        for g in range(groups):
            rows = total(2 * heads + g) * inv_len
            mean_ref[c, :, (heads + g) * head : (heads + g + 1) * head] = rows
            keys = normal(rows, kgain_ref[...])
            values = (total(2 * heads + groups + g) * inv_len).astype(bf16)
            for r in range(repeat):
                at = c * heads + g * repeat + r
                send_ref[at, :, 2 * head : 3 * head] = keys if r % 2 == 0 else values
        return carry

    lax.fori_loop(0, chunks, chunk, 0)


def attend_kernel(
    shard_ref,
    mine_ref,
    other_ref,
    qgain_ref,
    kgain_ref,
    dq_ref,
    keep_ref,
    give_ref,
    gain_ref,
    key_ref,
    value_ref,
    keyt_ref,
    raised0_ref,
    raised1_ref,
    dw0_ref,
    dw1_ref,
    dk_ref,
    dv_ref,
    dqt_ref,
):
    patches = mine_ref.shape[0]
    per = query_blk // key_blk
    count = patches // query_blk
    scaling = head ** (-0.5)
    raising = scaling * math.log2(math.e)
    raised_refs, dw_refs = (raised0_ref, raised1_ref), (dw0_ref, dw1_ref)
    even = is_even(shard_ref)

    @pl.when(even)
    def _():
        key_ref[...] = mine_ref[:, 2 * head :]
        value_ref[...] = other_ref[...]

    @pl.when(jnp.logical_not(even))
    def _():
        key_ref[...] = other_ref[...]
        value_ref[...] = mine_ref[:, 2 * head :]

    for n in range(patches // key_blk):
        keyt_ref[n] = key_ref[pl.ds(n * key_blk, key_blk), :].astype(f32).T.astype(bf16)
    dk_ref[...] = jnp.zeros_like(dk_ref)
    dv_ref[...] = jnp.zeros_like(dv_ref)

    def fold(block):
        return jnp.sum(block.reshape(block.shape[0] // 8, 8, block.shape[1]), axis=0)

    def rows(i, lane, part):
        return mine_ref[pl.ds(i * query_blk + lane, query_blk - lane), part * head : (part + 1) * head]

    def first(i, at, lane, sums, diagonal):
        keys = pl.ds(at, key_blk)
        scores = lax.dot_general(key_ref[keys, :], rows(i, lane, 0), nt, preferred_element_type=f32)
        raised = jnp.exp2(scores * raising)
        if diagonal:
            key_at = lax.broadcasted_iota(jnp.int32, raised.shape, 0)
            query_at = lax.broadcasted_iota(jnp.int32, raised.shape, 1)
            raised = jnp.where(key_at <= query_at, raised, 0.0)
        dweights = lax.dot_general(value_ref[keys, :], rows(i, lane, 1), nt, preferred_element_type=f32)
        raised_refs[i % 2][keys, lane:] = raised
        dw_refs[i % 2][keys, lane:] = dweights
        added = fold(raised), fold(raised * dweights)
        if lane:
            none = jnp.zeros((8, lane), f32)
            added = tuple(jnp.concatenate([none, x], axis=1) for x in added)
        return (sums[0] + added[0], sums[1] + added[1])

    def second(i, at, lane, stats):
        keys = pl.ds(at, key_blk)
        inv_sum, delta = stats[0][:, lane:], stats[1][:, lane:]
        weights = raised_refs[i % 2][keys, lane:] * inv_sum
        dscores = (weights * (dw_refs[i % 2][keys, lane:] - delta)).astype(bf16)
        dv_ref[keys, :] += jnp.dot(weights.astype(bf16), rows(i, lane, 1), preferred_element_type=f32)
        dk_ref[keys, :] += jnp.dot(dscores, rows(i, lane, 0), preferred_element_type=f32)
        n = at // key_blk if isinstance(at, int) else lax.div(at, key_blk)
        dqt_ref[:, lane:] += jnp.dot(keyt_ref[n], dscores, preferred_element_type=f32)

    zero = jnp.zeros((8, query_blk), f32)
    total = jnp.zeros((1, head), f32)
    stats = None
    for i in range(count + 1):
        sums = (zero, zero)
        if i > 0:
            dqt_ref[...] = jnp.zeros_like(dqt_ref)

            def both(j, sums, i=i, stats=stats):
                second(i - 1, j * key_blk, 0, stats)
                return first(i, j * key_blk, 0, sums, False) if i < count else sums

            if i > 1:
                sums = lax.fori_loop(0, (i - 1) * per, both, sums, unroll=2)
            for n in range(per):
                at = (i - 1) * query_blk + n * key_blk
                second(i - 1, at, n * key_blk, stats)
                if i < count:
                    sums = first(i, at, 0, sums, False)
        if i < count:
            for n in range(per):
                sums = first(i, i * query_blk + n * key_blk, n * key_blk, sums, True)
        if i > 0:
            at = pl.ds((i - 1) * query_blk, query_blk)
            dq = dqt_ref[...].T * scaling
            dq_ref[at, :] = dq.astype(bf16)
            total = total + jnp.sum(dq * rows(i - 1, 0, 0).astype(f32), axis=0, keepdims=True)
        if i < count:
            inv_sum = 1.0 / jnp.sum(sums[0], axis=0, keepdims=True)
            stats = (inv_sum, jnp.sum(sums[1], axis=0, keepdims=True) * inv_sum)

    key_total = jnp.zeros((1, head), f32)
    for n in range(patches // key_blk):
        at = pl.ds(n * key_blk, key_blk)
        dk = dk_ref[at, :] * scaling
        dk_ref[at, :] = dk
        key_total = key_total + jnp.sum(dk * key_ref[at, :].astype(f32), axis=0, keepdims=True)

    @pl.when(even)
    def _():
        keep_ref[...] = dk_ref[...]
        give_ref[...] = dv_ref[...].astype(bf16)

    @pl.when(jnp.logical_not(even))
    def _():
        keep_ref[...] = dv_ref[...]
        give_ref[...] = dk_ref[...].astype(bf16)

    gain_ref[0:1, :] = total / qgain_ref[...]
    gain_ref[1:2, :] = key_total / kgain_ref[...]


def merge_kernel(dq_ref, keep_ref, got_ref, gain_ref, out_ref):
    gains = jnp.concatenate([gain_ref[0:1, :], gain_ref[1:2, :]], axis=1)
    high = gains.astype(bf16).astype(f32)
    middle = (gains - high).astype(bf16).astype(f32)
    low = gains - high - middle
    tail = jnp.concatenate([high, middle, low, jnp.zeros((extra - 3, 2 * head), f32)], axis=0)
    for n in range(out_ref.shape[0]):
        kept = keep_ref[n] + got_ref[n].astype(f32)
        body = jnp.concatenate([dq_ref[n].astype(f32), kept], axis=1)
        out_ref[n] = jnp.concatenate([body, tail], axis=0).astype(bf16)


def back_kernel(shard_ref, x_ref, mean_ref, inv_ref, qgain_ref, kgain_ref, rows_ref, mate_ref, far_ref, gain_ref):
    heads = x_ref.shape[0]
    chunks, own, width = mean_ref.shape
    per = heads // chunks
    groups = (width // head - per) * chunks
    repeat = heads // groups
    inv_len = inv_ref[...]
    even = is_even(shard_ref)

    def back(delta, gain, mean):
        inverse = lax.rsqrt(jnp.mean(mean * mean, axis=-1, keepdims=True) + eps_norm)
        unit = mean * inverse
        scaled = delta * gain
        return inverse * (scaled - unit * jnp.mean(scaled * unit, axis=-1, keepdims=True))

    def query_rows(h):
        at = h % per * head
        return back(x_ref[h, :own, :head].astype(f32), qgain_ref[...], mean_ref[h // per, :, at : at + head])

    def pair(n):
        low, high = x_ref[n, :own, head:].astype(f32), x_ref[n + 2, :own, head:].astype(f32)
        return low + high

    def keyval_rows(n):
        if n >= groups:
            return pair((n - groups) * repeat + 1)
        at = (per + n % (groups // chunks)) * head
        return back(pair(n * repeat), kgain_ref[...], mean_ref[n // (groups // chunks), :, at : at + head])

    tiles = 2 * groups // chunks
    for c in range(chunks):
        parts = [query_rows(c * per + n) for n in range(per)]
        parts += [keyval_rows(c * tiles + n) for n in range(tiles)]
        parts = [part * inv_len for part in parts]
        for n, part in enumerate(parts):
            rows_ref[c, :, n * head : (n + 1) * head] = part.astype(bf16)
        lone = jnp.concatenate([part[own - edge - 1 : own - edge] for part in parts], axis=1)
        lone = folded(lone, head)
        for_next = jnp.concatenate([part[own - edge :] for part in parts] + [lone], axis=1)
        for_prev = jnp.concatenate([part[:edge] for part in parts] + [jnp.zeros_like(lone)], axis=1)
        put_pair(even, mate_ref, far_ref, c, for_next.astype(bf16), for_prev.astype(bf16))

    tail = x_ref[0, own:, :].astype(f32)
    for h in range(1, heads):
        tail = tail + x_ref[h, own:, :].astype(f32)
    sums = tail[0:1] + tail[1:2] + tail[2:3]
    gain_ref[0:1, :] = sums[:, :head]
    gain_ref[1:2, :] = sums[:, head:]


def spread_kernel(shard_ref, edges_ref, mate_ref, far_ref, rows_ref, query_ref, keyval_ref, query_buf, keyval_buf, sems):
    bytes_dev, query_width = query_ref.shape
    chunks, own, width = rows_ref.shape
    qcols, vcols = query_width // chunks, keyval_ref.shape[1] // chunks
    start = edges_ref[0:1, :]
    end = edges_ref[1:2, :]
    place = lax.broadcasted_iota(jnp.int32, (bytes_dev, 128), 0)
    pick = jnp.where((start <= place) & (place < end), 1.0, 0.0).astype(bf16)
    pick = pick[:, : below_rows + own + above_rows]
    even = is_even(shard_ref)
    running = []
    for c in range(chunks):
        after, before = get_pair(even, mate_ref, far_ref, c)
        lone = bottom(unfolded(before[:, width:], width // head))
        early = jnp.concatenate([lone, before[:, :width]], axis=0).astype(bf16)
        rows = jnp.concatenate([early, rows_ref[c], after[:, :width].astype(bf16)], axis=0)
        out = jnp.dot(pick, rows, preferred_element_type=f32).astype(bf16)
        query_buf[:, c * qcols : (c + 1) * qcols] = out[:, :qcols]
        keyval_buf[:, c * vcols : (c + 1) * vcols] = out[:, qcols:]
        for n, (buf, ref, cols) in enumerate(((query_buf, query_ref, qcols), (keyval_buf, keyval_ref, vcols))):
            at = c * cols
            copy = pltpu.make_async_copy(buf.at[:, at : at + cols], ref.at[:, at : at + cols], sems.at[c, n])
            copy.start()
            running.append(copy)
    for copy in running:
        copy.wait()


def shards(byte_query, byte_key_value, out_grads, patch_starts, query_gain, key_gain):
    byte_query, byte_key_value, out_grads = byte_query[0], byte_key_value[0], out_grads[0]
    bytes_dev, query_width = byte_query.shape
    keyval_width = byte_key_value.shape[1]
    heads = query_width // head
    devices = lax.axis_size("ctx")
    shard = lax.axis_index("ctx")
    patches = patch_starts.shape[1]
    own = patches // devices
    chunks = 4
    qcols, kcols = query_width // chunks, keyval_width // 2 // chunks
    chunk_cols = 2 * qcols + 2 * kcols
    per = heads // chunks

    which = shard.astype(jnp.int32).reshape(1)

    def shape(kind, *dims):
        return jax.ShapeDtypeStruct(dims, kind)

    smem = pl.BlockSpec(memory_space=pltpu.SMEM)
    vmem = pl.BlockSpec(memory_space=pltpu.VMEM)
    hbm = pl.BlockSpec(memory_space=pltpu.HBM)
    mates = [(i, i ^ 1) for i in range(devices)]
    fars = [(i, i + 1) for i in range(1, devices - 1, 2)]
    fars = fars + [(j, i) for i, j in fars]

    def traded(mate, far):
        return lax.ppermute(mate, "ctx", mates), lax.ppermute(far, "ctx", fars)

    wide = chunk_cols + 2 * head
    inputs = (patch_starts, byte_query, byte_key_value, out_grads)
    sums, mate, far, inv_len, edges = pl.pallas_call(
        pool_kernel,
        in_specs=[smem] + [hbm] * 4,
        out_specs=[vmem] * 5,
        out_shape=[
            shape(f32, chunks, own, chunk_cols),
            shape(bf16, chunks, edge, wide),
            shape(bf16, chunks, edge, wide),
            shape(f32, own, head),
            shape(jnp.int32, 2, 128),
        ],
        scratch_shapes=[
            pltpu.VMEM((bytes_dev, query_width), bf16),
            pltpu.VMEM((bytes_dev, keyval_width), bf16),
            pltpu.VMEM((bytes_dev, query_width), bf16),
            pltpu.VMEM((1, patches), jnp.int32),
            pltpu.SemaphoreType.DMA((chunks + 1, 4)),
        ],
        compiler_params=limit(20),
        name="pool",
    )(which, *(pltpu.with_memory_space_constraint(x, pltpu.HBM) for x in inputs))
    mate, far = traded(mate, far)

    qgain, kgain = query_gain[None], key_gain[None]
    send, mean = pl.pallas_call(
        send_kernel,
        in_specs=[smem] + [vmem] * 6,
        out_specs=[vmem] * 2,
        out_shape=[shape(bf16, heads, own, 3 * head), shape(f32, chunks, own, qcols + kcols)],
        compiler_params=limit(20),
        name="send",
    )(which, sums, mate, far, inv_len, qgain, kgain)

    mine = lax.all_to_all(send, "ctx", 0, 0, tiled=True).reshape(patches, 3 * head)
    other = lax.ppermute(mine[:, 2 * head :], "ctx", mates)

    block = (patches, head)
    dq, keep, give, gains = pl.pallas_call(
        attend_kernel,
        in_specs=[smem] + [vmem] * 4,
        out_specs=[vmem] * 4,
        out_shape=[shape(bf16, *block), shape(f32, *block), shape(bf16, *block), shape(f32, 2, head)],
        scratch_shapes=[pltpu.VMEM(block, bf16)] * 2
        + [pltpu.VMEM((patches // key_blk, head, key_blk), bf16)]
        + [pltpu.VMEM((patches - query_blk, query_blk), f32), pltpu.VMEM((patches, query_blk), f32)] * 2
        + [pltpu.VMEM(block, f32)] * 2
        + [pltpu.VMEM((head, query_blk), f32)],
        compiler_params=limit(36),
        name="attend",
    )(which, mine, other, qgain, kgain)
    got = lax.ppermute(give, "ctx", mates)

    split = (devices, own, head)
    back = pl.pallas_call(
        merge_kernel,
        in_specs=[vmem] * 4,
        out_specs=vmem,
        out_shape=shape(bf16, devices, own + extra, 2 * head),
        compiler_params=limit(16),
        name="merge",
    )(dq.reshape(split), keep.reshape(split), got.reshape(split), gains)
    home = lax.all_to_all(back, "ctx", 0, 0, tiled=True)

    vcols = keyval_width // chunks
    wide = qcols + vcols + head
    rows, mate, far, gains = pl.pallas_call(
        back_kernel,
        in_specs=[smem] + [vmem] * 5,
        out_specs=[vmem] * 4,
        out_shape=[
            shape(bf16, chunks, own, qcols + vcols),
            shape(bf16, chunks, edge, wide),
            shape(bf16, chunks, edge, wide),
            shape(f32, 2, head),
        ],
        compiler_params=limit(20),
        name="back",
    )(which, home, mean, inv_len, qgain, kgain)
    mate, far = traded(mate, far)
    mate, gains = lax.optimization_barrier((mate, gains))
    docs = lax.axis_size("dp")
    turned = [lax.ppermute(gains, "dp", [(i, (i + n) % docs) for i in range(docs)]) for n in (1, 3, 2)]
    gains = (gains + turned[2]) + (turned[0] + turned[1])

    query_out, keyval_out = pl.pallas_call(
        spread_kernel,
        in_specs=[smem] + [vmem] * 4,
        out_specs=[hbm] * 2,
        out_shape=[shape(bf16, bytes_dev, query_width), shape(bf16, bytes_dev, keyval_width)],
        scratch_shapes=[
            pltpu.VMEM((bytes_dev, query_width), bf16),
            pltpu.VMEM((bytes_dev, keyval_width), bf16),
            pltpu.SemaphoreType.DMA((chunks, 2)),
        ],
        compiler_params=limit(20),
        name="spread",
    )(which, edges, mate, far, rows)
    return (query_out[None], keyval_out[None], gains[0], gains[1])


def solution(mesh):
    placed = (
        P("dp", "ctx", None),
        P("dp", "ctx", None),
        P("dp", "ctx", None),
        P("dp", None),
        P(),
        P(),
    )
    return jax.shard_map(
        shards,
        mesh=mesh,
        in_specs=placed,
        out_specs=(P("dp", "ctx", None), P("dp", "ctx", None), P(), P()),
        check_vma=False,
    )
```

```python
import functools
import math

import jax
import jax.numpy as jnp
from jax import lax
from jax.experimental import pallas as pl
from jax.experimental.pallas import tpu as pltpu
from jax.sharding import PartitionSpec as P

eps_norm = 1e-06
head = 128
below_rows = 32
above_rows = 16
edge = 16
query_blk = 1024
key_blk = 256
extra = 8
f32 = jnp.float32
bf16 = jnp.bfloat16
nt = (((1,), (1,)), ((), ()))


def limit(mib):
    return pltpu.CompilerParams(vmem_limit_bytes=mib * 1024 * 1024)


def folded(row, width):
    pieces = [row[:, at : at + width] for at in range(0, row.shape[1], width)]
    return jnp.concatenate(pieces + [jnp.zeros((edge - len(pieces), width), f32)], axis=0)


def unfolded(block, count):
    return jnp.concatenate([block[n : n + 1] for n in range(count)], axis=1)


def bottom(row):
    at = lax.broadcasted_iota(jnp.int32, (edge, row.shape[1]), 0)
    return jnp.where(at == edge - 1, row, 0.0)


def is_even(shard_ref):
    return lax.rem(shard_ref[0], 2) == 0


def put_pair(even, mate_ref, far_ref, at, for_next, for_prev):
    @pl.when(even)
    def _():
        mate_ref[at] = for_next
        far_ref[at] = for_prev

    @pl.when(jnp.logical_not(even))
    def _():
        mate_ref[at] = for_prev
        far_ref[at] = for_next


def get_pair(even, mate_ref, far_ref, at):
    mate, far = mate_ref[at].astype(f32), far_ref[at].astype(f32)
    return jnp.where(even, mate, far), jnp.where(even, far, mate)


def pool_kernel(
    shard_ref,
    starts_ref,
    query_ref,
    keyval_ref,
    grad_ref,
    own_ref,
    mate_ref,
    far_ref,
    inv_ref,
    edges_ref,
    query_buf,
    keyval_buf,
    grad_buf,
    starts_buf,
    sems,
):
    bytes_dev, query_width = query_ref.shape
    half = keyval_ref.shape[1] // 2
    patches = starts_ref.shape[1]
    chunks, own, _ = own_ref.shape
    qcols, kcols = query_width // chunks, half // chunks
    shard = shard_ref[0]
    used = below_rows + own + above_rows

    def parts(c):
        return (
            (query_ref, query_buf, c * qcols, qcols),
            (grad_ref, grad_buf, c * qcols, qcols),
            (keyval_ref, keyval_buf, c * kcols, kcols),
            (keyval_ref, keyval_buf, half + c * kcols, kcols),
        )

    def copies(c):
        return [
            pltpu.make_async_copy(ref.at[:, at : at + width], buf.at[:, at : at + width], sems.at[c, n])
            for n, (ref, buf, at, width) in enumerate(parts(c))
        ]

    starts_copy = pltpu.make_async_copy(starts_ref, starts_buf, sems.at[chunks, 0])
    starts_copy.start()
    for c in range(chunks):
        for copy in copies(c):
            copy.start()

    first_patch = shard * own - below_rows
    starts_copy.wait()
    around = jnp.broadcast_to(starts_buf[...], (8, patches))
    around = pltpu.roll(around, lax.rem(patches - first_patch, patches), 1)
    lane = lax.broadcasted_iota(jnp.int32, (1, 128), 1) + first_patch

    def limited(values, at):
        values = jnp.where(at < 0, 0, jnp.where(at >= patches, bytes_dev * (patches // own), values))
        return values - shard * bytes_dev

    start = limited(around[0:1, 0:128], lane)
    end = limited(around[0:1, 1:129], lane + 1)
    edges_ref[0:1, :] = start
    edges_ref[1:2, :] = end
    place = lax.broadcasted_iota(jnp.int32, (bytes_dev, 128), 0)
    inside = jnp.where((start <= place) & (place < end), 1.0, 0.0)
    pick = inside.T.astype(bf16)[:used, :]
    lengths = (end - start).astype(f32)
    row = lax.broadcasted_iota(jnp.int32, (128, 128), 0)
    col = lax.broadcasted_iota(jnp.int32, (128, 128), 1)
    tall = jnp.sum(jnp.where(row == col, lengths, 0.0), axis=1, keepdims=True)
    inv_ref[...] = jnp.broadcast_to(1.0 / tall[below_rows : below_rows + own], inv_ref.shape)

    even = is_even(shard_ref)
    for c in range(chunks):
        for copy in copies(c):
            copy.wait()
        out = 0
        below, above, lone = [], [], []
        for _, buf, at, width in parts(c):
            sums = jnp.dot(pick, buf[:, at : at + width], preferred_element_type=f32)
            own_ref[c, :, out : out + width] = sums[below_rows : below_rows + own]
            lone.append(sums[edge - 1 : edge])
            below.append(sums[edge:below_rows])
            above.append(sums[below_rows + own :])
            out += width
        lone = folded(jnp.concatenate(lone, axis=1), 2 * head)
        for_prev = jnp.concatenate(below + [lone], axis=1).astype(bf16)
        for_next = jnp.concatenate(above + [jnp.zeros_like(lone)], axis=1).astype(bf16)
        put_pair(even, mate_ref, far_ref, c, for_next, for_prev)


def send_kernel(shard_ref, own_ref, mate_ref, far_ref, inv_ref, qgain_ref, kgain_ref, send_ref, mean_ref):
    chunks, own, width = own_ref.shape
    heads = 2 * send_ref.shape[0] // chunks
    groups = (width // head - 2 * heads) // 2
    inv_len = inv_ref[...]
    even = is_even(shard_ref)

    def normal(rows, gain):
        inverse = lax.rsqrt(jnp.mean(rows * rows, axis=-1, keepdims=True) + eps_norm)
        return (rows * inverse * gain).astype(bf16)

    def chunk(c, carry):
        late, early = get_pair(even, mate_ref, far_ref, c)
        lone = unfolded(late[:, width:], width // (2 * head))

        def total(tile):
            cols = slice(tile * head, (tile + 1) * head)
            gap = jnp.zeros((own - 3 * edge, head), f32)
            return own_ref[c, :, cols] + jnp.concatenate(
                [early[:, cols], gap, bottom(lone[:, cols]), late[:, cols]], axis=0
            )

        chip = c * heads // 2
        for h in range(heads):
            rows = total(h) * inv_len
            mean_ref[c, :, h * head : (h + 1) * head] = rows
            at = h % 2 * own
            send_ref[chip + h // 2, at : at + own, :] = normal(rows, qgain_ref[...])
            at += 2 * own
            send_ref[chip + h // 2, at : at + own, :] = total(heads + h).astype(bf16)
        for g in range(groups):
            rows = total(2 * heads + g) * inv_len
            mean_ref[c, :, (heads + g) * head : (heads + g + 1) * head] = rows
            keys = normal(rows, kgain_ref[...])
            values = (total(2 * heads + groups + g) * inv_len).astype(bf16)
            for r in range(heads // 2 // groups):
                at = chip + g * (heads // 2 // groups) + r
                send_ref[at, 4 * own : 5 * own, :] = keys
                send_ref[at, 5 * own : 6 * own, :] = values
        return carry

    lax.fori_loop(0, chunks, chunk, 0)


def attend_kernel(
    shard_ref,
    mine_ref,
    other_ref,
    qgain_ref,
    kgain_ref,
    dq_ref,
    keep_ref,
    give_ref,
    gain_ref,
    key_ref,
    value_ref,
    keyt_ref,
    raised0_ref,
    raised1_ref,
    dw0_ref,
    dw1_ref,
    dk_ref,
    dv_ref,
    dqt_ref,
):
    chips, own = mine_ref.shape[0], mine_ref.shape[1] // 6
    patches = key_ref.shape[0]
    per = query_blk // key_blk
    count = patches // query_blk
    lanes = 2 * own
    scaling = head ** (-0.5)
    raising = scaling * math.log2(math.e)
    raised_refs, dw_refs = (raised0_ref, raised1_ref), (dw0_ref, dw1_ref)
    side = lax.rem(shard_ref[0], 2)

    def places(c):
        mine = pl.multiple_of(c * lanes + side * own, own)
        theirs = pl.multiple_of(c * lanes + (1 - side) * own, own)
        return pl.ds(mine, own), pl.ds(theirs, own)

    for c in range(chips):
        mine, theirs = places(c)
        key_ref[mine, :] = mine_ref[c, 4 * own : 5 * own, :]
        value_ref[mine, :] = mine_ref[c, 5 * own :, :]
        key_ref[theirs, :] = other_ref[c, :own, :]
        value_ref[theirs, :] = other_ref[c, own:, :]

    for n in range(patches // key_blk):
        keyt_ref[n] = key_ref[pl.ds(n * key_blk, key_blk), :].astype(f32).T.astype(bf16)
    dk_ref[...] = jnp.zeros_like(dk_ref)
    dv_ref[...] = jnp.zeros_like(dv_ref)

    def fold(block):
        return jnp.sum(block.reshape(block.shape[0] // 8, 8, block.shape[1]), axis=0)

    def rows(i, lane, part):
        first_chip, last_chip = (i * query_blk + lane) // lanes, (i + 1) * query_blk // lanes
        block = mine_ref[first_chip:last_chip, part * lanes : (part + 1) * lanes, :]
        return block.reshape(query_blk - lane, head)

    def first(i, at, lane, sums, diagonal):
        keys = pl.ds(at, key_blk)
        scores = lax.dot_general(key_ref[keys, :], rows(i, lane, 0), nt, preferred_element_type=f32)
        raised = jnp.exp2(scores * raising)
        if diagonal:
            key_at = lax.broadcasted_iota(jnp.int32, raised.shape, 0)
            query_at = lax.broadcasted_iota(jnp.int32, raised.shape, 1)
            query_at = query_at - lax.bitwise_and(query_at, own) + side * own
            raised = jnp.where(key_at <= query_at, raised, 0.0)
        dweights = lax.dot_general(value_ref[keys, :], rows(i, lane, 1), nt, preferred_element_type=f32)
        raised_refs[i % 2][keys, lane:] = raised
        dw_refs[i % 2][keys, lane:] = dweights
        added = fold(raised), fold(raised * dweights)
        if lane:
            none = jnp.zeros((8, lane), f32)
            added = tuple(jnp.concatenate([none, x], axis=1) for x in added)
        return (sums[0] + added[0], sums[1] + added[1])

    def second(i, at, lane, stats):
        keys = pl.ds(at, key_blk)
        inv_sum, delta = stats[0][:, lane:], stats[1][:, lane:]
        weights = raised_refs[i % 2][keys, lane:] * inv_sum
        dscores = (weights * (dw_refs[i % 2][keys, lane:] - delta)).astype(bf16)
        dv_ref[keys, :] += jnp.dot(weights.astype(bf16), rows(i, lane, 1), preferred_element_type=f32)
        dk_ref[keys, :] += jnp.dot(dscores, rows(i, lane, 0), preferred_element_type=f32)
        n = at // key_blk if isinstance(at, int) else lax.div(at, key_blk)
        dqt_ref[:, lane:] += jnp.dot(keyt_ref[n], dscores, preferred_element_type=f32)

    zero = jnp.zeros((8, query_blk), f32)
    total = jnp.zeros((1, head), f32)
    stats = None
    for i in range(count + 1):
        sums = (zero, zero)
        if i > 0:
            dqt_ref[...] = jnp.zeros_like(dqt_ref)

            def both(j, sums, i=i, stats=stats):
                second(i - 1, j * key_blk, 0, stats)
                return first(i, j * key_blk, 0, sums, False) if i < count else sums

            if i > 1:
                sums = lax.fori_loop(0, (i - 1) * per, both, sums, unroll=2)
            for n in range(per):
                at = (i - 1) * query_blk + n * key_blk
                second(i - 1, at, n * key_blk, stats)
                if i < count:
                    sums = first(i, at, 0, sums, False)
        if i < count:
            for n in range(per):
                sums = first(i, i * query_blk + n * key_blk, n * key_blk, sums, True)
        if i > 0:
            dq = dqt_ref[...].T * scaling
            at = query_blk // lanes
            dq_ref[(i - 1) * at : i * at] = dq.astype(bf16).reshape(at, lanes, head)
            total = total + jnp.sum(dq * rows(i - 1, 0, 0).astype(f32), axis=0, keepdims=True)
        if i < count:
            inv_sum = 1.0 / jnp.sum(sums[0], axis=0, keepdims=True)
            stats = (inv_sum, jnp.sum(sums[1], axis=0, keepdims=True) * inv_sum)

    key_total = jnp.zeros((1, head), f32)
    for n in range(patches // key_blk):
        at = pl.ds(n * key_blk, key_blk)
        dk = dk_ref[at, :] * scaling
        dk_ref[at, :] = dk
        key_total = key_total + jnp.sum(dk * key_ref[at, :].astype(f32), axis=0, keepdims=True)

    for c in range(chips):
        mine, theirs = places(c)
        keep_ref[c, :own, :] = dk_ref[mine, :]
        keep_ref[c, own:, :] = dv_ref[mine, :]
        give_ref[c, :own, :] = dk_ref[theirs, :].astype(bf16)
        give_ref[c, own:, :] = dv_ref[theirs, :].astype(bf16)
    gains = jnp.concatenate([total / qgain_ref[...], key_total / kgain_ref[...]], axis=0)
    parts = in_parts(gains)
    gain_ref[...] = parts
    give_ref[chips] = jnp.concatenate([parts, jnp.zeros((lanes - extra, head), f32)], axis=0).astype(bf16)


def in_parts(gains):
    high = gains.astype(bf16).astype(f32)
    middle = (gains - high).astype(bf16).astype(f32)
    low = (gains - high - middle).astype(bf16).astype(f32)
    return jnp.concatenate([high, middle, low, jnp.zeros((extra - 6, head), f32)], axis=0)


def joined(parts):
    return parts[0:2] + parts[2:4] + parts[4:6]


def merge_kernel(dq_ref, keep_ref, got_ref, gain_ref, out_ref):
    chips = out_ref.shape[0]
    tail = in_parts(joined(gain_ref[...]) + joined(got_ref[chips].astype(f32)))
    for c in range(chips):
        kept = keep_ref[c] + got_ref[c].astype(f32)
        out_ref[c] = jnp.concatenate([dq_ref[c].astype(f32), kept, tail], axis=0).astype(bf16)


def back_kernel(shard_ref, x_ref, mean_ref, inv_ref, qgain_ref, kgain_ref, rows_ref, mate_ref, far_ref, gain_ref):
    chips = x_ref.shape[0]
    chunks, own, width = mean_ref.shape
    per = 2 * chips // chunks
    groups = (width // head - per) * chunks
    repeat = chips // groups
    inv_len = inv_ref[...]
    even = is_even(shard_ref)

    def back(delta, gain, mean):
        inverse = lax.rsqrt(jnp.mean(mean * mean, axis=-1, keepdims=True) + eps_norm)
        unit = mean * inverse
        scaled = delta * gain
        return inverse * (scaled - unit * jnp.mean(scaled * unit, axis=-1, keepdims=True))

    def query_rows(h):
        at = h % per * head
        delta = x_ref[h // 2, h % 2 * own : (h % 2 + 1) * own, :].astype(f32)
        return back(delta, qgain_ref[...], mean_ref[h // per, :, at : at + head])

    def pair(group, part):
        rows = slice((2 + part) * own, (3 + part) * own)
        terms = [x_ref[group * repeat + r, rows, :].astype(f32) for r in range(repeat)]
        return sum(terms[1:], terms[0])

    def keyval_rows(n):
        if n >= groups:
            return pair(n - groups, 1)
        at = (per + n % (groups // chunks)) * head
        return back(pair(n, 0), kgain_ref[...], mean_ref[n // (groups // chunks), :, at : at + head])

    tiles = 2 * groups // chunks
    for c in range(chunks):
        parts = [query_rows(c * per + n) for n in range(per)]
        parts += [keyval_rows(c * tiles + n) for n in range(tiles)]
        parts = [part * inv_len for part in parts]
        for n, part in enumerate(parts):
            rows_ref[c, :, n * head : (n + 1) * head] = part.astype(bf16)
        lone = jnp.concatenate([part[own - edge - 1 : own - edge] for part in parts], axis=1)
        lone = folded(lone, head)
        for_next = jnp.concatenate([part[own - edge :] for part in parts] + [lone], axis=1)
        for_prev = jnp.concatenate([part[:edge] for part in parts] + [jnp.zeros_like(lone)], axis=1)
        put_pair(even, mate_ref, far_ref, c, for_next.astype(bf16), for_prev.astype(bf16))

    tail = x_ref[0, 4 * own :, :].astype(f32)
    for c in range(1, chips):
        tail = tail + x_ref[c, 4 * own :, :].astype(f32)
    gain_ref[...] = joined(tail)


def spread_kernel(shard_ref, edges_ref, mate_ref, far_ref, rows_ref, query_ref, keyval_ref, query_buf, keyval_buf, sems):
    bytes_dev, query_width = query_ref.shape
    chunks, own, width = rows_ref.shape
    qcols, vcols = query_width // chunks, keyval_ref.shape[1] // chunks
    start = edges_ref[0:1, :]
    end = edges_ref[1:2, :]
    place = lax.broadcasted_iota(jnp.int32, (bytes_dev, 128), 0)
    pick = jnp.where((start <= place) & (place < end), 1.0, 0.0).astype(bf16)
    pick = pick[:, : below_rows + own + above_rows]
    even = is_even(shard_ref)
    running = []
    for c in range(chunks):
        after, before = get_pair(even, mate_ref, far_ref, c)
        lone = bottom(unfolded(before[:, width:], width // head))
        early = jnp.concatenate([lone, before[:, :width]], axis=0).astype(bf16)
        rows = jnp.concatenate([early, rows_ref[c], after[:, :width].astype(bf16)], axis=0)
        out = jnp.dot(pick, rows, preferred_element_type=f32).astype(bf16)
        query_buf[:, c * qcols : (c + 1) * qcols] = out[:, :qcols]
        keyval_buf[:, c * vcols : (c + 1) * vcols] = out[:, qcols:]
        for n, (buf, ref, cols) in enumerate(((query_buf, query_ref, qcols), (keyval_buf, keyval_ref, vcols))):
            at = c * cols
            copy = pltpu.make_async_copy(buf.at[:, at : at + cols], ref.at[:, at : at + cols], sems.at[c, n])
            copy.start()
            running.append(copy)
    for copy in running:
        copy.wait()


def shards(byte_query, byte_key_value, out_grads, patch_starts, query_gain, key_gain):
    byte_query, byte_key_value, out_grads = byte_query[0], byte_key_value[0], out_grads[0]
    bytes_dev, query_width = byte_query.shape
    keyval_width = byte_key_value.shape[1]
    devices = lax.axis_size("ctx")
    chips = devices // 2
    shard = lax.axis_index("ctx")
    patches = patch_starts.shape[1]
    own = patches // devices
    chunks = 4
    qcols, kcols = query_width // chunks, keyval_width // 2 // chunks
    chunk_cols = 2 * qcols + 2 * kcols

    which = shard.astype(jnp.int32).reshape(1)

    def shape(kind, *dims):
        return jax.ShapeDtypeStruct(dims, kind)

    smem = pl.BlockSpec(memory_space=pltpu.SMEM)
    vmem = pl.BlockSpec(memory_space=pltpu.VMEM)
    hbm = pl.BlockSpec(memory_space=pltpu.HBM)
    mates = [(i, i ^ 1) for i in range(devices)]
    fars = [(i, i + 1) for i in range(1, devices - 1, 2)]
    fars = fars + [(j, i) for i, j in fars]

    def traded(mate, far):
        return lax.ppermute(mate, "ctx", mates), lax.ppermute(far, "ctx", fars)

    wide = chunk_cols + 2 * head
    inputs = (patch_starts, byte_query, byte_key_value, out_grads)
    sums, mate, far, inv_len, edges = pl.pallas_call(
        pool_kernel,
        in_specs=[smem] + [hbm] * 4,
        out_specs=[vmem] * 5,
        out_shape=[
            shape(f32, chunks, own, chunk_cols),
            shape(bf16, chunks, edge, wide),
            shape(bf16, chunks, edge, wide),
            shape(f32, own, head),
            shape(jnp.int32, 2, 128),
        ],
        scratch_shapes=[
            pltpu.VMEM((bytes_dev, query_width), bf16),
            pltpu.VMEM((bytes_dev, keyval_width), bf16),
            pltpu.VMEM((bytes_dev, query_width), bf16),
            pltpu.VMEM((1, patches), jnp.int32),
            pltpu.SemaphoreType.DMA((chunks + 1, 4)),
        ],
        compiler_params=limit(20),
        name="pool",
    )(which, *(pltpu.with_memory_space_constraint(x, pltpu.HBM) for x in inputs))
    mate, far = traded(mate, far)

    qgain, kgain = query_gain[None], key_gain[None]
    send, mean = pl.pallas_call(
        send_kernel,
        in_specs=[smem] + [vmem] * 6,
        out_specs=[vmem] * 2,
        out_shape=[shape(bf16, chips, 6 * own, head), shape(f32, chunks, own, qcols + kcols)],
        compiler_params=limit(20),
        name="send",
    )(which, sums, mate, far, inv_len, qgain, kgain)

    sides = [list(range(n, devices, 2)) for n in range(2)]
    mine = lax.all_to_all(send, "ctx", 0, 0, tiled=True, axis_index_groups=sides)
    other = lax.ppermute(mine[:, 4 * own :], "ctx", mates)

    block = (patches, head)
    dq, keep, give, gains = pl.pallas_call(
        attend_kernel,
        in_specs=[smem] + [vmem] * 4,
        out_specs=[vmem] * 4,
        out_shape=[
            shape(bf16, chips, 2 * own, head),
            shape(f32, chips, 2 * own, head),
            shape(bf16, chips + 1, 2 * own, head),
            shape(f32, extra, head),
        ],
        scratch_shapes=[pltpu.VMEM(block, bf16)] * 2
        + [pltpu.VMEM((patches // key_blk, head, key_blk), bf16)]
        + [pltpu.VMEM((patches - query_blk, query_blk), f32), pltpu.VMEM((patches, query_blk), f32)] * 2
        + [pltpu.VMEM(block, f32)] * 2
        + [pltpu.VMEM((head, query_blk), f32)],
        compiler_params=limit(36),
        name="attend",
    )(which, mine, other, qgain, kgain)
    got = lax.ppermute(give, "ctx", mates)

    back = pl.pallas_call(
        merge_kernel,
        in_specs=[vmem] * 4,
        out_specs=vmem,
        out_shape=shape(bf16, chips, 4 * own + extra, head),
        compiler_params=limit(16),
        name="merge",
    )(dq, keep, got, gains)
    home = lax.all_to_all(back, "ctx", 0, 0, tiled=True, axis_index_groups=sides)

    vcols = keyval_width // chunks
    wide = qcols + vcols + head
    rows, mate, far, gains = pl.pallas_call(
        back_kernel,
        in_specs=[smem] + [vmem] * 5,
        out_specs=[vmem] * 4,
        out_shape=[
            shape(bf16, chunks, own, qcols + vcols),
            shape(bf16, chunks, edge, wide),
            shape(bf16, chunks, edge, wide),
            shape(f32, 2, head),
        ],
        compiler_params=limit(20),
        name="back",
    )(which, home, mean, inv_len, qgain, kgain)
    mate, far = traded(mate, far)
    mate, gains = lax.optimization_barrier((mate, gains))
    docs = lax.axis_size("dp")
    turned = [lax.ppermute(gains, "dp", [(i, (i + n) % docs) for i in range(docs)]) for n in (1, 3, 2)]
    gains = (gains + turned[2]) + (turned[0] + turned[1])

    query_out, keyval_out = pl.pallas_call(
        spread_kernel,
        in_specs=[smem] + [vmem] * 4,
        out_specs=[hbm] * 2,
        out_shape=[shape(bf16, bytes_dev, query_width), shape(bf16, bytes_dev, keyval_width)],
        scratch_shapes=[
            pltpu.VMEM((bytes_dev, query_width), bf16),
            pltpu.VMEM((bytes_dev, keyval_width), bf16),
            pltpu.SemaphoreType.DMA((chunks, 2)),
        ],
        compiler_params=limit(20),
        name="spread",
    )(which, edges, mate, far, rows)
    return (query_out[None], keyval_out[None], gains[0], gains[1])


def solution(mesh):
    placed = (
        P("dp", "ctx", None),
        P("dp", "ctx", None),
        P("dp", "ctx", None),
        P("dp", None),
        P(),
        P(),
    )
    return jax.shard_map(
        shards,
        mesh=mesh,
        in_specs=placed,
        out_specs=(P("dp", "ctx", None), P("dp", "ctx", None), P(), P()),
        check_vma=False,
    )
```

```python
import functools
import math

import jax
import jax.numpy as jnp
from jax import lax
from jax.experimental import pallas as pl
from jax.experimental.pallas import tpu as pltpu
from jax.sharding import PartitionSpec as P

eps_norm = 1e-06
head = 128
below_rows = 32
above_rows = 16
edge = 16
query_blk = 1024
key_blk = 256
extra = 8
f32 = jnp.float32
bf16 = jnp.bfloat16
nt = (((1,), (1,)), ((), ()))


def limit(mib):
    return pltpu.CompilerParams(vmem_limit_bytes=mib * 1024 * 1024)


def folded(row, width):
    pieces = [row[:, at : at + width] for at in range(0, row.shape[1], width)]
    return jnp.concatenate(pieces + [jnp.zeros((edge - len(pieces), width), f32)], axis=0)


def unfolded(block, count):
    return jnp.concatenate([block[n : n + 1] for n in range(count)], axis=1)


def bottom(row):
    at = lax.broadcasted_iota(jnp.int32, (edge, row.shape[1]), 0)
    return jnp.where(at == edge - 1, row, 0.0)


def is_even(shard_ref):
    return lax.rem(shard_ref[0], 2) == 0


def put_pair(even, mate_ref, far_ref, at, for_next, for_prev):
    @pl.when(even)
    def _():
        mate_ref[at] = for_next
        far_ref[at] = for_prev

    @pl.when(jnp.logical_not(even))
    def _():
        mate_ref[at] = for_prev
        far_ref[at] = for_next


def get_pair(even, mate_ref, far_ref, at):
    mate, far = mate_ref[at].astype(f32), far_ref[at].astype(f32)
    return jnp.where(even, mate, far), jnp.where(even, far, mate)


def pool_kernel(
    shard_ref,
    starts_ref,
    query_ref,
    keyval_ref,
    grad_ref,
    own_ref,
    rims_ref,
    edges_ref,
    query_buf,
    keyval_buf,
    grad_buf,
    starts_buf,
    sems,
):
    bytes_dev, query_width = query_ref.shape
    half = keyval_ref.shape[1] // 2
    patches = starts_ref.shape[1]
    chunks, own, _ = own_ref.shape
    qcols, kcols = query_width // chunks, half // chunks
    shard = shard_ref[0]
    used = below_rows + own + above_rows

    def parts(c):
        return (
            (query_ref, query_buf, c * qcols, qcols),
            (grad_ref, grad_buf, c * qcols, qcols),
            (keyval_ref, keyval_buf, c * kcols, kcols),
            (keyval_ref, keyval_buf, half + c * kcols, kcols),
        )

    def copies(c):
        return [
            pltpu.make_async_copy(ref.at[:, at : at + width], buf.at[:, at : at + width], sems.at[c, n])
            for n, (ref, buf, at, width) in enumerate(parts(c))
        ]

    starts_copy = pltpu.make_async_copy(starts_ref, starts_buf, sems.at[chunks, 0])
    starts_copy.start()
    for c in range(chunks):
        for copy in copies(c):
            copy.start()

    first_patch = shard * own - below_rows
    starts_copy.wait()
    around = jnp.broadcast_to(starts_buf[...], (8, patches))
    around = pltpu.roll(around, lax.rem(patches - first_patch, patches), 1)
    lane = lax.broadcasted_iota(jnp.int32, (1, 128), 1) + first_patch

    def limited(values, at):
        values = jnp.where(at < 0, 0, jnp.where(at >= patches, bytes_dev * (patches // own), values))
        return values - shard * bytes_dev

    start = limited(around[0:1, 0:128], lane)
    end = limited(around[0:1, 1:129], lane + 1)
    edges_ref[0:1, :] = start
    edges_ref[1:2, :] = end
    place = lax.broadcasted_iota(jnp.int32, (bytes_dev, 128), 0)
    inside = jnp.where((start <= place) & (place < end), 1.0, 0.0)
    pick = inside.T.astype(bf16)[:used, :]
    for c in range(chunks):
        for copy in copies(c):
            copy.wait()
        out = 0
        below, above, lone = [], [], []
        for _, buf, at, width in parts(c):
            sums = jnp.dot(pick, buf[:, at : at + width], preferred_element_type=f32)
            own_ref[c, :, out : out + width] = sums[below_rows : below_rows + own]
            lone.append(sums[edge - 1 : edge])
            below.append(sums[edge:below_rows])
            above.append(sums[below_rows + own :])
            out += width
        lone = folded(jnp.concatenate(lone, axis=1), 2 * head)
        rims_ref[c, :edge, :] = jnp.concatenate(below + [lone], axis=1).astype(bf16)
        rims_ref[c, edge:, :] = jnp.concatenate(above + [jnp.zeros_like(lone)], axis=1).astype(bf16)


def rimmed(rows, early, lone, late):
    gap = jnp.zeros((rows.shape[0] - 3 * edge, rows.shape[1]), f32)
    return rows + jnp.concatenate([early, gap, bottom(lone), late], axis=0)


def send_kernel(shard_ref, own_ref, rims_ref, send_ref):
    chunks, own, width = own_ref.shape
    heads = 2 * send_ref.shape[0] // chunks
    groups = (width // head - 2 * heads) // 2
    even = is_even(shard_ref)

    def chunk(c, carry):
        got = rims_ref[c].astype(f32)
        below, above, lone = got[:edge, :width], got[edge:, :width], unfolded(got[:edge, width:], width // (2 * head))
        early, late = jnp.where(even, 0.0, above), jnp.where(even, below, 0.0)
        far, far_lone = jnp.where(even, above, below), jnp.where(even, 0.0, lone)
        lone = jnp.where(even, lone, 0.0)

        def put(chip, part, tile):
            cols = slice(tile * head, (tile + 1) * head)
            rows = rimmed(own_ref[c, :, cols], early[:, cols], lone[:, cols], late[:, cols])
            send_ref[chip, part * own : (part + 1) * own, :] = rows.astype(bf16)
            at = 6 * own + part * edge
            send_ref[chip, at : at + edge, :] = far[:, cols].astype(bf16)
            return far_lone[:, cols]

        for n in range(heads // 2):
            chip = c * heads // 2 + n
            group = n * groups // (heads // 2)
            tiles = [2 * n, 2 * n + 1, heads + 2 * n, heads + 2 * n + 1, 2 * heads + group, 2 * heads + groups + group]
            ends = [put(chip, part, tile) for part, tile in enumerate(tiles)]
            ends = jnp.concatenate(ends + [jnp.zeros((edge - 6, head), f32)], axis=0)
            send_ref[chip, 6 * (own + edge) :, :] = ends.astype(bf16)
        return carry

    lax.fori_loop(0, chunks, chunk, 0)


def summed_part(mine_ref, even, c, part, own):
    chips = mine_ref.shape[0]
    at = 6 * own + part * edge
    none = jnp.zeros((edge, head), f32)
    early = late = none
    lone = none[:1]
    if c > 0:
        early = jnp.where(even, mine_ref[c - 1, at : at + edge, :].astype(f32), 0.0)
    if c < chips - 1:
        late = jnp.where(even, 0.0, mine_ref[c + 1, at : at + edge, :].astype(f32))
        lone = mine_ref[c + 1, 6 * (own + edge) :, :].astype(f32)[part : part + 1]
        lone = jnp.where(even, 0.0, lone)
    return rimmed(mine_ref[c, part * own : (part + 1) * own, :].astype(f32), early, lone, late)


def inverse_rms(rows):
    return lax.rsqrt(jnp.mean(rows * rows, axis=-1, keepdims=True) + eps_norm)


def keys_kernel(shard_ref, starts_ref, mine_ref, kgain_ref, keyval_ref, mean_ref, inv_ref, *, document):
    chips, own, _ = inv_ref.shape
    patches = starts_ref.shape[1]
    lanes = patches // chips
    even = is_even(shard_ref)
    starts = starts_ref[...].astype(f32)
    ends = jnp.concatenate([starts[:, 1:], jnp.full((1, 1), document, f32)], axis=1)
    lengths = ends - starts
    table = jnp.concatenate([lengths[:, c * lanes : (c + 1) * lanes] for c in range(chips)], axis=0)
    table = 1.0 / table.T
    table = jnp.where(even, table[:own], table[own:])
    for c in range(chips):
        inv_len = jnp.broadcast_to(table[:, c : c + 1], (own, head))
        inv_ref[c] = inv_len
        rows = summed_part(mine_ref, even, c, 4, own) * inv_len
        mean_ref[c] = rows
        keyval_ref[c, :own, :] = (rows * inverse_rms(rows) * kgain_ref[...]).astype(bf16)
        keyval_ref[c, own:, :] = (summed_part(mine_ref, even, c, 5, own) * inv_len).astype(bf16)


def queries_kernel(shard_ref, mine_ref, inv_ref, qgain_ref, query_ref, grad_ref, mean_ref):
    chips, own, _ = inv_ref.shape
    even = is_even(shard_ref)
    for c in range(chips):
        for n in range(2):
            at = slice(n * own, (n + 1) * own)
            rows = summed_part(mine_ref, even, c, n, own) * inv_ref[c]
            mean_ref[c, at, :] = rows
            query_ref[c, at, :] = (rows * inverse_rms(rows) * qgain_ref[...]).astype(bf16)
            grad_ref[c, at, :] = summed_part(mine_ref, even, c, 2 + n, own).astype(bf16)


def attend_kernel(
    shard_ref,
    query_ref,
    grad_ref,
    mine_ref,
    other_ref,
    qgain_ref,
    kgain_ref,
    dq_ref,
    keep_ref,
    give_ref,
    gain_ref,
    key_ref,
    value_ref,
    keyt_ref,
    raised0_ref,
    raised1_ref,
    dw0_ref,
    dw1_ref,
    dk_ref,
    dv_ref,
    dqt_ref,
):
    chips, own = mine_ref.shape[0], mine_ref.shape[1] // 2
    patches = key_ref.shape[0]
    per = query_blk // key_blk
    count = patches // query_blk
    lanes = 2 * own
    scaling = head ** (-0.5)
    raising = scaling * math.log2(math.e)
    raised_refs, dw_refs = (raised0_ref, raised1_ref), (dw0_ref, dw1_ref)
    side = lax.rem(shard_ref[0], 2)

    def places(c):
        mine = pl.multiple_of(c * lanes + side * own, own)
        theirs = pl.multiple_of(c * lanes + (1 - side) * own, own)
        return pl.ds(mine, own), pl.ds(theirs, own)

    for c in range(chips):
        mine, theirs = places(c)
        key_ref[mine, :] = mine_ref[c, :own, :]
        value_ref[mine, :] = mine_ref[c, own:, :]
        key_ref[theirs, :] = other_ref[c, :own, :]
        value_ref[theirs, :] = other_ref[c, own:, :]

    for n in range(patches // key_blk):
        keyt_ref[n] = key_ref[pl.ds(n * key_blk, key_blk), :].astype(f32).T.astype(bf16)
    dk_ref[...] = jnp.zeros_like(dk_ref)
    dv_ref[...] = jnp.zeros_like(dv_ref)

    def fold(block):
        return jnp.sum(block.reshape(block.shape[0] // 8, 8, block.shape[1]), axis=0)

    def rows(i, lane, part):
        first_chip, last_chip = (i * query_blk + lane) // lanes, (i + 1) * query_blk // lanes
        block = (query_ref, grad_ref)[part][first_chip:last_chip]
        return block.reshape(query_blk - lane, head)

    def first(i, at, lane, sums, diagonal):
        keys = pl.ds(at, key_blk)
        scores = lax.dot_general(key_ref[keys, :], rows(i, lane, 0), nt, preferred_element_type=f32)
        raised = jnp.exp2(scores * raising)
        if diagonal:
            key_at = lax.broadcasted_iota(jnp.int32, raised.shape, 0)
            query_at = lax.broadcasted_iota(jnp.int32, raised.shape, 1)
            query_at = query_at - lax.bitwise_and(query_at, own) + side * own
            raised = jnp.where(key_at <= query_at, raised, 0.0)
        dweights = lax.dot_general(value_ref[keys, :], rows(i, lane, 1), nt, preferred_element_type=f32)
        raised_refs[i % 2][keys, lane:] = raised
        dw_refs[i % 2][keys, lane:] = dweights
        added = fold(raised), fold(raised * dweights)
        if lane:
            none = jnp.zeros((8, lane), f32)
            added = tuple(jnp.concatenate([none, x], axis=1) for x in added)
        return (sums[0] + added[0], sums[1] + added[1])

    def second(i, at, lane, stats):
        keys = pl.ds(at, key_blk)
        inv_sum, delta = stats[0][:, lane:], stats[1][:, lane:]
        weights = raised_refs[i % 2][keys, lane:] * inv_sum
        dscores = (weights * (dw_refs[i % 2][keys, lane:] - delta)).astype(bf16)
        dv_ref[keys, :] += jnp.dot(weights.astype(bf16), rows(i, lane, 1), preferred_element_type=f32)
        dk_ref[keys, :] += jnp.dot(dscores, rows(i, lane, 0), preferred_element_type=f32)
        n = at // key_blk if isinstance(at, int) else lax.div(at, key_blk)
        dqt_ref[:, lane:] += jnp.dot(keyt_ref[n], dscores, preferred_element_type=f32)

    zero = jnp.zeros((8, query_blk), f32)
    total = jnp.zeros((1, head), f32)
    stats = None
    for i in range(count + 1):
        sums = (zero, zero)
        if i > 0:
            dqt_ref[...] = jnp.zeros_like(dqt_ref)

            def both(j, sums, i=i, stats=stats):
                second(i - 1, j * key_blk, 0, stats)
                return first(i, j * key_blk, 0, sums, False) if i < count else sums

            if i > 1:
                sums = lax.fori_loop(0, (i - 1) * per, both, sums, unroll=2)
            for n in range(per):
                at = (i - 1) * query_blk + n * key_blk
                second(i - 1, at, n * key_blk, stats)
                if i < count:
                    sums = first(i, at, 0, sums, False)
        if i < count:
            for n in range(per):
                sums = first(i, i * query_blk + n * key_blk, n * key_blk, sums, True)
        if i > 0:
            dq = dqt_ref[...].T * scaling
            at = query_blk // lanes
            dq_ref[(i - 1) * at : i * at] = dq.reshape(at, lanes, head)
            total = total + jnp.sum(dq * rows(i - 1, 0, 0).astype(f32), axis=0, keepdims=True)
        if i < count:
            inv_sum = 1.0 / jnp.sum(sums[0], axis=0, keepdims=True)
            stats = (inv_sum, jnp.sum(sums[1], axis=0, keepdims=True) * inv_sum)

    key_total = jnp.zeros((1, head), f32)
    for n in range(patches // key_blk):
        at = pl.ds(n * key_blk, key_blk)
        dk = dk_ref[at, :] * scaling
        dk_ref[at, :] = dk
        key_total = key_total + jnp.sum(dk * key_ref[at, :].astype(f32), axis=0, keepdims=True)

    for c in range(chips):
        mine, theirs = places(c)
        keep_ref[c, :own, :] = dk_ref[mine, :]
        keep_ref[c, own:, :] = dv_ref[mine, :]
        give_ref[c, :own, :] = dk_ref[theirs, :].astype(bf16)
        give_ref[c, own:, :] = dv_ref[theirs, :].astype(bf16)
    gains = jnp.concatenate([total / qgain_ref[...], key_total / kgain_ref[...]], axis=0)
    parts = in_parts(gains)
    gain_ref[...] = parts
    give_ref[chips] = jnp.concatenate([parts, jnp.zeros((lanes - extra, head), f32)], axis=0).astype(bf16)


def in_parts(gains):
    high = gains.astype(bf16).astype(f32)
    middle = (gains - high).astype(bf16).astype(f32)
    low = (gains - high - middle).astype(bf16).astype(f32)
    return jnp.concatenate([high, middle, low, jnp.zeros((extra - 6, head), f32)], axis=0)


def joined(parts):
    return parts[0:2] + parts[2:4] + parts[4:6]


def norm_back(delta, gain, mean):
    inverse = inverse_rms(mean)
    unit = mean * inverse
    scaled = delta * gain
    return inverse * (scaled - unit * jnp.mean(scaled * unit, axis=-1, keepdims=True))


def merge_kernel(dq_ref, keep_ref, got_ref, gain_ref, qmean_ref, kmean_ref, inv_ref, qgain_ref, kgain_ref, out_ref):
    chips, own, _ = inv_ref.shape
    tail = in_parts(joined(gain_ref[...]) + joined(got_ref[chips].astype(f32)))
    for c in range(chips):
        inv_len = inv_ref[c]
        kept = keep_ref[c] + got_ref[c].astype(f32)
        queries = norm_back(dq_ref[c], qgain_ref[...], qmean_ref[c])
        rows = [
            queries[:own] * inv_len,
            queries[own:] * inv_len,
            norm_back(kept[:own], kgain_ref[...], kmean_ref[c]) * inv_len,
            kept[own:] * inv_len,
            tail,
        ]
        out_ref[c] = jnp.concatenate(rows, axis=0).astype(bf16)


def back_kernel(shard_ref, x_ref, rows_ref, mate_ref, far_ref, gain_ref):
    chips = x_ref.shape[0]
    chunks, own, width = rows_ref.shape
    per = 2 * chips // chunks
    groups = (width // head - per) * chunks // 2
    repeat = chips // groups
    even = is_even(shard_ref)

    def query_rows(h):
        return x_ref[h // 2, h % 2 * own : (h % 2 + 1) * own, :].astype(f32)

    def keyval_rows(n):
        part, group = n // groups, n % groups
        rows = slice((2 + part) * own, (3 + part) * own)
        terms = [x_ref[group * repeat + r, rows, :].astype(f32) for r in range(repeat)]
        return sum(terms[1:], terms[0])

    tiles = 2 * groups // chunks
    for c in range(chunks):
        parts = [query_rows(c * per + n) for n in range(per)]
        parts += [keyval_rows(c * tiles + n) for n in range(tiles)]
        for n, part in enumerate(parts):
            rows_ref[c, :, n * head : (n + 1) * head] = part.astype(bf16)
        lone = jnp.concatenate([part[own - edge - 1 : own - edge] for part in parts], axis=1)
        lone = folded(lone, head)
        for_next = jnp.concatenate([part[own - edge :] for part in parts] + [lone], axis=1)
        for_prev = jnp.concatenate([part[:edge] for part in parts] + [jnp.zeros_like(lone)], axis=1)
        put_pair(even, mate_ref, far_ref, c, for_next.astype(bf16), for_prev.astype(bf16))

    tail = x_ref[0, 4 * own :, :].astype(f32)
    for c in range(1, chips):
        tail = tail + x_ref[c, 4 * own :, :].astype(f32)
    gain_ref[...] = joined(tail)


def spread_kernel(shard_ref, edges_ref, mate_ref, far_ref, rows_ref, query_ref, keyval_ref, query_buf, keyval_buf, sems):
    bytes_dev, query_width = query_ref.shape
    chunks, own, width = rows_ref.shape
    qcols, vcols = query_width // chunks, keyval_ref.shape[1] // chunks
    start = edges_ref[0:1, :]
    end = edges_ref[1:2, :]
    place = lax.broadcasted_iota(jnp.int32, (bytes_dev, 128), 0)
    pick = jnp.where((start <= place) & (place < end), 1.0, 0.0).astype(bf16)
    pick = pick[:, : below_rows + own + above_rows]
    even = is_even(shard_ref)
    running = []
    for c in range(chunks):
        after, before = get_pair(even, mate_ref, far_ref, c)
        lone = bottom(unfolded(before[:, width:], width // head))
        early = jnp.concatenate([lone, before[:, :width]], axis=0).astype(bf16)
        rows = jnp.concatenate([early, rows_ref[c], after[:, :width].astype(bf16)], axis=0)
        out = jnp.dot(pick, rows, preferred_element_type=f32).astype(bf16)
        query_buf[:, c * qcols : (c + 1) * qcols] = out[:, :qcols]
        keyval_buf[:, c * vcols : (c + 1) * vcols] = out[:, qcols:]
        for n, (buf, ref, cols) in enumerate(((query_buf, query_ref, qcols), (keyval_buf, keyval_ref, vcols))):
            at = c * cols
            copy = pltpu.make_async_copy(buf.at[:, at : at + cols], ref.at[:, at : at + cols], sems.at[c, n])
            copy.start()
            running.append(copy)
    for copy in running:
        copy.wait()


def shards(byte_query, byte_key_value, out_grads, patch_starts, query_gain, key_gain):
    byte_query, byte_key_value, out_grads = byte_query[0], byte_key_value[0], out_grads[0]
    bytes_dev, query_width = byte_query.shape
    keyval_width = byte_key_value.shape[1]
    devices = lax.axis_size("ctx")
    chips = devices // 2
    shard = lax.axis_index("ctx")
    patches = patch_starts.shape[1]
    own = patches // devices
    chunks = 4
    qcols, kcols = query_width // chunks, keyval_width // 2 // chunks
    chunk_cols = 2 * qcols + 2 * kcols

    which = shard.astype(jnp.int32).reshape(1)

    def shape(kind, *dims):
        return jax.ShapeDtypeStruct(dims, kind)

    smem = pl.BlockSpec(memory_space=pltpu.SMEM)
    vmem = pl.BlockSpec(memory_space=pltpu.VMEM)
    hbm = pl.BlockSpec(memory_space=pltpu.HBM)
    mates = [(i, i ^ 1) for i in range(devices)]
    fars = [(i, i + 1) for i in range(1, devices - 1, 2)]
    fars = fars + [(j, i) for i, j in fars]

    def traded(mate, far):
        return lax.ppermute(mate, "ctx", mates), lax.ppermute(far, "ctx", fars)

    wide = chunk_cols + 2 * head
    inputs = (patch_starts, byte_query, byte_key_value, out_grads)
    sums, rims, edges = pl.pallas_call(
        pool_kernel,
        in_specs=[smem] + [hbm] * 4,
        out_specs=[vmem] * 3,
        out_shape=[
            shape(f32, chunks, own, chunk_cols),
            shape(bf16, chunks, 2 * edge, wide),
            shape(jnp.int32, 2, 128),
        ],
        scratch_shapes=[
            pltpu.VMEM((bytes_dev, query_width), bf16),
            pltpu.VMEM((bytes_dev, keyval_width), bf16),
            pltpu.VMEM((bytes_dev, query_width), bf16),
            pltpu.VMEM((1, patches), jnp.int32),
            pltpu.SemaphoreType.DMA((chunks + 1, 4)),
        ],
        compiler_params=limit(20),
        name="pool",
    )(which, *(pltpu.with_memory_space_constraint(x, pltpu.HBM) for x in inputs))
    rims = lax.ppermute(rims, "ctx", mates)

    send = pl.pallas_call(
        send_kernel,
        in_specs=[smem] + [vmem] * 2,
        out_specs=vmem,
        out_shape=shape(bf16, chips, 6 * (own + edge) + edge, head),
        compiler_params=limit(20),
        name="send",
    )(which, sums, rims)

    sides = [list(range(n, devices, 2)) for n in range(2)]
    mine = lax.all_to_all(send, "ctx", 0, 0, tiled=True, axis_index_groups=sides)
    qgain, kgain = query_gain[None], key_gain[None]
    pair = (chips, 2 * own, head)
    keyval, kmean, inv_len = pl.pallas_call(
        functools.partial(keys_kernel, document=bytes_dev * devices),
        in_specs=[smem] + [vmem] * 3,
        out_specs=[vmem] * 3,
        out_shape=[shape(bf16, *pair), shape(f32, chips, own, head), shape(f32, chips, own, head)],
        compiler_params=limit(20),
        name="keys",
    )(which, patch_starts, mine, kgain)
    other = lax.ppermute(keyval, "ctx", mates)
    query, grad, qmean = pl.pallas_call(
        queries_kernel,
        in_specs=[smem] + [vmem] * 3,
        out_specs=[vmem] * 3,
        out_shape=[shape(bf16, *pair), shape(bf16, *pair), shape(f32, *pair)],
        compiler_params=limit(20),
        name="queries",
    )(which, mine, inv_len, qgain)

    block = (patches, head)
    dq, keep, give, gains = pl.pallas_call(
        attend_kernel,
        in_specs=[smem] + [vmem] * 6,
        out_specs=[vmem] * 4,
        out_shape=[
            shape(f32, *pair),
            shape(f32, *pair),
            shape(bf16, chips + 1, 2 * own, head),
            shape(f32, extra, head),
        ],
        scratch_shapes=[pltpu.VMEM(block, bf16)] * 2
        + [pltpu.VMEM((patches // key_blk, head, key_blk), bf16)]
        + [pltpu.VMEM((patches - query_blk, query_blk), f32), pltpu.VMEM((patches, query_blk), f32)] * 2
        + [pltpu.VMEM(block, f32)] * 2
        + [pltpu.VMEM((head, query_blk), f32)],
        compiler_params=limit(36),
        name="attend",
    )(which, query, grad, keyval, other, qgain, kgain)
    got = lax.ppermute(give, "ctx", mates)

    back = pl.pallas_call(
        merge_kernel,
        in_specs=[vmem] * 9,
        out_specs=vmem,
        out_shape=shape(bf16, chips, 4 * own + extra, head),
        compiler_params=limit(16),
        name="merge",
    )(dq, keep, got, gains, qmean, kmean, inv_len, qgain, kgain)
    home = lax.all_to_all(back, "ctx", 0, 0, tiled=True, axis_index_groups=sides)

    vcols = keyval_width // chunks
    wide = qcols + vcols + head
    rows, mate, far, gains = pl.pallas_call(
        back_kernel,
        in_specs=[smem, vmem],
        out_specs=[vmem] * 4,
        out_shape=[
            shape(bf16, chunks, own, qcols + vcols),
            shape(bf16, chunks, edge, wide),
            shape(bf16, chunks, edge, wide),
            shape(f32, 2, head),
        ],
        compiler_params=limit(20),
        name="back",
    )(which, home)
    mate, far = traded(mate, far)
    mate, gains = lax.optimization_barrier((mate, gains))
    docs = lax.axis_size("dp")
    turned = [lax.ppermute(gains, "dp", [(i, (i + n) % docs) for i in range(docs)]) for n in (1, 3, 2)]
    gains = (gains + turned[2]) + (turned[0] + turned[1])

    query_out, keyval_out = pl.pallas_call(
        spread_kernel,
        in_specs=[smem] + [vmem] * 4,
        out_specs=[hbm] * 2,
        out_shape=[shape(bf16, bytes_dev, query_width), shape(bf16, bytes_dev, keyval_width)],
        scratch_shapes=[
            pltpu.VMEM((bytes_dev, query_width), bf16),
            pltpu.VMEM((bytes_dev, keyval_width), bf16),
            pltpu.SemaphoreType.DMA((chunks, 2)),
        ],
        compiler_params=limit(20),
        name="spread",
    )(which, edges, mate, far, rows)
    return (query_out[None], keyval_out[None], gains[0], gains[1])


def solution(mesh):
    placed = (
        P("dp", "ctx", None),
        P("dp", "ctx", None),
        P("dp", "ctx", None),
        P("dp", None),
        P(),
        P(),
    )
    return jax.shard_map(
        shards,
        mesh=mesh,
        in_specs=placed,
        out_specs=(P("dp", "ctx", None), P("dp", "ctx", None), P(), P()),
        check_vma=False,
    )
```

```python
import functools
import math

import jax
import jax.numpy as jnp
from jax import lax
from jax.experimental import pallas as pl
from jax.experimental.pallas import tpu as pltpu
from jax.sharding import PartitionSpec as P

eps_norm = 1e-06
head = 128
below_rows = 32
above_rows = 16
edge = 16
query_blk = 1024
key_blk = 256
extra = 8
f32 = jnp.float32
bf16 = jnp.bfloat16
nt = (((1,), (1,)), ((), ()))


def limit(mib):
    return pltpu.CompilerParams(vmem_limit_bytes=mib * 1024 * 1024)


def folded(row, width):
    pieces = [row[:, at : at + width] for at in range(0, row.shape[1], width)]
    return jnp.concatenate(pieces + [jnp.zeros((edge - len(pieces), width), f32)], axis=0)


def unfolded(block, count):
    return jnp.concatenate([block[n : n + 1] for n in range(count)], axis=1)


def bottom(row):
    at = lax.broadcasted_iota(jnp.int32, (edge, row.shape[1]), 0)
    return jnp.where(at == edge - 1, row, 0.0)


def is_even(shard_ref):
    return lax.rem(shard_ref[0], 2) == 0


def put_pair(even, mate_ref, far_ref, at, for_next, for_prev):
    @pl.when(even)
    def _():
        mate_ref[at] = for_next
        far_ref[at] = for_prev

    @pl.when(jnp.logical_not(even))
    def _():
        mate_ref[at] = for_prev
        far_ref[at] = for_next


def get_pair(even, mate_ref, far_ref, at):
    mate, far = mate_ref[at].astype(f32), far_ref[at].astype(f32)
    return jnp.where(even, mate, far), jnp.where(even, far, mate)


def pool_kernel(
    shard_ref,
    starts_ref,
    query_ref,
    keyval_ref,
    grad_ref,
    own_ref,
    rims_ref,
    edges_ref,
    query_buf,
    keyval_buf,
    grad_buf,
    starts_buf,
    sems,
):
    bytes_dev, query_width = query_ref.shape
    half = keyval_ref.shape[1] // 2
    patches = starts_ref.shape[1]
    chunks, own, _ = own_ref.shape
    qcols, kcols = query_width // chunks, half // chunks
    shard = shard_ref[0]
    used = below_rows + own + above_rows

    def parts(c):
        return (
            (query_ref, query_buf, c * qcols, qcols),
            (grad_ref, grad_buf, c * qcols, qcols),
            (keyval_ref, keyval_buf, c * kcols, kcols),
            (keyval_ref, keyval_buf, half + c * kcols, kcols),
        )

    def copies(c):
        return [
            pltpu.make_async_copy(ref.at[:, at : at + width], buf.at[:, at : at + width], sems.at[c, n])
            for n, (ref, buf, at, width) in enumerate(parts(c))
        ]

    starts_copy = pltpu.make_async_copy(starts_ref, starts_buf, sems.at[chunks, 0])
    starts_copy.start()
    for c in range(chunks):
        for copy in copies(c):
            copy.start()

    first_patch = shard * own - below_rows
    starts_copy.wait()
    around = jnp.broadcast_to(starts_buf[...], (8, patches))
    around = pltpu.roll(around, lax.rem(patches - first_patch, patches), 1)
    lane = lax.broadcasted_iota(jnp.int32, (1, 128), 1) + first_patch

    def limited(values, at):
        values = jnp.where(at < 0, 0, jnp.where(at >= patches, bytes_dev * (patches // own), values))
        return values - shard * bytes_dev

    start = limited(around[0:1, 0:128], lane)
    end = limited(around[0:1, 1:129], lane + 1)
    edges_ref[0:1, :] = start
    edges_ref[1:2, :] = end
    place = lax.broadcasted_iota(jnp.int32, (bytes_dev, 128), 0)
    inside = jnp.where((start <= place) & (place < end), 1.0, 0.0)
    pick = inside.T.astype(bf16)[:used, :]
    for c in range(chunks):
        for copy in copies(c):
            copy.wait()
        out = 0
        below, above, lone = [], [], []
        for _, buf, at, width in parts(c):
            sums = jnp.dot(pick, buf[:, at : at + width], preferred_element_type=f32)
            own_ref[c, :, out : out + width] = sums[below_rows : below_rows + own]
            lone.append(sums[edge - 1 : edge])
            below.append(sums[edge:below_rows])
            above.append(sums[below_rows + own :])
            out += width
        lone = folded(jnp.concatenate(lone, axis=1), 2 * head)
        rims_ref[c, :edge, :] = jnp.concatenate(below + [lone], axis=1).astype(bf16)
        rims_ref[c, edge:, :] = jnp.concatenate(above + [jnp.zeros_like(lone)], axis=1).astype(bf16)


def rimmed(rows, early, lone, late):
    gap = jnp.zeros((rows.shape[0] - 3 * edge, rows.shape[1]), f32)
    return rows + jnp.concatenate([early, gap, bottom(lone), late], axis=0)


def send_kernel(shard_ref, own_ref, rims_ref, send_ref):
    chunks, own, width = own_ref.shape
    heads = 2 * send_ref.shape[0] // chunks
    groups = (width // head - 2 * heads) // 2
    even = is_even(shard_ref)

    def chunk(c, carry):
        got = rims_ref[c].astype(f32)
        below, above, lone = got[:edge, :width], got[edge:, :width], unfolded(got[:edge, width:], width // (2 * head))
        early, late = jnp.where(even, 0.0, above), jnp.where(even, below, 0.0)
        far, far_lone = jnp.where(even, above, below), jnp.where(even, 0.0, lone)
        lone = jnp.where(even, lone, 0.0)

        def put(chip, part, tile):
            cols = slice(tile * head, (tile + 1) * head)
            rows = rimmed(own_ref[c, :, cols], early[:, cols], lone[:, cols], late[:, cols])
            send_ref[chip, part * own : (part + 1) * own, :] = rows.astype(bf16)
            at = 6 * own + part * edge
            send_ref[chip, at : at + edge, :] = far[:, cols].astype(bf16)
            return far_lone[:, cols]

        for n in range(heads // 2):
            chip = c * heads // 2 + n
            group = n * groups // (heads // 2)
            tiles = [2 * n, 2 * n + 1, heads + 2 * n, heads + 2 * n + 1, 2 * heads + group, 2 * heads + groups + group]
            ends = [put(chip, part, tile) for part, tile in enumerate(tiles)]
            ends = jnp.concatenate(ends + [jnp.zeros((extra - 6, head), f32)], axis=0)
            send_ref[chip, 6 * (own + edge) :, :] = ends.astype(bf16)
        return carry

    lax.fori_loop(0, chunks, chunk, 0)


def summed_part(mine_ref, even, c, part, own):
    chips = mine_ref.shape[0]
    at = 6 * own + part * edge
    none = jnp.zeros((edge, head), f32)
    early = late = none
    lone = none[:1]
    if c > 0:
        early = jnp.where(even, mine_ref[c - 1, at : at + edge, :].astype(f32), 0.0)
    if c < chips - 1:
        late = jnp.where(even, 0.0, mine_ref[c + 1, at : at + edge, :].astype(f32))
        lone = mine_ref[c + 1, 6 * (own + edge) :, :].astype(f32)[part : part + 1]
        lone = jnp.where(even, 0.0, lone)
    return rimmed(mine_ref[c, part * own : (part + 1) * own, :].astype(f32), early, lone, late)


def inverse_rms(rows):
    return lax.rsqrt(jnp.mean(rows * rows, axis=-1, keepdims=True) + eps_norm)


def lengths_kernel(shard_ref, starts_ref, inv_ref, *, document):
    chips, own, _ = inv_ref.shape
    lanes = starts_ref.shape[1] // chips
    starts = starts_ref[...].astype(f32)
    ends = jnp.concatenate([starts[:, 1:], jnp.full((1, 1), document, f32)], axis=1)
    lengths = ends - starts
    table = jnp.concatenate([lengths[:, c * lanes : (c + 1) * lanes] for c in range(chips)], axis=0)
    table = 1.0 / table.T
    table = jnp.where(is_even(shard_ref), table[:own], table[own:])
    for c in range(chips):
        inv_ref[c] = jnp.broadcast_to(table[:, c : c + 1], (own, head))


def keys_kernel(shard_ref, mine_ref, inv_ref, kgain_ref, keyval_ref, mean_ref):
    chips, own, _ = inv_ref.shape
    even = is_even(shard_ref)
    for c in range(chips):
        inv_len = inv_ref[c]
        rows = summed_part(mine_ref, even, c, 4, own) * inv_len
        mean_ref[c] = rows
        keyval_ref[c, :own, :] = (rows * inverse_rms(rows) * kgain_ref[...]).astype(bf16)
        keyval_ref[c, own:, :] = (summed_part(mine_ref, even, c, 5, own) * inv_len).astype(bf16)


def queries_kernel(shard_ref, mine_ref, inv_ref, qgain_ref, query_ref, grad_ref, unit_ref, scale_ref):
    chips, own, _ = inv_ref.shape
    even = is_even(shard_ref)
    for c in range(chips):
        for n in range(2):
            at = slice(n * own, (n + 1) * own)
            rows = summed_part(mine_ref, even, c, n, own) * inv_ref[c]
            inverse = inverse_rms(rows)
            unit = rows * inverse
            unit_ref[c, at, :] = unit
            scale_ref[c, at, :] = inverse * inv_ref[c]
            query_ref[c, at, :] = (unit * qgain_ref[...]).astype(bf16)
            grad_ref[c, at, :] = summed_part(mine_ref, even, c, 2 + n, own).astype(bf16)


def attend_kernel(
    shard_ref,
    query_ref,
    grad_ref,
    mine_ref,
    other_ref,
    qgain_ref,
    kgain_ref,
    dq_ref,
    keep_ref,
    give_ref,
    gain_ref,
    key_ref,
    value_ref,
    keyt_ref,
    raised0_ref,
    raised1_ref,
    dw0_ref,
    dw1_ref,
    dk_ref,
    dv_ref,
    dqt_ref,
):
    chips, own = mine_ref.shape[0], mine_ref.shape[1] // 2
    patches = key_ref.shape[0]
    per = query_blk // key_blk
    count = patches // query_blk
    lanes = 2 * own
    scaling = head ** (-0.5)
    raising = scaling * math.log2(math.e)
    raised_refs, dw_refs = (raised0_ref, raised1_ref), (dw0_ref, dw1_ref)
    side = lax.rem(shard_ref[0], 2)

    def places(c):
        mine = pl.multiple_of(c * lanes + side * own, own)
        theirs = pl.multiple_of(c * lanes + (1 - side) * own, own)
        return pl.ds(mine, own), pl.ds(theirs, own)

    for c in range(chips):
        mine, theirs = places(c)
        key_ref[mine, :] = mine_ref[c, :own, :]
        value_ref[mine, :] = mine_ref[c, own:, :]
        key_ref[theirs, :] = other_ref[c, :own, :]
        value_ref[theirs, :] = other_ref[c, own:, :]

    for n in range(patches // key_blk):
        keyt_ref[n] = key_ref[pl.ds(n * key_blk, key_blk), :].astype(f32).T.astype(bf16)
    dk_ref[...] = jnp.zeros_like(dk_ref)
    dv_ref[...] = jnp.zeros_like(dv_ref)

    def fold(block):
        return jnp.sum(block.reshape(block.shape[0] // 8, 8, block.shape[1]), axis=0)

    def rows(i, lane, part):
        first_chip, last_chip = (i * query_blk + lane) // lanes, (i + 1) * query_blk // lanes
        block = (query_ref, grad_ref)[part][first_chip:last_chip]
        return block.reshape(query_blk - lane, head)

    def first(i, at, lane, sums, diagonal):
        keys = pl.ds(at, key_blk)
        scores = lax.dot_general(key_ref[keys, :], rows(i, lane, 0), nt, preferred_element_type=f32)
        raised = jnp.exp2(scores * raising)
        if diagonal:
            key_at = lax.broadcasted_iota(jnp.int32, raised.shape, 0)
            query_at = lax.broadcasted_iota(jnp.int32, raised.shape, 1)
            query_at = query_at - lax.bitwise_and(query_at, own) + side * own
            raised = jnp.where(key_at <= query_at, raised, 0.0)
        dweights = lax.dot_general(value_ref[keys, :], rows(i, lane, 1), nt, preferred_element_type=f32)
        raised_refs[i % 2][keys, lane:] = raised
        dw_refs[i % 2][keys, lane:] = dweights
        added = fold(raised), fold(raised * dweights)
        if lane:
            none = jnp.zeros((8, lane), f32)
            added = tuple(jnp.concatenate([none, x], axis=1) for x in added)
        return (sums[0] + added[0], sums[1] + added[1])

    def second(i, at, lane, stats):
        keys = pl.ds(at, key_blk)
        inv_sum, delta = stats[0][:, lane:], stats[1][:, lane:]
        weights = raised_refs[i % 2][keys, lane:] * inv_sum
        dscores = (weights * (dw_refs[i % 2][keys, lane:] - delta)).astype(bf16)
        dv_ref[keys, :] += jnp.dot(weights.astype(bf16), rows(i, lane, 1), preferred_element_type=f32)
        dk_ref[keys, :] += jnp.dot(dscores, rows(i, lane, 0), preferred_element_type=f32)
        n = at // key_blk if isinstance(at, int) else lax.div(at, key_blk)
        dqt_ref[:, lane:] += jnp.dot(keyt_ref[n], dscores, preferred_element_type=f32)

    zero = jnp.zeros((8, query_blk), f32)
    total = jnp.zeros((1, head), f32)
    stats = None
    for i in range(count + 1):
        sums = (zero, zero)
        if i > 0:
            dqt_ref[...] = jnp.zeros_like(dqt_ref)

            def both(j, sums, i=i, stats=stats):
                second(i - 1, j * key_blk, 0, stats)
                return first(i, j * key_blk, 0, sums, False) if i < count else sums

            if i > 1:
                sums = lax.fori_loop(0, (i - 1) * per, both, sums, unroll=2)
            for n in range(per):
                at = (i - 1) * query_blk + n * key_blk
                second(i - 1, at, n * key_blk, stats)
                if i < count:
                    sums = first(i, at, 0, sums, False)
        if i < count:
            for n in range(per):
                sums = first(i, i * query_blk + n * key_blk, n * key_blk, sums, True)
        if i > 0:
            dq = dqt_ref[...].T * scaling
            at = query_blk // lanes
            dq_ref[(i - 1) * at : i * at] = dq.reshape(at, lanes, head)
            total = total + jnp.sum(dq * rows(i - 1, 0, 0).astype(f32), axis=0, keepdims=True)
        if i < count:
            inv_sum = 1.0 / jnp.sum(sums[0], axis=0, keepdims=True)
            stats = (inv_sum, jnp.sum(sums[1], axis=0, keepdims=True) * inv_sum)

    key_total = jnp.zeros((1, head), f32)
    for n in range(patches // key_blk):
        at = pl.ds(n * key_blk, key_blk)
        dk = dk_ref[at, :] * scaling
        dk_ref[at, :] = dk
        key_total = key_total + jnp.sum(dk * key_ref[at, :].astype(f32), axis=0, keepdims=True)

    for c in range(chips):
        mine, theirs = places(c)
        keep_ref[c, :own, :] = dk_ref[mine, :]
        keep_ref[c, own:, :] = dv_ref[mine, :]
        give_ref[c, :own, :] = dk_ref[theirs, :].astype(bf16)
        give_ref[c, own:, :] = dv_ref[theirs, :].astype(bf16)
    gains = jnp.concatenate([total / qgain_ref[...], key_total / kgain_ref[...]], axis=0)
    parts = in_parts(gains)
    gain_ref[...] = parts
    give_ref[chips] = jnp.concatenate([parts, jnp.zeros((lanes - extra, head), f32)], axis=0).astype(bf16)


def in_parts(gains):
    high = gains.astype(bf16).astype(f32)
    middle = (gains - high).astype(bf16).astype(f32)
    low = (gains - high - middle).astype(bf16).astype(f32)
    return jnp.concatenate([high, middle, low, jnp.zeros((extra - 6, head), f32)], axis=0)


def joined(parts):
    return parts[0:2] + parts[2:4] + parts[4:6]


def norm_back(delta, gain, unit, scale):
    scaled = delta * gain
    return scale * (scaled - unit * jnp.mean(scaled * unit, axis=-1, keepdims=True))


def finish_kernel(dq_ref, unit_ref, scale_ref, qgain_ref, kmean_ref, inv_ref, rows_ref, kunit_ref, kscale_ref):
    for c in range(rows_ref.shape[0]):
        rows_ref[c] = norm_back(dq_ref[c], qgain_ref[...], unit_ref[c], scale_ref[c]).astype(bf16)
        mean = kmean_ref[c]
        inverse = inverse_rms(mean)
        kunit_ref[c] = mean * inverse
        kscale_ref[c] = inverse * inv_ref[c]


def merge_kernel(rows_ref, keep_ref, got_ref, gain_ref, kunit_ref, kscale_ref, inv_ref, kgain_ref, out_ref):
    chips, own, _ = inv_ref.shape
    tail = in_parts(joined(gain_ref[...]) + joined(got_ref[chips].astype(f32)))
    for c in range(chips):
        kept = keep_ref[c] + got_ref[c].astype(f32)
        keys = norm_back(kept[:own], kgain_ref[...], kunit_ref[c], kscale_ref[c])
        rest = jnp.concatenate([keys, kept[own:] * inv_ref[c], tail], axis=0)
        out_ref[c, : 2 * own, :] = rows_ref[c]
        out_ref[c, 2 * own :, :] = rest.astype(bf16)


def back_kernel(shard_ref, x_ref, rows_ref, mate_ref, far_ref, gain_ref):
    chips = x_ref.shape[0]
    chunks, own, width = rows_ref.shape
    per = 2 * chips // chunks
    groups = (width // head - per) * chunks // 2
    repeat = chips // groups
    even = is_even(shard_ref)

    def query_rows(h):
        return x_ref[h // 2, h % 2 * own : (h % 2 + 1) * own, :].astype(f32)

    def keyval_rows(n):
        part, group = n // groups, n % groups
        rows = slice((2 + part) * own, (3 + part) * own)
        terms = [x_ref[group * repeat + r, rows, :].astype(f32) for r in range(repeat)]
        return sum(terms[1:], terms[0])

    tiles = 2 * groups // chunks
    for c in range(chunks):
        parts = [query_rows(c * per + n) for n in range(per)]
        parts += [keyval_rows(c * tiles + n) for n in range(tiles)]
        for n, part in enumerate(parts):
            rows_ref[c, :, n * head : (n + 1) * head] = part.astype(bf16)
        lone = jnp.concatenate([part[own - edge - 1 : own - edge] for part in parts], axis=1)
        lone = folded(lone, head)
        for_next = jnp.concatenate([part[own - edge :] for part in parts] + [lone], axis=1)
        for_prev = jnp.concatenate([part[:edge] for part in parts] + [jnp.zeros_like(lone)], axis=1)
        put_pair(even, mate_ref, far_ref, c, for_next.astype(bf16), for_prev.astype(bf16))

    tail = x_ref[0, 4 * own :, :].astype(f32)
    for c in range(1, chips):
        tail = tail + x_ref[c, 4 * own :, :].astype(f32)
    gain_ref[...] = joined(tail)


def spread_kernel(shard_ref, edges_ref, mate_ref, far_ref, rows_ref, query_ref, keyval_ref, query_buf, keyval_buf, sems):
    bytes_dev, query_width = query_ref.shape
    chunks, own, width = rows_ref.shape
    qcols, vcols = query_width // chunks, keyval_ref.shape[1] // chunks
    start = edges_ref[0:1, :]
    end = edges_ref[1:2, :]
    place = lax.broadcasted_iota(jnp.int32, (bytes_dev, 128), 0)
    pick = jnp.where((start <= place) & (place < end), 1.0, 0.0).astype(bf16)
    pick = pick[:, : below_rows + own + above_rows]
    even = is_even(shard_ref)
    running = []
    for c in range(chunks):
        after, before = get_pair(even, mate_ref, far_ref, c)
        lone = bottom(unfolded(before[:, width:], width // head))
        early = jnp.concatenate([lone, before[:, :width]], axis=0).astype(bf16)
        rows = jnp.concatenate([early, rows_ref[c], after[:, :width].astype(bf16)], axis=0)
        out = jnp.dot(pick, rows, preferred_element_type=f32).astype(bf16)
        query_buf[:, c * qcols : (c + 1) * qcols] = out[:, :qcols]
        keyval_buf[:, c * vcols : (c + 1) * vcols] = out[:, qcols:]
        for n, (buf, ref, cols) in enumerate(((query_buf, query_ref, qcols), (keyval_buf, keyval_ref, vcols))):
            at = c * cols
            copy = pltpu.make_async_copy(buf.at[:, at : at + cols], ref.at[:, at : at + cols], sems.at[c, n])
            copy.start()
            running.append(copy)
    for copy in running:
        copy.wait()


def shards(byte_query, byte_key_value, out_grads, patch_starts, query_gain, key_gain):
    byte_query, byte_key_value, out_grads = byte_query[0], byte_key_value[0], out_grads[0]
    bytes_dev, query_width = byte_query.shape
    keyval_width = byte_key_value.shape[1]
    devices = lax.axis_size("ctx")
    chips = devices // 2
    shard = lax.axis_index("ctx")
    patches = patch_starts.shape[1]
    own = patches // devices
    chunks = 4
    qcols, kcols = query_width // chunks, keyval_width // 2 // chunks
    chunk_cols = 2 * qcols + 2 * kcols

    which = shard.astype(jnp.int32).reshape(1)

    def shape(kind, *dims):
        return jax.ShapeDtypeStruct(dims, kind)

    smem = pl.BlockSpec(memory_space=pltpu.SMEM)
    vmem = pl.BlockSpec(memory_space=pltpu.VMEM)
    hbm = pl.BlockSpec(memory_space=pltpu.HBM)
    mates = [(i, i ^ 1) for i in range(devices)]
    fars = [(i, i + 1) for i in range(1, devices - 1, 2)]
    fars = fars + [(j, i) for i, j in fars]

    def traded(mate, far):
        return lax.ppermute(mate, "ctx", mates), lax.ppermute(far, "ctx", fars)

    wide = chunk_cols + 2 * head
    inputs = (patch_starts, byte_query, byte_key_value, out_grads)
    sums, rims, edges = pl.pallas_call(
        pool_kernel,
        in_specs=[smem] + [hbm] * 4,
        out_specs=[vmem] * 3,
        out_shape=[
            shape(f32, chunks, own, chunk_cols),
            shape(bf16, chunks, 2 * edge, wide),
            shape(jnp.int32, 2, 128),
        ],
        scratch_shapes=[
            pltpu.VMEM((bytes_dev, query_width), bf16),
            pltpu.VMEM((bytes_dev, keyval_width), bf16),
            pltpu.VMEM((bytes_dev, query_width), bf16),
            pltpu.VMEM((1, patches), jnp.int32),
            pltpu.SemaphoreType.DMA((chunks + 1, 4)),
        ],
        compiler_params=limit(20),
        name="pool",
    )(which, *(pltpu.with_memory_space_constraint(x, pltpu.HBM) for x in inputs))
    rims = lax.ppermute(rims, "ctx", mates)
    inv_len = pl.pallas_call(
        functools.partial(lengths_kernel, document=bytes_dev * devices),
        in_specs=[smem, vmem],
        out_specs=vmem,
        out_shape=shape(f32, chips, own, head),
        compiler_params=limit(16),
        name="lengths",
    )(which, patch_starts)
    rims, inv_len = lax.optimization_barrier((rims, inv_len))

    send = pl.pallas_call(
        send_kernel,
        in_specs=[smem] + [vmem] * 2,
        out_specs=vmem,
        out_shape=shape(bf16, chips, 6 * (own + edge) + extra, head),
        compiler_params=limit(20),
        name="send",
    )(which, sums, rims)

    sides = [list(range(n, devices, 2)) for n in range(2)]
    mine = lax.all_to_all(send, "ctx", 0, 0, tiled=True, axis_index_groups=sides)
    qgain, kgain = query_gain[None], key_gain[None]
    pair = (chips, 2 * own, head)
    keyval, kmean = pl.pallas_call(
        keys_kernel,
        in_specs=[smem] + [vmem] * 3,
        out_specs=[vmem] * 2,
        out_shape=[shape(bf16, *pair), shape(f32, chips, own, head)],
        compiler_params=limit(20),
        name="keys",
    )(which, mine, inv_len, kgain)
    other = lax.ppermute(keyval, "ctx", mates)
    query, grad, qunit, qscale = pl.pallas_call(
        queries_kernel,
        in_specs=[smem] + [vmem] * 3,
        out_specs=[vmem] * 4,
        out_shape=[shape(bf16, *pair), shape(bf16, *pair), shape(f32, *pair), shape(f32, *pair)],
        compiler_params=limit(20),
        name="queries",
    )(which, mine, inv_len, qgain)

    block = (patches, head)
    dq, keep, give, gains = pl.pallas_call(
        attend_kernel,
        in_specs=[smem] + [vmem] * 6,
        out_specs=[vmem] * 4,
        out_shape=[
            shape(f32, *pair),
            shape(f32, *pair),
            shape(bf16, chips + 1, 2 * own, head),
            shape(f32, extra, head),
        ],
        scratch_shapes=[pltpu.VMEM(block, bf16)] * 2
        + [pltpu.VMEM((patches // key_blk, head, key_blk), bf16)]
        + [pltpu.VMEM((patches - query_blk, query_blk), f32), pltpu.VMEM((patches, query_blk), f32)] * 2
        + [pltpu.VMEM(block, f32)] * 2
        + [pltpu.VMEM((head, query_blk), f32)],
        compiler_params=limit(36),
        name="attend",
    )(which, query, grad, keyval, other, qgain, kgain)
    got = lax.ppermute(give, "ctx", mates)

    rows, kunit, kscale = pl.pallas_call(
        finish_kernel,
        in_specs=[vmem] * 6,
        out_specs=[vmem] * 3,
        out_shape=[shape(bf16, *pair), shape(f32, chips, own, head), shape(f32, chips, own, head)],
        compiler_params=limit(20),
        name="finish",
    )(dq, qunit, qscale, qgain, kmean, inv_len)
    back = pl.pallas_call(
        merge_kernel,
        in_specs=[vmem] * 8,
        out_specs=vmem,
        out_shape=shape(bf16, chips, 4 * own + extra, head),
        compiler_params=limit(16),
        name="merge",
    )(rows, keep, got, gains, kunit, kscale, inv_len, kgain)
    home = lax.all_to_all(back, "ctx", 0, 0, tiled=True, axis_index_groups=sides)

    vcols = keyval_width // chunks
    wide = qcols + vcols + head
    rows, mate, far, gains = pl.pallas_call(
        back_kernel,
        in_specs=[smem, vmem],
        out_specs=[vmem] * 4,
        out_shape=[
            shape(bf16, chunks, own, qcols + vcols),
            shape(bf16, chunks, edge, wide),
            shape(bf16, chunks, edge, wide),
            shape(f32, 2, head),
        ],
        compiler_params=limit(20),
        name="back",
    )(which, home)
    mate, far = traded(mate, far)
    mate, gains = lax.optimization_barrier((mate, gains))
    docs = lax.axis_size("dp")
    turned = [lax.ppermute(gains, "dp", [(i, (i + n) % docs) for i in range(docs)]) for n in (1, 3, 2)]
    gains = (gains + turned[2]) + (turned[0] + turned[1])

    query_out, keyval_out = pl.pallas_call(
        spread_kernel,
        in_specs=[smem] + [vmem] * 4,
        out_specs=[hbm] * 2,
        out_shape=[shape(bf16, bytes_dev, query_width), shape(bf16, bytes_dev, keyval_width)],
        scratch_shapes=[
            pltpu.VMEM((bytes_dev, query_width), bf16),
            pltpu.VMEM((bytes_dev, keyval_width), bf16),
            pltpu.SemaphoreType.DMA((chunks, 2)),
        ],
        compiler_params=limit(20),
        name="spread",
    )(which, edges, mate, far, rows)
    return (query_out[None], keyval_out[None], gains[0], gains[1])


def solution(mesh):
    placed = (
        P("dp", "ctx", None),
        P("dp", "ctx", None),
        P("dp", "ctx", None),
        P("dp", None),
        P(),
        P(),
    )
    return jax.shard_map(
        shards,
        mesh=mesh,
        in_specs=placed,
        out_specs=(P("dp", "ctx", None), P("dp", "ctx", None), P(), P()),
        check_vma=False,
    )
```

```python
import functools
import math

import jax
import jax.numpy as jnp
from jax import lax
from jax.experimental import pallas as pl
from jax.experimental.pallas import tpu as pltpu
from jax.sharding import PartitionSpec as P

eps_norm = 1e-06
head = 128
below_rows = 32
above_rows = 16
edge = 16
query_blk = 1024
key_blk = 256
extra = 8
f32 = jnp.float32
bf16 = jnp.bfloat16
nt = (((1,), (1,)), ((), ()))


def limit(mib):
    return pltpu.CompilerParams(vmem_limit_bytes=mib * 1024 * 1024)


def folded(row, width):
    pieces = [row[:, at : at + width] for at in range(0, row.shape[1], width)]
    return jnp.concatenate(pieces + [jnp.zeros((edge - len(pieces), width), f32)], axis=0)


def unfolded(block, count):
    return jnp.concatenate([block[n : n + 1] for n in range(count)], axis=1)


def bottom(row):
    at = lax.broadcasted_iota(jnp.int32, (edge, row.shape[1]), 0)
    return jnp.where(at == edge - 1, row, 0.0)


def is_even(shard_ref):
    return lax.rem(shard_ref[0], 2) == 0


def pool_kernel(
    shard_ref,
    starts_ref,
    query_ref,
    keyval_ref,
    grad_ref,
    own_ref,
    rims_ref,
    edges_ref,
    query_buf,
    keyval_buf,
    grad_buf,
    starts_buf,
    sems,
):
    bytes_dev, query_width = query_ref.shape
    half = keyval_ref.shape[1] // 2
    patches = starts_ref.shape[1]
    chunks, own, _ = own_ref.shape
    qcols, kcols = query_width // chunks, half // chunks
    shard = shard_ref[0]
    used = below_rows + own + above_rows

    def parts(c):
        return (
            (query_buf, c * qcols, qcols),
            (grad_buf, c * qcols, qcols),
            (keyval_buf, c * kcols, kcols),
            (keyval_buf, half + c * kcols, kcols),
        )

    def copies(c):
        cols = slice(c * qcols, (c + 1) * qcols)
        pairs = [(query_ref.at[:, cols], query_buf.at[:, cols]), (grad_ref.at[:, cols], grad_buf.at[:, cols])]
        if c == 0:
            pairs = [(keyval_ref, keyval_buf)] + pairs
        return [pltpu.make_async_copy(ref, buf, sems.at[c, n]) for n, (ref, buf) in enumerate(pairs)]

    starts_copy = pltpu.make_async_copy(starts_ref, starts_buf, sems.at[chunks, 0])
    starts_copy.start()
    for c in range(chunks):
        for copy in copies(c):
            copy.start()

    first_patch = shard * own - below_rows
    starts_copy.wait()
    around = jnp.broadcast_to(starts_buf[...], (8, patches))
    around = pltpu.roll(around, lax.rem(patches - first_patch, patches), 1)
    lane = lax.broadcasted_iota(jnp.int32, (1, 128), 1) + first_patch

    def limited(values, at):
        values = jnp.where(at < 0, 0, jnp.where(at >= patches, bytes_dev * (patches // own), values))
        return values - shard * bytes_dev

    start = limited(around[0:1, 0:128], lane)
    end = limited(around[0:1, 1:129], lane + 1)
    edges_ref[0:1, :] = start
    edges_ref[1:2, :] = end
    place = lax.broadcasted_iota(jnp.int32, (bytes_dev, 128), 0)
    inside = jnp.where((start <= place) & (place < end), 1.0, 0.0)
    pick = inside.T.astype(bf16)[:used, :]
    for c in range(chunks):
        for copy in copies(c):
            copy.wait()
        out = 0
        below, above, lone = [], [], []
        for buf, at, width in parts(c):
            sums = jnp.dot(pick, buf[:, at : at + width], preferred_element_type=f32)
            own_ref[c, :, out : out + width] = sums[below_rows : below_rows + own]
            lone.append(sums[edge - 1 : edge])
            below.append(sums[edge:below_rows])
            above.append(sums[below_rows + own :])
            out += width
        lone = folded(jnp.concatenate(lone, axis=1), 2 * head)
        rims_ref[c, :edge, :] = jnp.concatenate(below + [lone], axis=1).astype(bf16)
        rims_ref[c, edge:, :] = jnp.concatenate(above + [jnp.zeros_like(lone)], axis=1).astype(bf16)


def rimmed(rows, early, lone, late):
    gap = jnp.zeros((rows.shape[0] - 3 * edge, rows.shape[1]), f32)
    return rows + jnp.concatenate([early, gap, bottom(lone), late], axis=0)


def send_kernel(shard_ref, own_ref, rims_ref, send_ref):
    chunks, own, width = own_ref.shape
    heads = 2 * send_ref.shape[0] // chunks
    groups = (width // head - 2 * heads) // 2
    even = is_even(shard_ref)

    def chunk(c, carry):
        got = rims_ref[c].astype(f32)
        below, above, lone = got[:edge, :width], got[edge:, :width], unfolded(got[:edge, width:], width // (2 * head))
        early, late = jnp.where(even, 0.0, above), jnp.where(even, below, 0.0)
        far, far_lone = jnp.where(even, above, below), jnp.where(even, 0.0, lone)
        lone = jnp.where(even, lone, 0.0)

        def put(chip, part, tile):
            cols = slice(tile * head, (tile + 1) * head)
            rows = rimmed(own_ref[c, :, cols], early[:, cols], lone[:, cols], late[:, cols])
            send_ref[chip, part * own : (part + 1) * own, :] = rows.astype(bf16)
            at = 6 * own + part * edge
            send_ref[chip, at : at + edge, :] = far[:, cols].astype(bf16)
            return far_lone[:, cols]

        for n in range(heads // 2):
            chip = c * heads // 2 + n
            group = n * groups // (heads // 2)
            tiles = [2 * n, 2 * n + 1, heads + 2 * n, heads + 2 * n + 1, 2 * heads + group, 2 * heads + groups + group]
            ends = [put(chip, part, tile) for part, tile in enumerate(tiles)]
            ends = jnp.concatenate(ends + [jnp.zeros((extra - 6, head), f32)], axis=0)
            send_ref[chip, 6 * (own + edge) :, :] = ends.astype(bf16)
        return carry

    lax.fori_loop(0, chunks, chunk, 0)


def summed_part(mine_ref, even, c, part, own):
    chips = mine_ref.shape[0]
    at = 6 * own + part * edge
    none = jnp.zeros((edge, head), f32)
    early = late = none
    lone = none[:1]
    if c > 0:
        early = jnp.where(even, mine_ref[c - 1, at : at + edge, :].astype(f32), 0.0)
    if c < chips - 1:
        late = jnp.where(even, 0.0, mine_ref[c + 1, at : at + edge, :].astype(f32))
        lone = mine_ref[c + 1, 6 * (own + edge) :, :].astype(f32)[part : part + 1]
        lone = jnp.where(even, 0.0, lone)
    return rimmed(mine_ref[c, part * own : (part + 1) * own, :].astype(f32), early, lone, late)


def inverse_rms(rows):
    return lax.rsqrt(jnp.mean(rows * rows, axis=-1, keepdims=True) + eps_norm)


def lengths_kernel(shard_ref, starts_ref, inv_ref, *, document):
    chips, own, _ = inv_ref.shape
    lanes = starts_ref.shape[1] // chips
    starts = starts_ref[...].astype(f32)
    ends = jnp.concatenate([starts[:, 1:], jnp.full((1, 1), document, f32)], axis=1)
    lengths = ends - starts
    table = jnp.concatenate([lengths[:, c * lanes : (c + 1) * lanes] for c in range(chips)], axis=0)
    table = 1.0 / table.T
    table = jnp.where(is_even(shard_ref), table[:own], table[own:])
    for c in range(chips):
        inv_ref[c] = jnp.broadcast_to(table[:, c : c + 1], (own, head))


def keys_kernel(shard_ref, mine_ref, inv_ref, kgain_ref, keyval_ref, mean_ref):
    chips, own, _ = inv_ref.shape
    even = is_even(shard_ref)
    for c in range(chips):
        inv_len = inv_ref[c]
        rows = summed_part(mine_ref, even, c, 4, own) * inv_len
        mean_ref[c] = rows
        keyval_ref[c, :own, :] = (rows * inverse_rms(rows) * kgain_ref[...]).astype(bf16)
        keyval_ref[c, own:, :] = (summed_part(mine_ref, even, c, 5, own) * inv_len).astype(bf16)


def queries_kernel(shard_ref, mine_ref, inv_ref, qgain_ref, query_ref, grad_ref, unit_ref, scale_ref):
    chips, own, _ = inv_ref.shape
    even = is_even(shard_ref)
    for c in range(chips):
        for n in range(2):
            at = slice(n * own, (n + 1) * own)
            rows = summed_part(mine_ref, even, c, n, own) * inv_ref[c]
            inverse = inverse_rms(rows)
            unit = rows * inverse
            unit_ref[c, at, :] = unit
            scale_ref[c, at, :] = inverse * inv_ref[c]
            query_ref[c, at, :] = (unit * qgain_ref[...]).astype(bf16)
            grad_ref[c, at, :] = summed_part(mine_ref, even, c, 2 + n, own).astype(bf16)


def attend_kernel(
    shard_ref,
    query_ref,
    grad_ref,
    mine_ref,
    other_ref,
    qgain_ref,
    kgain_ref,
    dq_ref,
    keep_ref,
    give_ref,
    gain_ref,
    key_ref,
    value_ref,
    keyt_ref,
    raised0_ref,
    raised1_ref,
    dw0_ref,
    dw1_ref,
    dk_ref,
    dv_ref,
    dqt_ref,
):
    chips, own = mine_ref.shape[0], mine_ref.shape[1] // 2
    patches = key_ref.shape[0]
    per = query_blk // key_blk
    count = patches // query_blk
    lanes = 2 * own
    scaling = head ** (-0.5)
    raising = scaling * math.log2(math.e)
    raised_refs, dw_refs = (raised0_ref, raised1_ref), (dw0_ref, dw1_ref)
    side = lax.rem(shard_ref[0], 2)

    def places(c):
        mine = pl.multiple_of(c * lanes + side * own, own)
        theirs = pl.multiple_of(c * lanes + (1 - side) * own, own)
        return pl.ds(mine, own), pl.ds(theirs, own)

    for c in range(chips):
        mine, theirs = places(c)
        key_ref[mine, :] = mine_ref[c, :own, :]
        value_ref[mine, :] = mine_ref[c, own:, :]
        key_ref[theirs, :] = other_ref[c, :own, :]
        value_ref[theirs, :] = other_ref[c, own:, :]

    for n in range(patches // key_blk):
        keyt_ref[n] = key_ref[pl.ds(n * key_blk, key_blk), :].astype(f32).T.astype(bf16)
    dk_ref[...] = jnp.zeros_like(dk_ref)
    dv_ref[...] = jnp.zeros_like(dv_ref)

    def fold(block):
        return jnp.sum(block.reshape(block.shape[0] // 8, 8, block.shape[1]), axis=0)

    def rows(i, lane, part):
        first_chip, last_chip = (i * query_blk + lane) // lanes, (i + 1) * query_blk // lanes
        block = (query_ref, grad_ref)[part][first_chip:last_chip]
        return block.reshape(query_blk - lane, head)

    def first(i, at, lane, sums, diagonal):
        keys = pl.ds(at, key_blk)
        scores = lax.dot_general(key_ref[keys, :], rows(i, lane, 0), nt, preferred_element_type=f32)
        raised = jnp.exp2(scores * raising)
        if diagonal:
            key_at = lax.broadcasted_iota(jnp.int32, raised.shape, 0)
            query_at = lax.broadcasted_iota(jnp.int32, raised.shape, 1)
            query_at = query_at - lax.bitwise_and(query_at, own) + side * own
            raised = jnp.where(key_at <= query_at, raised, 0.0)
        dweights = lax.dot_general(value_ref[keys, :], rows(i, lane, 1), nt, preferred_element_type=f32)
        raised_refs[i % 2][keys, lane:] = raised
        dw_refs[i % 2][keys, lane:] = dweights
        added = fold(raised), fold(raised * dweights)
        if lane:
            none = jnp.zeros((8, lane), f32)
            added = tuple(jnp.concatenate([none, x], axis=1) for x in added)
        return (sums[0] + added[0], sums[1] + added[1])

    def second(i, at, lane, stats):
        keys = pl.ds(at, key_blk)
        inv_sum, delta = stats[0][:, lane:], stats[1][:, lane:]
        weights = raised_refs[i % 2][keys, lane:] * inv_sum
        dscores = (weights * (dw_refs[i % 2][keys, lane:] - delta)).astype(bf16)
        dv_ref[keys, :] += jnp.dot(weights.astype(bf16), rows(i, lane, 1), preferred_element_type=f32)
        dk_ref[keys, :] += jnp.dot(dscores, rows(i, lane, 0), preferred_element_type=f32)
        n = at // key_blk if isinstance(at, int) else lax.div(at, key_blk)
        dqt_ref[:, lane:] += jnp.dot(keyt_ref[n], dscores, preferred_element_type=f32)

    zero = jnp.zeros((8, query_blk), f32)
    total = jnp.zeros((1, head), f32)
    stats = None
    for i in range(count + 1):
        sums = (zero, zero)
        if i > 0:
            dqt_ref[...] = jnp.zeros_like(dqt_ref)

            def both(j, sums, i=i, stats=stats):
                second(i - 1, j * key_blk, 0, stats)
                return first(i, j * key_blk, 0, sums, False) if i < count else sums

            if i > 1:
                sums = lax.fori_loop(0, (i - 1) * per, both, sums, unroll=2)
            for n in range(per):
                at = (i - 1) * query_blk + n * key_blk
                second(i - 1, at, n * key_blk, stats)
                if i < count:
                    sums = first(i, at, 0, sums, False)
        if i < count:
            for n in range(per):
                sums = first(i, i * query_blk + n * key_blk, n * key_blk, sums, True)
        if i > 0:
            dq = dqt_ref[...].T * scaling
            at = query_blk // lanes
            dq_ref[(i - 1) * at : i * at] = dq.reshape(at, lanes, head)
            total = total + jnp.sum(dq * rows(i - 1, 0, 0).astype(f32), axis=0, keepdims=True)
        if i < count:
            inv_sum = 1.0 / jnp.sum(sums[0], axis=0, keepdims=True)
            stats = (inv_sum, jnp.sum(sums[1], axis=0, keepdims=True) * inv_sum)

    key_total = jnp.zeros((1, head), f32)
    for n in range(patches // key_blk):
        at = pl.ds(n * key_blk, key_blk)
        dk = dk_ref[at, :] * scaling
        dk_ref[at, :] = dk
        key_total = key_total + jnp.sum(dk * key_ref[at, :].astype(f32), axis=0, keepdims=True)

    for c in range(chips):
        mine, theirs = places(c)
        keep_ref[c, :own, :] = dk_ref[mine, :]
        keep_ref[c, own:, :] = dv_ref[mine, :]
        give_ref[c, :own, :] = dk_ref[theirs, :].astype(bf16)
        give_ref[c, own:, :] = dv_ref[theirs, :].astype(bf16)
    gains = jnp.concatenate([total / qgain_ref[...], key_total / kgain_ref[...]], axis=0)
    parts = in_parts(gains)
    gain_ref[...] = parts
    give_ref[chips] = jnp.concatenate([parts, jnp.zeros((lanes - extra, head), f32)], axis=0).astype(bf16)


def in_parts(gains):
    high = gains.astype(bf16).astype(f32)
    middle = (gains - high).astype(bf16).astype(f32)
    low = (gains - high - middle).astype(bf16).astype(f32)
    return jnp.concatenate([high, middle, low, jnp.zeros((extra - 6, head), f32)], axis=0)


def joined(parts):
    return parts[0:2] + parts[2:4] + parts[4:6]


def norm_back(delta, gain, unit, scale):
    scaled = delta * gain
    return scale * (scaled - unit * jnp.mean(scaled * unit, axis=-1, keepdims=True))


def finish_kernel(dq_ref, unit_ref, scale_ref, qgain_ref, kmean_ref, inv_ref, rows_ref, kunit_ref, kscale_ref):
    for c in range(rows_ref.shape[0]):
        rows_ref[c] = norm_back(dq_ref[c], qgain_ref[...], unit_ref[c], scale_ref[c]).astype(bf16)
        mean = kmean_ref[c]
        inverse = inverse_rms(mean)
        kunit_ref[c] = mean * inverse
        kscale_ref[c] = inverse * inv_ref[c]


def merge_kernel(
    shard_ref, rows_ref, keep_ref, got_ref, gain_ref, kunit_ref, kscale_ref, inv_ref, kgain_ref, out_ref
):
    chips, own, _ = inv_ref.shape
    even = is_even(shard_ref)
    tail = in_parts(joined(gain_ref[...]) + joined(got_ref[chips].astype(f32)))[:6]
    for c in range(chips):
        kept = keep_ref[c] + got_ref[c].astype(f32)
        keys = norm_back(kept[:own], kgain_ref[...], kunit_ref[c], kscale_ref[c])
        out_ref[c, : 2 * own, :] = rows_ref[c]
        out_ref[c, 2 * own : 3 * own, :] = keys.astype(bf16)
        out_ref[c, 3 * own : 4 * own, :] = (kept[own:] * inv_ref[c]).astype(bf16)
    none = jnp.zeros((edge, head), f32)
    for c in range(chips):
        lones = []
        for part in range(4):
            above = below = lone = none
            if c < chips - 1:
                above = out_ref[c + 1, part * own : part * own + edge, :].astype(f32)
            if c > 0:
                end = (part + 1) * own
                below = out_ref[c - 1, end - edge : end, :].astype(f32)
                lone = out_ref[c - 1, end - 2 * edge : end - edge, :].astype(f32)
            at = 4 * own + part * edge
            out_ref[c, at : at + edge, :] = jnp.where(even, above, below).astype(bf16)
            lones.append(lone[edge - 1 :])
        last = jnp.concatenate([tail] + lones + [none[: edge - 10]], axis=0)
        out_ref[c, 4 * (own + edge) :, :] = last.astype(bf16)


def back_kernel(shard_ref, x_ref, rows_ref, rims_ref, gain_ref):
    chips = x_ref.shape[0]
    chunks, own, width = rows_ref.shape
    per = 2 * chips // chunks
    groups = (width // head - per) * chunks // 2
    repeat = chips // groups
    even = is_even(shard_ref)

    def pieces(chip, part):
        at = 4 * own + part * edge
        ends = x_ref[chip, 4 * (own + edge) :, :].astype(f32)
        return (
            x_ref[chip, part * own : (part + 1) * own, :].astype(f32),
            x_ref[chip, at : at + edge, :].astype(f32),
            ends[6 + part : 7 + part],
        )

    def keyval_pieces(n):
        part, group = n // groups, n % groups
        terms = [pieces(group * repeat + r, 2 + part) for r in range(repeat)]
        return tuple(sum(term[1:], term[0]) for term in zip(*terms))

    tiles = 2 * groups // chunks
    for c in range(chunks):
        parts = [pieces((c * per + n) // 2, n % 2) for n in range(per)]
        parts += [keyval_pieces(c * tiles + n) for n in range(tiles)]
        before, after, lone = [], [], []
        for n, (rows, far, far_lone) in enumerate(parts):
            rows_ref[c, :, n * head : (n + 1) * head] = rows.astype(bf16)
            before.append(jnp.where(even, rows[own - edge :], far))
            after.append(jnp.where(even, far, rows[:edge]))
            lone.append(jnp.where(even, rows[own - edge - 1 : own - edge], far_lone))
        lone = folded(jnp.concatenate(lone, axis=1), head)
        rims_ref[c, :edge, :] = jnp.concatenate(before + [lone], axis=1).astype(bf16)
        rims_ref[c, edge:, :] = jnp.concatenate(after + [jnp.zeros_like(lone)], axis=1).astype(bf16)

    tail = x_ref[0, 4 * (own + edge) :, :].astype(f32)
    for c in range(1, chips):
        tail = tail + x_ref[c, 4 * (own + edge) :, :].astype(f32)
    gain_ref[...] = joined(tail)


def spread_kernel(edges_ref, rims_ref, rows_ref, query_ref, keyval_ref, query_buf, keyval_buf, sems):
    bytes_dev, query_width = query_ref.shape
    chunks, own, width = rows_ref.shape
    qcols, vcols = query_width // chunks, keyval_ref.shape[1] // chunks
    start = edges_ref[0:1, :]
    end = edges_ref[1:2, :]
    place = lax.broadcasted_iota(jnp.int32, (bytes_dev, 128), 0)
    pick = jnp.where((start <= place) & (place < end), 1.0, 0.0).astype(bf16)
    pick = pick[:, : below_rows + own + above_rows]
    running = []
    for c in range(chunks):
        before, after = rims_ref[c, :edge, :].astype(f32), rims_ref[c, edge:, :]
        lone = bottom(unfolded(before[:, width:], width // head))
        early = jnp.concatenate([lone, before[:, :width]], axis=0).astype(bf16)
        rows = jnp.concatenate([early, rows_ref[c], after[:, :width]], axis=0)
        out = jnp.dot(pick, rows, preferred_element_type=f32).astype(bf16)
        query_buf[:, c * qcols : (c + 1) * qcols] = out[:, :qcols]
        keyval_buf[:, c * vcols : (c + 1) * vcols] = out[:, qcols:]
        for n, (buf, ref, cols) in enumerate(((query_buf, query_ref, qcols), (keyval_buf, keyval_ref, vcols))):
            at = c * cols
            copy = pltpu.make_async_copy(buf.at[:, at : at + cols], ref.at[:, at : at + cols], sems.at[c, n])
            copy.start()
            running.append(copy)
    for copy in running:
        copy.wait()


def shards(byte_query, byte_key_value, out_grads, patch_starts, query_gain, key_gain):
    byte_query, byte_key_value, out_grads = byte_query[0], byte_key_value[0], out_grads[0]
    bytes_dev, query_width = byte_query.shape
    keyval_width = byte_key_value.shape[1]
    devices = lax.axis_size("ctx")
    chips = devices // 2
    shard = lax.axis_index("ctx")
    patches = patch_starts.shape[1]
    own = patches // devices
    chunks = 4
    qcols, kcols = query_width // chunks, keyval_width // 2 // chunks
    chunk_cols = 2 * qcols + 2 * kcols

    which = shard.astype(jnp.int32).reshape(1)

    def shape(kind, *dims):
        return jax.ShapeDtypeStruct(dims, kind)

    smem = pl.BlockSpec(memory_space=pltpu.SMEM)
    vmem = pl.BlockSpec(memory_space=pltpu.VMEM)
    hbm = pl.BlockSpec(memory_space=pltpu.HBM)
    mates = [(i, i ^ 1) for i in range(devices)]

    wide = chunk_cols + 2 * head
    inputs = (patch_starts, byte_query, byte_key_value, out_grads)
    sums, rims, edges = pl.pallas_call(
        pool_kernel,
        in_specs=[smem] + [hbm] * 4,
        out_specs=[vmem] * 3,
        out_shape=[
            shape(f32, chunks, own, chunk_cols),
            shape(bf16, chunks, 2 * edge, wide),
            shape(jnp.int32, 2, 128),
        ],
        scratch_shapes=[
            pltpu.VMEM((bytes_dev, query_width), bf16),
            pltpu.VMEM((bytes_dev, keyval_width), bf16),
            pltpu.VMEM((bytes_dev, query_width), bf16),
            pltpu.VMEM((1, patches), jnp.int32),
            pltpu.SemaphoreType.DMA((chunks + 1, 3)),
        ],
        compiler_params=limit(20),
        name="pool",
    )(which, *(pltpu.with_memory_space_constraint(x, pltpu.HBM) for x in inputs))
    rims = lax.ppermute(rims, "ctx", mates)
    inv_len = pl.pallas_call(
        functools.partial(lengths_kernel, document=bytes_dev * devices),
        in_specs=[smem, vmem],
        out_specs=vmem,
        out_shape=shape(f32, chips, own, head),
        compiler_params=limit(16),
        name="lengths",
    )(which, patch_starts)
    rims, inv_len = lax.optimization_barrier((rims, inv_len))

    send = pl.pallas_call(
        send_kernel,
        in_specs=[smem] + [vmem] * 2,
        out_specs=vmem,
        out_shape=shape(bf16, chips, 6 * (own + edge) + extra, head),
        compiler_params=limit(20),
        name="send",
    )(which, sums, rims)

    sides = [list(range(n, devices, 2)) for n in range(2)]
    mine = lax.all_to_all(send, "ctx", 0, 0, tiled=True, axis_index_groups=sides)
    qgain, kgain = query_gain[None], key_gain[None]
    pair = (chips, 2 * own, head)
    keyval, kmean = pl.pallas_call(
        keys_kernel,
        in_specs=[smem] + [vmem] * 3,
        out_specs=[vmem] * 2,
        out_shape=[shape(bf16, *pair), shape(f32, chips, own, head)],
        compiler_params=limit(20),
        name="keys",
    )(which, mine, inv_len, kgain)
    other = lax.ppermute(keyval, "ctx", mates)
    query, grad, qunit, qscale = pl.pallas_call(
        queries_kernel,
        in_specs=[smem] + [vmem] * 3,
        out_specs=[vmem] * 4,
        out_shape=[shape(bf16, *pair), shape(bf16, *pair), shape(f32, *pair), shape(f32, *pair)],
        compiler_params=limit(20),
        name="queries",
    )(which, mine, inv_len, qgain)

    block = (patches, head)
    dq, keep, give, gains = pl.pallas_call(
        attend_kernel,
        in_specs=[smem] + [vmem] * 6,
        out_specs=[vmem] * 4,
        out_shape=[
            shape(f32, *pair),
            shape(f32, *pair),
            shape(bf16, chips + 1, 2 * own, head),
            shape(f32, extra, head),
        ],
        scratch_shapes=[pltpu.VMEM(block, bf16)] * 2
        + [pltpu.VMEM((patches // key_blk, head, key_blk), bf16)]
        + [pltpu.VMEM((patches - query_blk, query_blk), f32), pltpu.VMEM((patches, query_blk), f32)] * 2
        + [pltpu.VMEM(block, f32)] * 2
        + [pltpu.VMEM((head, query_blk), f32)],
        compiler_params=limit(36),
        name="attend",
    )(which, query, grad, keyval, other, qgain, kgain)
    got = lax.ppermute(give, "ctx", mates)

    rows, kunit, kscale = pl.pallas_call(
        finish_kernel,
        in_specs=[vmem] * 6,
        out_specs=[vmem] * 3,
        out_shape=[shape(bf16, *pair), shape(f32, chips, own, head), shape(f32, chips, own, head)],
        compiler_params=limit(20),
        name="finish",
    )(dq, qunit, qscale, qgain, kmean, inv_len)
    back = pl.pallas_call(
        merge_kernel,
        in_specs=[smem] + [vmem] * 8,
        out_specs=vmem,
        out_shape=shape(bf16, chips, 4 * (own + edge) + edge, head),
        compiler_params=limit(16),
        name="merge",
    )(which, rows, keep, got, gains, kunit, kscale, inv_len, kgain)
    home = lax.all_to_all(back, "ctx", 0, 0, tiled=True, axis_index_groups=sides)

    vcols = keyval_width // chunks
    wide = qcols + vcols + head
    rows, rims, gains = pl.pallas_call(
        back_kernel,
        in_specs=[smem, vmem],
        out_specs=[vmem] * 3,
        out_shape=[
            shape(bf16, chunks, own, qcols + vcols),
            shape(bf16, chunks, 2 * edge, wide),
            shape(f32, 2, head),
        ],
        compiler_params=limit(32),
        name="back",
    )(which, home)
    rims = lax.ppermute(rims, "ctx", mates)
    docs = lax.axis_size("dp")
    turned = [lax.ppermute(gains, "dp", [(i, (i + n) % docs) for i in range(docs)]) for n in (1, 3, 2)]
    query_out, keyval_out = pl.pallas_call(
        spread_kernel,
        in_specs=[vmem] * 3,
        out_specs=[hbm] * 2,
        out_shape=[shape(bf16, bytes_dev, query_width), shape(bf16, bytes_dev, keyval_width)],
        scratch_shapes=[
            pltpu.VMEM((bytes_dev, query_width), bf16),
            pltpu.VMEM((bytes_dev, keyval_width), bf16),
            pltpu.SemaphoreType.DMA((chunks, 2)),
        ],
        compiler_params=limit(20),
        name="spread",
    )(edges, rims, rows)
    keyval_out, *turned = lax.optimization_barrier((keyval_out, *turned))
    gains = (gains + turned[2]) + (turned[0] + turned[1])
    return (query_out[None], keyval_out[None], gains[0], gains[1])


def solution(mesh):
    placed = (
        P("dp", "ctx", None),
        P("dp", "ctx", None),
        P("dp", "ctx", None),
        P("dp", None),
        P(),
        P(),
    )
    return jax.shard_map(
        shards,
        mesh=mesh,
        in_specs=placed,
        out_specs=(P("dp", "ctx", None), P("dp", "ctx", None), P(), P()),
        check_vma=False,
    )
```

```python
import functools
import math

import jax
import jax.numpy as jnp
from jax import lax
from jax.experimental import pallas as pl
from jax.experimental.pallas import tpu as pltpu
from jax.sharding import PartitionSpec as P

eps_norm = 1e-06
head = 128
below_rows = 32
above_rows = 16
edge = 16
query_blk = 1024
key_blk = 256
extra = 8
f32 = jnp.float32
bf16 = jnp.bfloat16
nt = (((1,), (1,)), ((), ()))


def limit(mib):
    return pltpu.CompilerParams(vmem_limit_bytes=mib * 1024 * 1024)


def folded(row, width):
    pieces = [row[:, at : at + width] for at in range(0, row.shape[1], width)]
    return jnp.concatenate(pieces + [jnp.zeros((edge - len(pieces), width), f32)], axis=0)


def unfolded(block, count):
    return jnp.concatenate([block[n : n + 1] for n in range(count)], axis=1)


def bottom(row):
    at = lax.broadcasted_iota(jnp.int32, (edge, row.shape[1]), 0)
    return jnp.where(at == edge - 1, row, 0.0)


def is_even(shard_ref):
    return lax.rem(shard_ref[0], 2) == 0


def pool_kernel(
    shard_ref,
    starts_ref,
    query_ref,
    keyval_ref,
    grad_ref,
    own_ref,
    rims_ref,
    edges_ref,
    query_buf,
    keyval_buf,
    grad_buf,
    starts_buf,
    sems,
):
    bytes_dev, query_width = query_ref.shape
    half = keyval_ref.shape[1] // 2
    patches = starts_ref.shape[1]
    chunks, own, _ = own_ref.shape
    qcols, kcols = query_width // chunks, half // chunks
    shard = shard_ref[0]
    used = below_rows + own + above_rows

    def parts(c):
        return (
            (query_buf, c * qcols, qcols),
            (grad_buf, c * qcols, qcols),
            (keyval_buf, c * kcols, kcols),
            (keyval_buf, half + c * kcols, kcols),
        )

    def copies(c):
        cols = slice(c * qcols, (c + 1) * qcols)
        pairs = [(query_ref.at[:, cols], query_buf.at[:, cols]), (grad_ref.at[:, cols], grad_buf.at[:, cols])]
        if c == 0:
            pairs = [(keyval_ref, keyval_buf)] + pairs
        return [pltpu.make_async_copy(ref, buf, sems.at[c, n]) for n, (ref, buf) in enumerate(pairs)]

    starts_copy = pltpu.make_async_copy(starts_ref, starts_buf, sems.at[chunks, 0])
    starts_copy.start()
    for c in range(chunks):
        for copy in copies(c):
            copy.start()

    first_patch = shard * own - below_rows
    starts_copy.wait()
    around = jnp.broadcast_to(starts_buf[...], (8, patches))
    around = pltpu.roll(around, lax.rem(patches - first_patch, patches), 1)
    lane = lax.broadcasted_iota(jnp.int32, (1, 128), 1) + first_patch

    def limited(values, at):
        values = jnp.where(at < 0, 0, jnp.where(at >= patches, bytes_dev * (patches // own), values))
        return values - shard * bytes_dev

    start = limited(around[0:1, 0:128], lane)
    end = limited(around[0:1, 1:129], lane + 1)
    edges_ref[0:1, :] = start
    edges_ref[1:2, :] = end
    place = lax.broadcasted_iota(jnp.int32, (bytes_dev, 128), 0)
    inside = jnp.where((start <= place) & (place < end), 1.0, 0.0)
    pick = inside.T.astype(bf16)[:used, :]
    for c in range(chunks):
        for copy in copies(c):
            copy.wait()
        out = 0
        below, above, lone = [], [], []
        for buf, at, width in parts(c):
            sums = jnp.dot(pick, buf[:, at : at + width], preferred_element_type=f32)
            own_ref[c, :, out : out + width] = sums[below_rows : below_rows + own]
            lone.append(sums[edge - 1 : edge])
            below.append(sums[edge:below_rows])
            above.append(sums[below_rows + own :])
            out += width
        lone = folded(jnp.concatenate(lone, axis=1), 2 * head)
        rims_ref[c, :edge, :] = jnp.concatenate(below + [lone], axis=1).astype(bf16)
        rims_ref[c, edge:, :] = jnp.concatenate(above + [jnp.zeros_like(lone)], axis=1).astype(bf16)


def rimmed(rows, early, lone, late):
    gap = jnp.zeros((rows.shape[0] - 3 * edge, rows.shape[1]), f32)
    return rows + jnp.concatenate([early, gap, bottom(lone), late], axis=0)


def send_kernel(shard_ref, own_ref, rims_ref, send_ref):
    chunks, own, width = own_ref.shape
    heads = 2 * send_ref.shape[0] // chunks
    groups = (width // head - 2 * heads) // 2
    even = is_even(shard_ref)

    def chunk(c, carry):
        got = rims_ref[c].astype(f32)
        below, above, lone = got[:edge, :width], got[edge:, :width], unfolded(got[:edge, width:], width // (2 * head))
        early, late = jnp.where(even, 0.0, above), jnp.where(even, below, 0.0)
        far, far_lone = jnp.where(even, above, below), jnp.where(even, 0.0, lone)
        lone = jnp.where(even, lone, 0.0)

        def put(chip, part, tile):
            cols = slice(tile * head, (tile + 1) * head)
            rows = rimmed(own_ref[c, :, cols], early[:, cols], lone[:, cols], late[:, cols])
            send_ref[chip, part * own : (part + 1) * own, :] = rows.astype(bf16)
            at = 6 * own + part * edge
            send_ref[chip, at : at + edge, :] = far[:, cols].astype(bf16)
            return far_lone[:, cols]

        for n in range(heads // 2):
            chip = c * heads // 2 + n
            group = n * groups // (heads // 2)
            tiles = [2 * n, 2 * n + 1, heads + 2 * n, heads + 2 * n + 1, 2 * heads + group, 2 * heads + groups + group]
            ends = [put(chip, part, tile) for part, tile in enumerate(tiles)]
            ends = jnp.concatenate(ends + [jnp.zeros((extra - 6, head), f32)], axis=0)
            send_ref[chip, 6 * (own + edge) :, :] = ends.astype(bf16)
        return carry

    lax.fori_loop(0, chunks, chunk, 0)


def summed_part(mine_ref, even, c, part, own):
    chips = mine_ref.shape[0]
    at = 6 * own + part * edge
    none = jnp.zeros((edge, head), f32)
    early = late = none
    lone = none[:1]
    if c > 0:
        early = jnp.where(even, mine_ref[c - 1, at : at + edge, :].astype(f32), 0.0)
    if c < chips - 1:
        late = jnp.where(even, 0.0, mine_ref[c + 1, at : at + edge, :].astype(f32))
        lone = mine_ref[c + 1, 6 * (own + edge) :, :].astype(f32)[part : part + 1]
        lone = jnp.where(even, 0.0, lone)
    return rimmed(mine_ref[c, part * own : (part + 1) * own, :].astype(f32), early, lone, late)


def inverse_rms(rows):
    return lax.rsqrt(jnp.mean(rows * rows, axis=-1, keepdims=True) + eps_norm)


def lengths_kernel(shard_ref, starts_ref, inv_ref, *, document):
    chips, own, _ = inv_ref.shape
    lanes = starts_ref.shape[1] // chips
    starts = starts_ref[...].astype(f32)
    ends = jnp.concatenate([starts[:, 1:], jnp.full((1, 1), document, f32)], axis=1)
    lengths = ends - starts
    table = jnp.concatenate([lengths[:, c * lanes : (c + 1) * lanes] for c in range(chips)], axis=0)
    table = 1.0 / table.T
    table = jnp.where(is_even(shard_ref), table[:own], table[own:])
    for c in range(chips):
        inv_ref[c] = jnp.broadcast_to(table[:, c : c + 1], (own, head))


def keys_kernel(shard_ref, mine_ref, inv_ref, kgain_ref, keyval_ref, mean_ref):
    chips, own, _ = inv_ref.shape
    even = is_even(shard_ref)
    for c in range(chips):
        inv_len = inv_ref[c]
        rows = summed_part(mine_ref, even, c, 4, own) * inv_len
        mean_ref[c] = rows
        keyval_ref[c, :own, :] = (rows * inverse_rms(rows) * kgain_ref[...]).astype(bf16)
        keyval_ref[c, own:, :] = (summed_part(mine_ref, even, c, 5, own) * inv_len).astype(bf16)


def queries_kernel(shard_ref, mine_ref, inv_ref, qgain_ref, query_ref, grad_ref, unit_ref, scale_ref):
    chips, own, _ = inv_ref.shape
    even = is_even(shard_ref)
    for c in range(chips):
        for n in range(2):
            at = slice(n * own, (n + 1) * own)
            rows = summed_part(mine_ref, even, c, n, own) * inv_ref[c]
            inverse = inverse_rms(rows)
            unit = rows * inverse
            unit_ref[c, at, :] = unit
            scale_ref[c, at, :] = inverse * inv_ref[c]
            query_ref[c, at, :] = (unit * qgain_ref[...]).astype(bf16)
            grad_ref[c, at, :] = summed_part(mine_ref, even, c, 2 + n, own).astype(bf16)


def attend_kernel(
    shard_ref,
    query_ref,
    grad_ref,
    mine_ref,
    other_ref,
    qgain_ref,
    kgain_ref,
    dq_ref,
    keep_ref,
    give_ref,
    gain_ref,
    key_ref,
    value_ref,
    keyt_ref,
    raised0_ref,
    raised1_ref,
    dw0_ref,
    dw1_ref,
    dk_ref,
    dv_ref,
    dqt_ref,
):
    chips, own = mine_ref.shape[0], mine_ref.shape[1] // 2
    patches = key_ref.shape[0]
    per = query_blk // key_blk
    count = patches // query_blk
    lanes = 2 * own
    scaling = head ** (-0.5)
    raising = scaling * math.log2(math.e)
    raised_refs, dw_refs = (raised0_ref, raised1_ref), (dw0_ref, dw1_ref)
    side = lax.rem(shard_ref[0], 2)

    def places(c):
        mine = pl.multiple_of(c * lanes + side * own, own)
        theirs = pl.multiple_of(c * lanes + (1 - side) * own, own)
        return pl.ds(mine, own), pl.ds(theirs, own)

    for c in range(chips):
        mine, theirs = places(c)
        key_ref[mine, :] = mine_ref[c, :own, :]
        value_ref[mine, :] = mine_ref[c, own:, :]
        key_ref[theirs, :] = other_ref[c, :own, :]
        value_ref[theirs, :] = other_ref[c, own:, :]

    for n in range(patches // key_blk):
        keyt_ref[n] = key_ref[pl.ds(n * key_blk, key_blk), :].astype(f32).T.astype(bf16)
    dk_ref[...] = jnp.zeros_like(dk_ref)
    dv_ref[...] = jnp.zeros_like(dv_ref)

    def fold(block):
        return jnp.sum(block.reshape(block.shape[0] // 8, 8, block.shape[1]), axis=0)

    def rows(i, lane, part):
        first_chip, last_chip = (i * query_blk + lane) // lanes, (i + 1) * query_blk // lanes
        block = (query_ref, grad_ref)[part][first_chip:last_chip]
        return block.reshape(query_blk - lane, head)

    def first(i, at, lane, sums, diagonal):
        keys = pl.ds(at, key_blk)
        scores = lax.dot_general(key_ref[keys, :], rows(i, lane, 0), nt, preferred_element_type=f32)
        raised = jnp.exp2(scores * raising)
        if diagonal:
            key_at = lax.broadcasted_iota(jnp.int32, raised.shape, 0)
            query_at = lax.broadcasted_iota(jnp.int32, raised.shape, 1)
            query_at = query_at - lax.bitwise_and(query_at, own) + side * own
            raised = jnp.where(key_at <= query_at, raised, 0.0)
        dweights = lax.dot_general(value_ref[keys, :], rows(i, lane, 1), nt, preferred_element_type=f32)
        raised_refs[i % 2][keys, lane:] = raised
        dw_refs[i % 2][keys, lane:] = dweights
        added = fold(raised), fold(raised * dweights)
        if lane:
            none = jnp.zeros((8, lane), f32)
            added = tuple(jnp.concatenate([none, x], axis=1) for x in added)
        return (sums[0] + added[0], sums[1] + added[1])

    def second(i, at, lane, stats):
        keys = pl.ds(at, key_blk)
        inv_sum, delta = stats[0][:, lane:], stats[1][:, lane:]
        weights = raised_refs[i % 2][keys, lane:] * inv_sum
        dscores = (weights * (dw_refs[i % 2][keys, lane:] - delta)).astype(bf16)
        dv_ref[keys, :] += jnp.dot(weights.astype(bf16), rows(i, lane, 1), preferred_element_type=f32)
        dk_ref[keys, :] += jnp.dot(dscores, rows(i, lane, 0), preferred_element_type=f32)
        n = at // key_blk if isinstance(at, int) else lax.div(at, key_blk)
        dqt_ref[:, lane:] += jnp.dot(keyt_ref[n], dscores, preferred_element_type=f32)

    zero = jnp.zeros((8, query_blk), f32)
    total = jnp.zeros((1, head), f32)
    stats = None
    for i in range(count + 1):
        sums = (zero, zero)
        if i > 0:
            dqt_ref[...] = jnp.zeros_like(dqt_ref)

            def both(j, sums, i=i, stats=stats):
                second(i - 1, j * key_blk, 0, stats)
                return first(i, j * key_blk, 0, sums, False) if i < count else sums

            if i > 1:
                sums = lax.fori_loop(0, (i - 1) * per, both, sums, unroll=2)
            for n in range(per):
                at = (i - 1) * query_blk + n * key_blk
                second(i - 1, at, n * key_blk, stats)
                if i < count:
                    sums = first(i, at, 0, sums, False)
        if i < count:
            for n in range(per):
                sums = first(i, i * query_blk + n * key_blk, n * key_blk, sums, True)
        if i > 0:
            dq = dqt_ref[...].T * scaling
            at = query_blk // lanes
            dq_ref[(i - 1) * at : i * at] = dq.reshape(at, lanes, head)
            total = total + jnp.sum(dq * rows(i - 1, 0, 0).astype(f32), axis=0, keepdims=True)
        if i < count:
            inv_sum = 1.0 / jnp.sum(sums[0], axis=0, keepdims=True)
            stats = (inv_sum, jnp.sum(sums[1], axis=0, keepdims=True) * inv_sum)

    key_total = jnp.zeros((1, head), f32)
    for n in range(patches // key_blk):
        at = pl.ds(n * key_blk, key_blk)
        dk = dk_ref[at, :] * scaling
        dk_ref[at, :] = dk
        key_total = key_total + jnp.sum(dk * key_ref[at, :].astype(f32), axis=0, keepdims=True)

    for c in range(chips):
        mine, theirs = places(c)
        keep_ref[c, :own, :] = dk_ref[mine, :]
        keep_ref[c, own:, :] = dv_ref[mine, :]
        give_ref[c, :own, :] = dk_ref[theirs, :].astype(bf16)
        give_ref[c, own:, :] = dv_ref[theirs, :].astype(bf16)
    gains = jnp.concatenate([total / qgain_ref[...], key_total / kgain_ref[...]], axis=0)
    parts = in_parts(gains)
    gain_ref[...] = parts
    give_ref[chips] = jnp.concatenate([parts, jnp.zeros((lanes - extra, head), f32)], axis=0).astype(bf16)


def in_parts(gains):
    high = gains.astype(bf16).astype(f32)
    middle = (gains - high).astype(bf16).astype(f32)
    low = (gains - high - middle).astype(bf16).astype(f32)
    return jnp.concatenate([high, middle, low, jnp.zeros((extra - 6, head), f32)], axis=0)


def joined(parts):
    return parts[0:2] + parts[2:4] + parts[4:6]


def norm_back(delta, gain, unit, scale):
    scaled = delta * gain
    return scale * (scaled - unit * jnp.mean(scaled * unit, axis=-1, keepdims=True))


def finish_kernel(dq_ref, unit_ref, scale_ref, qgain_ref, kmean_ref, inv_ref, rows_ref, kunit_ref, kscale_ref):
    for c in range(rows_ref.shape[0]):
        rows_ref[c] = norm_back(dq_ref[c], qgain_ref[...], unit_ref[c], scale_ref[c]).astype(bf16)
        mean = kmean_ref[c]
        inverse = inverse_rms(mean)
        kunit_ref[c] = mean * inverse
        kscale_ref[c] = inverse * inv_ref[c]


def merge_kernel(
    shard_ref, rows_ref, keep_ref, got_ref, gain_ref, near_ref, cross_ref, kunit_ref, kscale_ref, inv_ref, kgain_ref, out_ref
):
    chips, own, _ = inv_ref.shape
    even = is_even(shard_ref)
    here = joined(gain_ref[...]) + joined(got_ref[chips].astype(f32))
    tail = in_parts(here + (joined(near_ref[...]) + joined(cross_ref[...])))[:6]
    for c in range(chips):
        kept = keep_ref[c] + got_ref[c].astype(f32)
        keys = norm_back(kept[:own], kgain_ref[...], kunit_ref[c], kscale_ref[c])
        out_ref[c, : 2 * own, :] = rows_ref[c]
        out_ref[c, 2 * own : 3 * own, :] = keys.astype(bf16)
        out_ref[c, 3 * own : 4 * own, :] = (kept[own:] * inv_ref[c]).astype(bf16)
    none = jnp.zeros((edge, head), f32)
    for c in range(chips):
        lones = []
        for part in range(4):
            above = below = lone = none
            if c < chips - 1:
                above = out_ref[c + 1, part * own : part * own + edge, :].astype(f32)
            if c > 0:
                end = (part + 1) * own
                below = out_ref[c - 1, end - edge : end, :].astype(f32)
                lone = out_ref[c - 1, end - 2 * edge : end - edge, :].astype(f32)
            at = 4 * own + part * edge
            out_ref[c, at : at + edge, :] = jnp.where(even, above, below).astype(bf16)
            lones.append(lone[edge - 1 :])
        last = jnp.concatenate([tail] + lones + [none[: edge - 10]], axis=0)
        out_ref[c, 4 * (own + edge) :, :] = last.astype(bf16)


def back_kernel(shard_ref, x_ref, rows_ref, rims_ref, gain_ref):
    chips = x_ref.shape[0]
    chunks, own, width = rows_ref.shape
    per = 2 * chips // chunks
    groups = (width // head - per) * chunks // 2
    repeat = chips // groups
    even = is_even(shard_ref)

    def pieces(chip, part):
        at = 4 * own + part * edge
        ends = x_ref[chip, 4 * (own + edge) :, :].astype(f32)
        return (
            x_ref[chip, part * own : (part + 1) * own, :].astype(f32),
            x_ref[chip, at : at + edge, :].astype(f32),
            ends[6 + part : 7 + part],
        )

    def keyval_pieces(n):
        part, group = n // groups, n % groups
        terms = [pieces(group * repeat + r, 2 + part) for r in range(repeat)]
        return tuple(sum(term[1:], term[0]) for term in zip(*terms))

    tiles = 2 * groups // chunks
    for c in range(chunks):
        parts = [pieces((c * per + n) // 2, n % 2) for n in range(per)]
        parts += [keyval_pieces(c * tiles + n) for n in range(tiles)]
        before, after, lone = [], [], []
        for n, (rows, far, far_lone) in enumerate(parts):
            rows_ref[c, :, n * head : (n + 1) * head] = rows.astype(bf16)
            before.append(jnp.where(even, rows[own - edge :], far))
            after.append(jnp.where(even, far, rows[:edge]))
            lone.append(jnp.where(even, rows[own - edge - 1 : own - edge], far_lone))
        lone = folded(jnp.concatenate(lone, axis=1), head)
        rims_ref[c, :edge, :] = jnp.concatenate(before + [lone], axis=1).astype(bf16)
        rims_ref[c, edge:, :] = jnp.concatenate(after + [jnp.zeros_like(lone)], axis=1).astype(bf16)

    tail = x_ref[0, 4 * (own + edge) :, :].astype(f32)
    for c in range(1, chips):
        tail = tail + x_ref[c, 4 * (own + edge) :, :].astype(f32)
    gain_ref[...] = joined(tail)


def spread_kernel(edges_ref, rims_ref, rows_ref, query_ref, keyval_ref, query_buf, keyval_buf, sems):
    bytes_dev, query_width = query_ref.shape
    chunks, own, width = rows_ref.shape
    qcols, vcols = query_width // chunks, keyval_ref.shape[1] // chunks
    start = edges_ref[0:1, :]
    end = edges_ref[1:2, :]
    place = lax.broadcasted_iota(jnp.int32, (bytes_dev, 128), 0)
    pick = jnp.where((start <= place) & (place < end), 1.0, 0.0).astype(bf16)
    pick = pick[:, : below_rows + own + above_rows]
    running = []
    for c in range(chunks):
        before, after = rims_ref[c, :edge, :].astype(f32), rims_ref[c, edge:, :]
        lone = bottom(unfolded(before[:, width:], width // head))
        early = jnp.concatenate([lone, before[:, :width]], axis=0).astype(bf16)
        rows = jnp.concatenate([early, rows_ref[c], after[:, :width]], axis=0)
        out = jnp.dot(pick, rows, preferred_element_type=f32).astype(bf16)
        query_buf[:, c * qcols : (c + 1) * qcols] = out[:, :qcols]
        keyval_buf[:, c * vcols : (c + 1) * vcols] = out[:, qcols:]
        for n, (buf, ref, cols) in enumerate(((query_buf, query_ref, qcols), (keyval_buf, keyval_ref, vcols))):
            at = c * cols
            copy = pltpu.make_async_copy(buf.at[:, at : at + cols], ref.at[:, at : at + cols], sems.at[c, n])
            copy.start()
            running.append(copy)
    for copy in running:
        copy.wait()


def shards(byte_query, byte_key_value, out_grads, patch_starts, query_gain, key_gain):
    byte_query, byte_key_value, out_grads = byte_query[0], byte_key_value[0], out_grads[0]
    bytes_dev, query_width = byte_query.shape
    keyval_width = byte_key_value.shape[1]
    devices = lax.axis_size("ctx")
    chips = devices // 2
    shard = lax.axis_index("ctx")
    patches = patch_starts.shape[1]
    own = patches // devices
    chunks = 4
    qcols, kcols = query_width // chunks, keyval_width // 2 // chunks
    chunk_cols = 2 * qcols + 2 * kcols

    which = shard.astype(jnp.int32).reshape(1)

    def shape(kind, *dims):
        return jax.ShapeDtypeStruct(dims, kind)

    smem = pl.BlockSpec(memory_space=pltpu.SMEM)
    vmem = pl.BlockSpec(memory_space=pltpu.VMEM)
    hbm = pl.BlockSpec(memory_space=pltpu.HBM)
    mates = [(i, i ^ 1) for i in range(devices)]

    wide = chunk_cols + 2 * head
    inputs = (patch_starts, byte_query, byte_key_value, out_grads)
    sums, rims, edges = pl.pallas_call(
        pool_kernel,
        in_specs=[smem] + [hbm] * 4,
        out_specs=[vmem] * 3,
        out_shape=[
            shape(f32, chunks, own, chunk_cols),
            shape(bf16, chunks, 2 * edge, wide),
            shape(jnp.int32, 2, 128),
        ],
        scratch_shapes=[
            pltpu.VMEM((bytes_dev, query_width), bf16),
            pltpu.VMEM((bytes_dev, keyval_width), bf16),
            pltpu.VMEM((bytes_dev, query_width), bf16),
            pltpu.VMEM((1, patches), jnp.int32),
            pltpu.SemaphoreType.DMA((chunks + 1, 3)),
        ],
        compiler_params=limit(20),
        name="pool",
    )(which, *(pltpu.with_memory_space_constraint(x, pltpu.HBM) for x in inputs))
    rims = lax.ppermute(rims, "ctx", mates)
    inv_len = pl.pallas_call(
        functools.partial(lengths_kernel, document=bytes_dev * devices),
        in_specs=[smem, vmem],
        out_specs=vmem,
        out_shape=shape(f32, chips, own, head),
        compiler_params=limit(16),
        name="lengths",
    )(which, patch_starts)
    rims, inv_len = lax.optimization_barrier((rims, inv_len))

    send = pl.pallas_call(
        send_kernel,
        in_specs=[smem] + [vmem] * 2,
        out_specs=vmem,
        out_shape=shape(bf16, chips, 6 * (own + edge) + extra, head),
        compiler_params=limit(20),
        name="send",
    )(which, sums, rims)

    sides = [list(range(n, devices, 2)) for n in range(2)]
    mine = lax.all_to_all(send, "ctx", 0, 0, tiled=True, axis_index_groups=sides)
    qgain, kgain = query_gain[None], key_gain[None]
    pair = (chips, 2 * own, head)
    keyval, kmean = pl.pallas_call(
        keys_kernel,
        in_specs=[smem] + [vmem] * 3,
        out_specs=[vmem] * 2,
        out_shape=[shape(bf16, *pair), shape(f32, chips, own, head)],
        compiler_params=limit(20),
        name="keys",
    )(which, mine, inv_len, kgain)
    other = lax.ppermute(keyval, "ctx", mates)
    query, grad, qunit, qscale = pl.pallas_call(
        queries_kernel,
        in_specs=[smem] + [vmem] * 3,
        out_specs=[vmem] * 4,
        out_shape=[shape(bf16, *pair), shape(bf16, *pair), shape(f32, *pair), shape(f32, *pair)],
        compiler_params=limit(20),
        name="queries",
    )(which, mine, inv_len, qgain)

    block = (patches, head)
    dq, keep, give, gains = pl.pallas_call(
        attend_kernel,
        in_specs=[smem] + [vmem] * 6,
        out_specs=[vmem] * 4,
        out_shape=[
            shape(f32, *pair),
            shape(f32, *pair),
            shape(bf16, chips + 1, 2 * own, head),
            shape(f32, extra, head),
        ],
        scratch_shapes=[pltpu.VMEM(block, bf16)] * 2
        + [pltpu.VMEM((patches // key_blk, head, key_blk), bf16)]
        + [pltpu.VMEM((patches - query_blk, query_blk), f32), pltpu.VMEM((patches, query_blk), f32)] * 2
        + [pltpu.VMEM(block, f32)] * 2
        + [pltpu.VMEM((head, query_blk), f32)],
        compiler_params=limit(36),
        name="attend",
    )(which, query, grad, keyval, other, qgain, kgain)
    got = lax.ppermute(give, "ctx", mates)
    docs = lax.axis_size("dp")
    near = lax.ppermute(gains, "dp", [(i, i ^ 1) for i in range(docs)])
    crossed = [(d * devices + i, (d ^ 1) * devices + (i ^ 1)) for d in range(docs) for i in range(devices)]
    cross = lax.ppermute(gains, ("dp", "ctx"), crossed)

    rows, kunit, kscale = pl.pallas_call(
        finish_kernel,
        in_specs=[vmem] * 6,
        out_specs=[vmem] * 3,
        out_shape=[shape(bf16, *pair), shape(f32, chips, own, head), shape(f32, chips, own, head)],
        compiler_params=limit(20),
        name="finish",
    )(dq, qunit, qscale, qgain, kmean, inv_len)
    back = pl.pallas_call(
        merge_kernel,
        in_specs=[smem] + [vmem] * 10,
        out_specs=vmem,
        out_shape=shape(bf16, chips, 4 * (own + edge) + edge, head),
        compiler_params=limit(16),
        name="merge",
    )(which, rows, keep, got, gains, near, cross, kunit, kscale, inv_len, kgain)
    home = lax.all_to_all(back, "ctx", 0, 0, tiled=True, axis_index_groups=sides)

    vcols = keyval_width // chunks
    wide = qcols + vcols + head
    rows, rims, gains = pl.pallas_call(
        back_kernel,
        in_specs=[smem, vmem],
        out_specs=[vmem] * 3,
        out_shape=[
            shape(bf16, chunks, own, qcols + vcols),
            shape(bf16, chunks, 2 * edge, wide),
            shape(f32, 2, head),
        ],
        compiler_params=limit(32),
        name="back",
    )(which, home)
    rims = lax.ppermute(rims, "ctx", mates)
    opposite = lax.ppermute(gains, "dp", [(i, docs - 1 - i) for i in range(docs)])
    query_out, keyval_out = pl.pallas_call(
        spread_kernel,
        in_specs=[vmem] * 3,
        out_specs=[hbm] * 2,
        out_shape=[shape(bf16, bytes_dev, query_width), shape(bf16, bytes_dev, keyval_width)],
        scratch_shapes=[
            pltpu.VMEM((bytes_dev, query_width), bf16),
            pltpu.VMEM((bytes_dev, keyval_width), bf16),
            pltpu.SemaphoreType.DMA((chunks, 2)),
        ],
        compiler_params=limit(20),
        name="spread",
    )(edges, rims, rows)
    keyval_out, opposite = lax.optimization_barrier((keyval_out, opposite))
    gains = gains + opposite
    return (query_out[None], keyval_out[None], gains[0], gains[1])


def solution(mesh):
    placed = (
        P("dp", "ctx", None),
        P("dp", "ctx", None),
        P("dp", "ctx", None),
        P("dp", None),
        P(),
        P(),
    )
    return jax.shard_map(
        shards,
        mesh=mesh,
        in_specs=placed,
        out_specs=(P("dp", "ctx", None), P("dp", "ctx", None), P(), P()),
        check_vma=False,
    )
```

```python
import functools
import math

import jax
import jax.numpy as jnp
from jax import lax
from jax.experimental import pallas as pl
from jax.experimental.pallas import tpu as pltpu
from jax.sharding import PartitionSpec as P

eps_norm = 1e-06
head = 128
below_rows = 32
above_rows = 16
edge = 16
query_blk = 1024
key_blk = 256
extra = 8
f32 = jnp.float32
bf16 = jnp.bfloat16
nt = (((1,), (1,)), ((), ()))


def limit(mib):
    return pltpu.CompilerParams(vmem_limit_bytes=mib * 1024 * 1024)


def folded(row, width):
    pieces = [row[:, at : at + width] for at in range(0, row.shape[1], width)]
    return jnp.concatenate(pieces + [jnp.zeros((edge - len(pieces), width), f32)], axis=0)


def unfolded(block, count):
    return jnp.concatenate([block[n : n + 1] for n in range(count)], axis=1)


def bottom(row):
    at = lax.broadcasted_iota(jnp.int32, (edge, row.shape[1]), 0)
    return jnp.where(at == edge - 1, row, 0.0)


def is_even(shard_ref):
    return lax.rem(shard_ref[0], 2) == 0


def pool_kernel(
    shard_ref,
    starts_ref,
    query_ref,
    keyval_ref,
    grad_ref,
    own_ref,
    rims_ref,
    edges_ref,
    query_buf,
    keyval_buf,
    grad_buf,
    starts_buf,
    sems,
):
    bytes_dev, query_width = query_ref.shape
    half = keyval_ref.shape[1] // 2
    patches = starts_ref.shape[1]
    chunks, own, _ = own_ref.shape
    qcols, kcols = query_width // chunks, half // chunks
    shard = shard_ref[0]
    used = below_rows + own + above_rows

    def parts(c):
        return (
            (query_buf, c * qcols, qcols),
            (grad_buf, c * qcols, qcols),
            (keyval_buf, c * kcols, kcols),
            (keyval_buf, half + c * kcols, kcols),
        )

    def copies(c):
        cols = slice(c * qcols, (c + 1) * qcols)
        pairs = [(query_ref.at[:, cols], query_buf.at[:, cols]), (grad_ref.at[:, cols], grad_buf.at[:, cols])]
        if c == 0:
            pairs = [(keyval_ref, keyval_buf)] + pairs
        return [pltpu.make_async_copy(ref, buf, sems.at[c, n]) for n, (ref, buf) in enumerate(pairs)]

    starts_copy = pltpu.make_async_copy(starts_ref, starts_buf, sems.at[chunks, 0])
    starts_copy.start()
    for c in range(chunks):
        for copy in copies(c):
            copy.start()

    first_patch = shard * own - below_rows
    starts_copy.wait()
    around = jnp.broadcast_to(starts_buf[...], (8, patches))
    around = pltpu.roll(around, lax.rem(patches - first_patch, patches), 1)
    lane = lax.broadcasted_iota(jnp.int32, (1, 128), 1) + first_patch

    def limited(values, at):
        values = jnp.where(at < 0, 0, jnp.where(at >= patches, bytes_dev * (patches // own), values))
        return values - shard * bytes_dev

    start = limited(around[0:1, 0:128], lane)
    end = limited(around[0:1, 1:129], lane + 1)
    edges_ref[0:1, :] = start
    edges_ref[1:2, :] = end
    place = lax.broadcasted_iota(jnp.int32, (bytes_dev, 128), 0)
    inside = jnp.where((start <= place) & (place < end), 1.0, 0.0)
    pick = inside.T.astype(bf16)[:used, :]
    for c in range(chunks):
        for copy in copies(c):
            copy.wait()
        out = 0
        below, above, lone = [], [], []
        for buf, at, width in parts(c):
            sums = jnp.dot(pick, buf[:, at : at + width], preferred_element_type=f32)
            own_ref[c, :, out : out + width] = sums[below_rows : below_rows + own]
            lone.append(sums[edge - 1 : edge])
            below.append(sums[edge:below_rows])
            above.append(sums[below_rows + own :])
            out += width
        lone = folded(jnp.concatenate(lone, axis=1), 2 * head)
        rims_ref[c, :edge, :] = jnp.concatenate(below + [lone], axis=1).astype(bf16)
        rims_ref[c, edge:, :] = jnp.concatenate(above + [jnp.zeros_like(lone)], axis=1).astype(bf16)


def rimmed(rows, early, lone, late):
    gap = jnp.zeros((rows.shape[0] - 3 * edge, rows.shape[1]), f32)
    return rows + jnp.concatenate([early, gap, bottom(lone), late], axis=0)


def send_kernel(shard_ref, own_ref, rims_ref, send_ref):
    chunks, own, width = own_ref.shape
    heads = 2 * send_ref.shape[0] // chunks
    groups = (width // head - 2 * heads) // 2
    even = is_even(shard_ref)

    def chunk(c, carry):
        got = rims_ref[c].astype(f32)
        below, above, lone = got[:edge, :width], got[edge:, :width], unfolded(got[:edge, width:], width // (2 * head))
        early, late = jnp.where(even, 0.0, above), jnp.where(even, below, 0.0)
        far, far_lone = jnp.where(even, above, below), jnp.where(even, 0.0, lone)
        lone = jnp.where(even, lone, 0.0)

        def put(chip, part, tile):
            cols = slice(tile * head, (tile + 1) * head)
            rows = rimmed(own_ref[c, :, cols], early[:, cols], lone[:, cols], late[:, cols])
            send_ref[chip, part * own : (part + 1) * own, :] = rows.astype(bf16)
            at = 6 * own + part * edge
            send_ref[chip, at : at + edge, :] = far[:, cols].astype(bf16)
            return far_lone[:, cols]

        for n in range(heads // 2):
            chip = c * heads // 2 + n
            group = n * groups // (heads // 2)
            tiles = [2 * n, 2 * n + 1, heads + 2 * n, heads + 2 * n + 1, 2 * heads + group, 2 * heads + groups + group]
            ends = [put(chip, part, tile) for part, tile in enumerate(tiles)]
            ends = jnp.concatenate(ends + [jnp.zeros((extra - 6, head), f32)], axis=0)
            send_ref[chip, 6 * (own + edge) :, :] = ends.astype(bf16)
        return carry

    lax.fori_loop(0, chunks, chunk, 0)


def summed_part(mine_ref, even, c, part, own):
    chips = mine_ref.shape[0]
    at = 6 * own + part * edge
    none = jnp.zeros((edge, head), f32)
    early = late = none
    lone = none[:1]
    if c > 0:
        early = jnp.where(even, mine_ref[c - 1, at : at + edge, :].astype(f32), 0.0)
    if c < chips - 1:
        late = jnp.where(even, 0.0, mine_ref[c + 1, at : at + edge, :].astype(f32))
        lone = mine_ref[c + 1, 6 * (own + edge) :, :].astype(f32)[part : part + 1]
        lone = jnp.where(even, 0.0, lone)
    return rimmed(mine_ref[c, part * own : (part + 1) * own, :].astype(f32), early, lone, late)


def inverse_rms(rows):
    return lax.rsqrt(jnp.mean(rows * rows, axis=-1, keepdims=True) + eps_norm)


def lengths_kernel(shard_ref, starts_ref, inv_ref, *, document):
    chips, own, _ = inv_ref.shape
    lanes = starts_ref.shape[1] // chips
    starts = starts_ref[...].astype(f32)
    ends = jnp.concatenate([starts[:, 1:], jnp.full((1, 1), document, f32)], axis=1)
    lengths = ends - starts
    table = jnp.concatenate([lengths[:, c * lanes : (c + 1) * lanes] for c in range(chips)], axis=0)
    table = 1.0 / table.T
    table = jnp.where(is_even(shard_ref), table[:own], table[own:])
    for c in range(chips):
        inv_ref[c] = jnp.broadcast_to(table[:, c : c + 1], (own, head))


def keys_kernel(shard_ref, mine_ref, inv_ref, kgain_ref, keyval_ref, mean_ref):
    chips, own, _ = inv_ref.shape
    even = is_even(shard_ref)
    for c in range(chips):
        inv_len = inv_ref[c]
        rows = summed_part(mine_ref, even, c, 4, own) * inv_len
        mean_ref[c] = rows
        keyval_ref[c, :own, :] = (rows * inverse_rms(rows) * kgain_ref[...]).astype(bf16)
        keyval_ref[c, own:, :] = (summed_part(mine_ref, even, c, 5, own) * inv_len).astype(bf16)


def queries_kernel(shard_ref, mine_ref, inv_ref, qgain_ref, query_ref, grad_ref, unit_ref, scale_ref):
    chips, own, _ = inv_ref.shape
    even = is_even(shard_ref)
    for c in range(chips):
        for n in range(2):
            at = slice(n * own, (n + 1) * own)
            rows = summed_part(mine_ref, even, c, n, own) * inv_ref[c]
            inverse = inverse_rms(rows)
            unit = rows * inverse
            unit_ref[c, at, :] = unit
            scale_ref[c, at, :] = inverse * inv_ref[c]
            query_ref[c, at, :] = (unit * qgain_ref[...]).astype(bf16)
            grad_ref[c, at, :] = summed_part(mine_ref, even, c, 2 + n, own).astype(bf16)


def attend_kernel(
    shard_ref,
    query_ref,
    grad_ref,
    mine_ref,
    other_ref,
    dq_ref,
    keep_ref,
    give_ref,
    gain_ref,
    key_ref,
    value_ref,
    keyt_ref,
    raised0_ref,
    raised1_ref,
    dw0_ref,
    dw1_ref,
    dk_ref,
    dv_ref,
    dqt_ref,
):
    chips, own = mine_ref.shape[0], mine_ref.shape[1] // 2
    patches = key_ref.shape[0]
    per = query_blk // key_blk
    count = patches // query_blk
    lanes = 2 * own
    scaling = head ** (-0.5)
    raising = scaling * math.log2(math.e)
    raised_refs, dw_refs = (raised0_ref, raised1_ref), (dw0_ref, dw1_ref)
    side = lax.rem(shard_ref[0], 2)

    def places(c):
        mine = pl.multiple_of(c * lanes + side * own, own)
        theirs = pl.multiple_of(c * lanes + (1 - side) * own, own)
        return pl.ds(mine, own), pl.ds(theirs, own)

    for c in range(chips):
        mine, theirs = places(c)
        key_ref[mine, :] = mine_ref[c, :own, :]
        value_ref[mine, :] = mine_ref[c, own:, :]
        key_ref[theirs, :] = other_ref[c, :own, :]
        value_ref[theirs, :] = other_ref[c, own:, :]

    for n in range(patches // key_blk):
        keyt_ref[n] = key_ref[pl.ds(n * key_blk, key_blk), :].astype(f32).T.astype(bf16)
    dk_ref[...] = jnp.zeros_like(dk_ref)
    dv_ref[...] = jnp.zeros_like(dv_ref)

    def fold(block):
        return jnp.sum(block.reshape(block.shape[0] // 8, 8, block.shape[1]), axis=0)

    def rows(i, lane, part):
        first_chip, last_chip = (i * query_blk + lane) // lanes, (i + 1) * query_blk // lanes
        block = (query_ref, grad_ref)[part][first_chip:last_chip]
        return block.reshape(query_blk - lane, head)

    def first(i, at, lane, sums, diagonal):
        keys = pl.ds(at, key_blk)
        scores = lax.dot_general(key_ref[keys, :], rows(i, lane, 0), nt, preferred_element_type=f32)
        raised = jnp.exp2(scores * raising)
        if diagonal:
            key_at = lax.broadcasted_iota(jnp.int32, raised.shape, 0)
            query_at = lax.broadcasted_iota(jnp.int32, raised.shape, 1)
            query_at = query_at - lax.bitwise_and(query_at, own) + side * own
            raised = jnp.where(key_at <= query_at, raised, 0.0)
        dweights = lax.dot_general(value_ref[keys, :], rows(i, lane, 1), nt, preferred_element_type=f32)
        raised_refs[i % 2][keys, lane:] = raised
        dw_refs[i % 2][keys, lane:] = dweights
        added = fold(raised), fold(raised * dweights)
        if lane:
            none = jnp.zeros((8, lane), f32)
            added = tuple(jnp.concatenate([none, x], axis=1) for x in added)
        return (sums[0] + added[0], sums[1] + added[1])

    def second(i, at, lane, stats):
        keys = pl.ds(at, key_blk)
        inv_sum, delta = stats[0][:, lane:], stats[1][:, lane:]
        weights = raised_refs[i % 2][keys, lane:] * inv_sum
        dscores = (weights * (dw_refs[i % 2][keys, lane:] - delta)).astype(bf16)
        dv_ref[keys, :] += jnp.dot(weights.astype(bf16), rows(i, lane, 1), preferred_element_type=f32)
        dk_ref[keys, :] += jnp.dot(dscores, rows(i, lane, 0), preferred_element_type=f32)
        n = at // key_blk if isinstance(at, int) else lax.div(at, key_blk)
        dqt_ref[:, lane:] += jnp.dot(keyt_ref[n], dscores, preferred_element_type=f32)

    zero = jnp.zeros((8, query_blk), f32)
    total = jnp.zeros((1, head), f32)
    stats = None
    for i in range(count + 1):
        sums = (zero, zero)
        if i > 0:
            dqt_ref[...] = jnp.zeros_like(dqt_ref)

            def both(j, sums, i=i, stats=stats):
                second(i - 1, j * key_blk, 0, stats)
                return first(i, j * key_blk, 0, sums, False) if i < count else sums

            if i > 1:
                sums = lax.fori_loop(0, (i - 1) * per, both, sums, unroll=2)
            for n in range(per):
                at = (i - 1) * query_blk + n * key_blk
                second(i - 1, at, n * key_blk, stats)
                if i < count:
                    sums = first(i, at, 0, sums, False)
        if i < count:
            for n in range(per):
                sums = first(i, i * query_blk + n * key_blk, n * key_blk, sums, True)
        if i > 0:
            dq = dqt_ref[...].T * scaling
            at = query_blk // lanes
            dq_ref[(i - 1) * at : i * at] = dq.reshape(at, lanes, head)
            total = total + jnp.sum(dq * rows(i - 1, 0, 0).astype(f32), axis=0, keepdims=True)
        if i < count:
            inv_sum = 1.0 / jnp.sum(sums[0], axis=0, keepdims=True)
            stats = (inv_sum, jnp.sum(sums[1], axis=0, keepdims=True) * inv_sum)

    for n in range(patches // key_blk):
        at = pl.ds(n * key_blk, key_blk)
        dk_ref[at, :] = dk_ref[at, :] * scaling

    for c in range(chips):
        mine, theirs = places(c)
        keep_ref[c, :own, :] = dk_ref[mine, :]
        keep_ref[c, own:, :] = dv_ref[mine, :]
        give_ref[c, :own, :] = dk_ref[theirs, :].astype(bf16)
        give_ref[c, own:, :] = dv_ref[theirs, :].astype(bf16)
    parts = in_parts(total)
    gain_ref[...] = parts
    give_ref[chips] = jnp.concatenate([parts, jnp.zeros((lanes - extra, head), f32)], axis=0).astype(bf16)


def in_parts(gains):
    high = gains.astype(bf16).astype(f32)
    middle = (gains - high).astype(bf16).astype(f32)
    low = (gains - high - middle).astype(bf16).astype(f32)
    return jnp.concatenate([high, middle, low, jnp.zeros((extra - 3, head), f32)], axis=0)


def joined(parts):
    return parts[0:1] + parts[1:2] + parts[2:3]


def norm_back(delta, gain, unit, scale):
    scaled = delta * gain
    return scale * (scaled - unit * jnp.mean(scaled * unit, axis=-1, keepdims=True))


def finish_kernel(dq_ref, unit_ref, scale_ref, qgain_ref, kmean_ref, inv_ref, rows_ref, kunit_ref, kscale_ref):
    for c in range(rows_ref.shape[0]):
        rows_ref[c] = norm_back(dq_ref[c], qgain_ref[...], unit_ref[c], scale_ref[c]).astype(bf16)
        mean = kmean_ref[c]
        inverse = inverse_rms(mean)
        kunit_ref[c] = mean * inverse
        kscale_ref[c] = inverse * inv_ref[c]


def merge_kernel(
    shard_ref, rows_ref, keep_ref, got_ref, gain_ref, near_ref, cross_ref, kunit_ref, kscale_ref, inv_ref, kgain_ref, out_ref
):
    chips, own, _ = inv_ref.shape
    even = is_even(shard_ref)
    here = joined(gain_ref[...]) + joined(got_ref[chips].astype(f32))
    tail = in_parts(here + (joined(near_ref[...]) + joined(cross_ref[...])))[:3]
    for c in range(chips):
        kept = keep_ref[c] + got_ref[c].astype(f32)
        keys = norm_back(kept[:own], kgain_ref[...], kunit_ref[c], kscale_ref[c])
        out_ref[c, : 2 * own, :] = rows_ref[c]
        out_ref[c, 2 * own : 3 * own, :] = keys.astype(bf16)
        out_ref[c, 3 * own : 4 * own, :] = (kept[own:] * inv_ref[c]).astype(bf16)
    none = jnp.zeros((edge, head), f32)
    for c in range(chips):
        lones = []
        for part in range(4):
            above = below = lone = none
            if c < chips - 1:
                above = out_ref[c + 1, part * own : part * own + edge, :].astype(f32)
            if c > 0:
                end = (part + 1) * own
                below = out_ref[c - 1, end - edge : end, :].astype(f32)
                lone = out_ref[c - 1, end - 2 * edge : end - edge, :].astype(f32)
            at = 4 * own + part * edge
            out_ref[c, at : at + edge, :] = jnp.where(even, above, below).astype(bf16)
            lones.append(lone[edge - 1 :])
        last = jnp.concatenate([tail] + lones + [none[: extra - 7]], axis=0)
        out_ref[c, 4 * (own + edge) :, :] = last.astype(bf16)


def back_kernel(shard_ref, x_ref, qgain_ref, kgain_ref, rows_ref, rims_ref, gain_ref):
    chips = x_ref.shape[0]
    chunks, own, width = rows_ref.shape
    per = 2 * chips // chunks
    groups = (width // head - per) * chunks // 2
    repeat = chips // groups
    even = is_even(shard_ref)

    def pieces(chip, part):
        at = 4 * own + part * edge
        ends = x_ref[chip, 4 * (own + edge) :, :].astype(f32)
        return (
            x_ref[chip, part * own : (part + 1) * own, :].astype(f32),
            x_ref[chip, at : at + edge, :].astype(f32),
            ends[3 + part : 4 + part],
        )

    def keyval_pieces(n):
        part, group = n // groups, n % groups
        terms = [pieces(group * repeat + r, 2 + part) for r in range(repeat)]
        return tuple(sum(term[1:], term[0]) for term in zip(*terms))

    tiles = 2 * groups // chunks
    for c in range(chunks):
        parts = [pieces((c * per + n) // 2, n % 2) for n in range(per)]
        parts += [keyval_pieces(c * tiles + n) for n in range(tiles)]
        before, after, lone = [], [], []
        for n, (rows, far, far_lone) in enumerate(parts):
            rows_ref[c, :, n * head : (n + 1) * head] = rows.astype(bf16)
            before.append(jnp.where(even, rows[own - edge :], far))
            after.append(jnp.where(even, far, rows[:edge]))
            lone.append(jnp.where(even, rows[own - edge - 1 : own - edge], far_lone))
        lone = folded(jnp.concatenate(lone, axis=1), head)
        rims_ref[c, :edge, :] = jnp.concatenate(before + [lone], axis=1).astype(bf16)
        rims_ref[c, edge:, :] = jnp.concatenate(after + [jnp.zeros_like(lone)], axis=1).astype(bf16)

    tail = x_ref[0, 4 * (own + edge) :, :].astype(f32)
    for c in range(1, chips):
        tail = tail + x_ref[c, 4 * (own + edge) :, :].astype(f32)
    gain_ref[0:1, :] = joined(tail) / qgain_ref[...]
    gain_ref[1:2, :] = joined(tail) / kgain_ref[...]


def spread_kernel(edges_ref, rims_ref, rows_ref, query_ref, keyval_ref, query_buf, keyval_buf, sems):
    bytes_dev, query_width = query_ref.shape
    chunks, own, width = rows_ref.shape
    qcols, vcols = query_width // chunks, keyval_ref.shape[1] // chunks
    start = edges_ref[0:1, :]
    end = edges_ref[1:2, :]
    place = lax.broadcasted_iota(jnp.int32, (bytes_dev, 128), 0)
    pick = jnp.where((start <= place) & (place < end), 1.0, 0.0).astype(bf16)
    pick = pick[:, : below_rows + own + above_rows]
    running = []
    for c in range(chunks):
        before, after = rims_ref[c, :edge, :].astype(f32), rims_ref[c, edge:, :]
        lone = bottom(unfolded(before[:, width:], width // head))
        early = jnp.concatenate([lone, before[:, :width]], axis=0).astype(bf16)
        rows = jnp.concatenate([early, rows_ref[c], after[:, :width]], axis=0)
        out = jnp.dot(pick, rows, preferred_element_type=f32).astype(bf16)
        query_buf[:, c * qcols : (c + 1) * qcols] = out[:, :qcols]
        keyval_buf[:, c * vcols : (c + 1) * vcols] = out[:, qcols:]
        for n, (buf, ref, cols) in enumerate(((query_buf, query_ref, qcols), (keyval_buf, keyval_ref, vcols))):
            at = c * cols
            copy = pltpu.make_async_copy(buf.at[:, at : at + cols], ref.at[:, at : at + cols], sems.at[c, n])
            copy.start()
            running.append(copy)
    for copy in running:
        copy.wait()


def shards(byte_query, byte_key_value, out_grads, patch_starts, query_gain, key_gain):
    byte_query, byte_key_value, out_grads = byte_query[0], byte_key_value[0], out_grads[0]
    bytes_dev, query_width = byte_query.shape
    keyval_width = byte_key_value.shape[1]
    devices = lax.axis_size("ctx")
    chips = devices // 2
    shard = lax.axis_index("ctx")
    patches = patch_starts.shape[1]
    own = patches // devices
    chunks = 4
    qcols, kcols = query_width // chunks, keyval_width // 2 // chunks
    chunk_cols = 2 * qcols + 2 * kcols

    which = shard.astype(jnp.int32).reshape(1)

    def shape(kind, *dims):
        return jax.ShapeDtypeStruct(dims, kind)

    smem = pl.BlockSpec(memory_space=pltpu.SMEM)
    vmem = pl.BlockSpec(memory_space=pltpu.VMEM)
    hbm = pl.BlockSpec(memory_space=pltpu.HBM)
    mates = [(i, i ^ 1) for i in range(devices)]

    wide = chunk_cols + 2 * head
    inputs = (patch_starts, byte_query, byte_key_value, out_grads)
    sums, rims, edges = pl.pallas_call(
        pool_kernel,
        in_specs=[smem] + [hbm] * 4,
        out_specs=[vmem] * 3,
        out_shape=[
            shape(f32, chunks, own, chunk_cols),
            shape(bf16, chunks, 2 * edge, wide),
            shape(jnp.int32, 2, 128),
        ],
        scratch_shapes=[
            pltpu.VMEM((bytes_dev, query_width), bf16),
            pltpu.VMEM((bytes_dev, keyval_width), bf16),
            pltpu.VMEM((bytes_dev, query_width), bf16),
            pltpu.VMEM((1, patches), jnp.int32),
            pltpu.SemaphoreType.DMA((chunks + 1, 3)),
        ],
        compiler_params=limit(20),
        name="pool",
    )(which, *(pltpu.with_memory_space_constraint(x, pltpu.HBM) for x in inputs))
    rims = lax.ppermute(rims, "ctx", mates)
    inv_len = pl.pallas_call(
        functools.partial(lengths_kernel, document=bytes_dev * devices),
        in_specs=[smem, vmem],
        out_specs=vmem,
        out_shape=shape(f32, chips, own, head),
        compiler_params=limit(16),
        name="lengths",
    )(which, patch_starts)
    rims, inv_len = lax.optimization_barrier((rims, inv_len))

    send = pl.pallas_call(
        send_kernel,
        in_specs=[smem] + [vmem] * 2,
        out_specs=vmem,
        out_shape=shape(bf16, chips, 6 * (own + edge) + extra, head),
        compiler_params=limit(20),
        name="send",
    )(which, sums, rims)

    sides = [list(range(n, devices, 2)) for n in range(2)]
    mine = lax.all_to_all(send, "ctx", 0, 0, tiled=True, axis_index_groups=sides)
    qgain, kgain = query_gain[None], key_gain[None]
    pair = (chips, 2 * own, head)
    keyval, kmean = pl.pallas_call(
        keys_kernel,
        in_specs=[smem] + [vmem] * 3,
        out_specs=[vmem] * 2,
        out_shape=[shape(bf16, *pair), shape(f32, chips, own, head)],
        compiler_params=limit(20),
        name="keys",
    )(which, mine, inv_len, kgain)
    other = lax.ppermute(keyval, "ctx", mates)
    query, grad, qunit, qscale = pl.pallas_call(
        queries_kernel,
        in_specs=[smem] + [vmem] * 3,
        out_specs=[vmem] * 4,
        out_shape=[shape(bf16, *pair), shape(bf16, *pair), shape(f32, *pair), shape(f32, *pair)],
        compiler_params=limit(20),
        name="queries",
    )(which, mine, inv_len, qgain)

    block = (patches, head)
    dq, keep, give, gains = pl.pallas_call(
        attend_kernel,
        in_specs=[smem] + [vmem] * 4,
        out_specs=[vmem] * 4,
        out_shape=[
            shape(f32, *pair),
            shape(f32, *pair),
            shape(bf16, chips + 1, 2 * own, head),
            shape(f32, extra, head),
        ],
        scratch_shapes=[pltpu.VMEM(block, bf16)] * 2
        + [pltpu.VMEM((patches // key_blk, head, key_blk), bf16)]
        + [pltpu.VMEM((patches - query_blk, query_blk), f32), pltpu.VMEM((patches, query_blk), f32)] * 2
        + [pltpu.VMEM(block, f32)] * 2
        + [pltpu.VMEM((head, query_blk), f32)],
        compiler_params=limit(36),
        name="attend",
    )(which, query, grad, keyval, other)
    got = lax.ppermute(give, "ctx", mates)
    docs = lax.axis_size("dp")
    near = lax.ppermute(gains, "dp", [(i, i ^ 1) for i in range(docs)])
    crossed = [(d * devices + i, (d ^ 1) * devices + (i ^ 1)) for d in range(docs) for i in range(devices)]
    cross = lax.ppermute(gains, ("dp", "ctx"), crossed)

    rows, kunit, kscale = pl.pallas_call(
        finish_kernel,
        in_specs=[vmem] * 6,
        out_specs=[vmem] * 3,
        out_shape=[shape(bf16, *pair), shape(f32, chips, own, head), shape(f32, chips, own, head)],
        compiler_params=limit(20),
        name="finish",
    )(dq, qunit, qscale, qgain, kmean, inv_len)
    back = pl.pallas_call(
        merge_kernel,
        in_specs=[smem] + [vmem] * 10,
        out_specs=vmem,
        out_shape=shape(bf16, chips, 4 * (own + edge) + extra, head),
        compiler_params=limit(16),
        name="merge",
    )(which, rows, keep, got, gains, near, cross, kunit, kscale, inv_len, kgain)
    home = lax.all_to_all(back, "ctx", 0, 0, tiled=True, axis_index_groups=sides)

    vcols = keyval_width // chunks
    wide = qcols + vcols + head
    rows, rims, gains = pl.pallas_call(
        back_kernel,
        in_specs=[smem] + [vmem] * 3,
        out_specs=[vmem] * 3,
        out_shape=[
            shape(bf16, chunks, own, qcols + vcols),
            shape(bf16, chunks, 2 * edge, wide),
            shape(f32, 2, head),
        ],
        compiler_params=limit(32),
        name="back",
    )(which, home, qgain, kgain)
    rims = lax.ppermute(rims, "ctx", mates)
    opposite = lax.ppermute(gains, "dp", [(i, docs - 1 - i) for i in range(docs)])
    query_out, keyval_out = pl.pallas_call(
        spread_kernel,
        in_specs=[vmem] * 3,
        out_specs=[hbm] * 2,
        out_shape=[shape(bf16, bytes_dev, query_width), shape(bf16, bytes_dev, keyval_width)],
        scratch_shapes=[
            pltpu.VMEM((bytes_dev, query_width), bf16),
            pltpu.VMEM((bytes_dev, keyval_width), bf16),
            pltpu.SemaphoreType.DMA((chunks, 2)),
        ],
        compiler_params=limit(20),
        name="spread",
    )(edges, rims, rows)
    keyval_out, opposite = lax.optimization_barrier((keyval_out, opposite))
    gains = gains + opposite
    return (query_out[None], keyval_out[None], gains[0], gains[1])


def solution(mesh):
    placed = (
        P("dp", "ctx", None),
        P("dp", "ctx", None),
        P("dp", "ctx", None),
        P("dp", None),
        P(),
        P(),
    )
    return jax.shard_map(
        shards,
        mesh=mesh,
        in_specs=placed,
        out_specs=(P("dp", "ctx", None), P("dp", "ctx", None), P(), P()),
        check_vma=False,
    )
```
